32 devices in a mesh: dp: 8 (over y, x, core), shard: 4 (over z).
Axes of the slice: x: 2, y: 2, z: 4, core: 2. Of those that a mesh axis runs over, the one named last changes fastest.
Arguments:
- tokens: bfloat16 [32768, 768], P(('dp', 'shard'))
- out_grad: bfloat16 [32768, 768], P(('dp', 'shard'))
- first_lengths: int32 [32], P(('dp', 'shard')), may hold values from 512 to 1024, as said below
- quant_scales: float32 [6], replicated, as said below
- attn_quant: bfloat16 [768, 3072], P('dp', 'shard'), may hold values from -127 to 127
- up_quant: bfloat16 [768, 3072], P('dp', 'shard'), may hold values from -127 to 127
- down_quant: bfloat16 [3072, 768], P('dp', 'shard'), may hold values from -127 to 127
- attn_master: float32 [768, 3072], P('dp', 'shard'), as said below
- attn_first: float32 [768, 3072], P('dp', 'shard')
- attn_second: float32 [768, 3072], P('dp', 'shard'), as said below
- attn_average: float32 [768, 3072], P('dp', 'shard'), may hold values from -0.21875 to 0.21875
- up_master: float32 [768, 3072], P('dp', 'shard'), as said below
- up_first: float32 [768, 3072], P('dp', 'shard')
- up_second: float32 [768, 3072], P('dp', 'shard'), as said below
- up_average: float32 [768, 3072], P('dp', 'shard'), may hold values from -0.21875 to 0.21875
- down_master: float32 [3072, 768], P('dp', 'shard'), as said below
- down_first: float32 [3072, 768], P('dp', 'shard')
- down_second: float32 [3072, 768], P('dp', 'shard'), as said below
- down_average: float32 [3072, 768], P('dp', 'shard'), may hold values from -0.109375 to 0.109375
- vector_master: float32 [768, 12], P('dp', 'shard')
- vector_first: float32 [768, 12], P('dp', 'shard')
- vector_second: float32 [768, 12], P('dp', 'shard'), as said below
- vector_average: float32 [768, 12], P('dp', 'shard'), may hold values from -3 to 3
Outputs:
- layer_out: bfloat16 [32768, 768], P(('dp', 'shard'))
- input_grad: bfloat16 [32768, 768], P(('dp', 'shard'))
- grad_norm: float32 [], replicated
- attn_first_new: float32 [768, 3072], P('dp', 'shard')
- attn_second_new: float32 [768, 3072], P('dp', 'shard')
- attn_master_new: float32 [768, 3072], P('dp', 'shard')
- attn_average_new: float32 [768, 3072], P('dp', 'shard')
- up_first_new: float32 [768, 3072], P('dp', 'shard')
- up_second_new: float32 [768, 3072], P('dp', 'shard')
- up_master_new: float32 [768, 3072], P('dp', 'shard')
- up_average_new: float32 [768, 3072], P('dp', 'shard')
- down_first_new: float32 [3072, 768], P('dp', 'shard')
- down_second_new: float32 [3072, 768], P('dp', 'shard')
- down_master_new: float32 [3072, 768], P('dp', 'shard')
- down_average_new: float32 [3072, 768], P('dp', 'shard')
- vector_first_new: float32 [768, 12], P('dp', 'shard')
- vector_second_new: float32 [768, 12], P('dp', 'shard')
- vector_master_new: float32 [768, 12], P('dp', 'shard')
- vector_average_new: float32 [768, 12], P('dp', 'shard')
The draws below stay inside these ranges and needn't reach their ends.
Inputs may be any that keep to these rules, and one draw needn't show every extreme that they name: `first_lengths`: each buffer of 1024 rows holds one sequence of 1024 tokens (value 1024) or two of 512 tokens (value 1024 / 2); both kinds occur in every draw. `quant_scales`: positive. `attn_master`: each entry within half a quantization step of the integer copy times its scale. `up_master`: each entry within half a quantization step of the integer copy times its scale. `down_master`: each entry within half a quantization step of the integer copy times its scale. `attn_second`: positive. `up_second`: positive. `down_second`: positive. `vector_second`: positive.
All inputs are finite; a program needn't handle non-finite values.
Results may differ from the reference program's by a relative error of at most 0.012.
Values may be sent and summed in bfloat16 or wider, within the bound.
No kernel may reach another device: no remote copies, remote signals or barrier semaphores. Data moves between devices by JAX's collectives and lax.ppermute only.
A program may use at most 256 MiB of HBM per device.

```python
import math
import jax
import jax.numpy as jnp
from jax import lax

D = 768
FF = 3072
HEADS = 12
HEAD_DIM = 64
TOK_DEV = 1024
STEP = 10
SLOTS = 32
TOKENS = 32768


def param_total():
    return 4 * D * D + 2 * D * FF + (8 + FF // D) * D


def rising(length, low_end, high_end):
    fraction = jnp.arange(length, dtype=jnp.float32) / (length - 1)
    return low_end * (high_end / low_end) ** fraction


def quant_parts(key):
    key = jax.random.fold_in(key, 50)
    key_list = jax.random.split(key, 7)
    spread = jnp.exp(jax.random.uniform(key_list[0], (6,), jnp.float32, -0.22, 0.22))
    output_boost = math.sqrt(TOK_DEV) / 4.0
    fan_scale = jnp.array([D ** (-0.5), D ** (-0.5), D ** (-0.5), output_boost * D ** (-0.5), D ** (-0.5), FF ** (-0.5)], jnp.float32)
    scales = fan_scale * spread / 73.6
    attn_int = jax.random.randint(key_list[1], (D, 4 * D), -127, 128).astype(jnp.float32)
    up_int = jax.random.randint(key_list[2], (D, FF), -127, 128).astype(jnp.float32)
    down_int = jax.random.randint(key_list[3], (FF, D), -127, 128).astype(jnp.float32)
    attn_frac = jax.random.uniform(key_list[4], (D, 4 * D), jnp.float32, -0.5, 0.5)
    up_frac = jax.random.uniform(key_list[5], (D, FF), jnp.float32, -0.5, 0.5)
    down_frac = jax.random.uniform(key_list[6], (FF, D), jnp.float32, -0.5, 0.5)
    column_scale = jnp.repeat(scales[:4], D)
    attn_real = (attn_int + attn_frac) * column_scale[None, :]
    up_real = (up_int + up_frac) * scales[4]
    down_real = (down_int + down_frac) * scales[5]
    return (scales, attn_int, up_int, down_int, attn_real, up_real, down_real)


def first_moment(key, rows_total, cols_total, size_scale):
    return jax.random.normal(key, (rows_total, cols_total), jnp.float32) * (size_scale * (1.0 - 0.9) / 0.9)


def second_moment(key, rows_total, cols_total, size_scale):
    spread = jnp.exp(jax.random.uniform(key, (rows_total, cols_total), jnp.float32, math.log(0.5), math.log(8.0)))
    return spread * (size_scale * size_scale * (1.0 - 0.999) / 0.999)


def matrix_size():
    return 2.0 / math.sqrt(param_total())


def vector_size():
    return 6.0 / math.sqrt(param_total())


def draw_tokens(key, part):
    key = jax.random.fold_in(key, 1)
    base = jax.random.normal(key, (TOKENS, D), jnp.float32)
    result = base * rising(D, 0.6, 1.8)[None, :]
    return result.astype(jnp.bfloat16)


def draw_out_grad(key, part):
    key = jax.random.fold_in(key, 2)
    base = jax.random.normal(key, (TOKENS, D), jnp.float32)
    result = base * rising(D, 0.6, 1.8)[None, :]
    return result.astype(jnp.bfloat16)


def draw_first_lengths(key, part):
    key = jax.random.fold_in(key, 3)
    key_flag, key_chosen = jax.random.split(key)
    long_flag = jax.random.randint(key_flag, (SLOTS,), 0, 2)
    chosen = jax.random.randint(key_chosen, (), 0, SLOTS)
    slot_index = jnp.arange(SLOTS)
    long_flag = jnp.where(slot_index == chosen, 1, long_flag)
    long_flag = jnp.where(slot_index == (chosen + 1) % SLOTS, 0, long_flag)
    return (TOK_DEV // 2 * (1 + long_flag)).astype(jnp.int32)


def draw_quant_scales(key, part):
    return quant_parts(key)[0]


def draw_attn_quant(key, part):
    return quant_parts(key)[1].astype(jnp.bfloat16)


def draw_up_quant(key, part):
    return quant_parts(key)[2].astype(jnp.bfloat16)


def draw_down_quant(key, part):
    return quant_parts(key)[3].astype(jnp.bfloat16)


def draw_attn_master(key, part):
    return quant_parts(key)[4]


def draw_up_master(key, part):
    return quant_parts(key)[5]


def draw_down_master(key, part):
    return quant_parts(key)[6]


def draw_attn_first(key, part):
    key = jax.random.fold_in(key, 11)
    return first_moment(key, D, 4 * D, matrix_size())


def draw_attn_second(key, part):
    key = jax.random.fold_in(key, 12)
    return second_moment(key, D, 4 * D, matrix_size())


def draw_up_first(key, part):
    key = jax.random.fold_in(key, 13)
    return first_moment(key, D, FF, matrix_size())


def draw_up_second(key, part):
    key = jax.random.fold_in(key, 14)
    return second_moment(key, D, FF, matrix_size())


def draw_down_first(key, part):
    key = jax.random.fold_in(key, 15)
    return first_moment(key, FF, D, matrix_size())


def draw_down_second(key, part):
    key = jax.random.fold_in(key, 16)
    return second_moment(key, FF, D, matrix_size())


def draw_vector_first(key, part):
    key = jax.random.fold_in(key, 17)
    return first_moment(key, D, 8 + FF // D, vector_size())


def draw_vector_second(key, part):
    key = jax.random.fold_in(key, 18)
    return second_moment(key, D, 8 + FF // D, vector_size())


def draw_vector_master(key, part):
    key = jax.random.fold_in(key, 20)
    key_bias, key_gain = jax.random.split(key)
    base = jax.random.normal(key_bias, (D, 8 + FF // D), jnp.float32) * 0.2
    gains = rising(D, 0.6, 1.8)[:, None] * jax.random.uniform(key_gain, (D, 2), jnp.float32, 0.85, 1.15)
    base = base.at[:, 3].set(gains[:, 0])
    base = base.at[:, 6].set(gains[:, 1])
    return base


def levels(stream_key, extent, cuts, low, largest):
    gain = 1.0
    for axis_at, shards_of in cuts:
        steps = jax.random.uniform(jax.random.fold_in(jax.random.fold_in(stream_key, 6), axis_at), (shards_of,), jnp.float32, low / len(cuts), largest / len(cuts))
        gain = gain * jnp.repeat(jnp.exp(steps), extent[axis_at] // shards_of).reshape((-1,) + (1,) * (len(extent) - 1 - axis_at))
    return gain


def scatter_about(stream_key, shape, width, most, shards=(), kind=jnp.bfloat16):
    drawn = jax.random.normal(stream_key, shape, jnp.float32) * width
    if len(shards) > 0:
        drawn = levels(stream_key, shape, shards, -0.22, 0.18) * drawn
    return jnp.clip(drawn, min=-most, max=most).astype(kind)


def setup_inputs(seed: int = 0) -> dict:
    arg_keys = jax.random.split(jax.random.key(seed), 24)
    tokens = draw_tokens(jax.random.fold_in(arg_keys[23], 71), 0)
    out_grad = draw_out_grad(jax.random.fold_in(arg_keys[23], 71), 0)
    first_lengths = draw_first_lengths(jax.random.fold_in(arg_keys[23], 71), 0)
    quant_scales = draw_quant_scales(jax.random.fold_in(arg_keys[23], 71), 0)
    attn_quant = draw_attn_quant(jax.random.fold_in(arg_keys[23], 71), 0)
    up_quant = draw_up_quant(jax.random.fold_in(arg_keys[23], 71), 0)
    down_quant = draw_down_quant(jax.random.fold_in(arg_keys[23], 71), 0)
    attn_master = draw_attn_master(jax.random.fold_in(arg_keys[23], 71), 0)
    attn_first = draw_attn_first(jax.random.fold_in(arg_keys[23], 71), 0)
    attn_second = draw_attn_second(jax.random.fold_in(arg_keys[23], 71), 0)
    attn_average = scatter_about(arg_keys[10], (D, 4 * D), D ** -0.5, 0.21875, ((0, 8), (1, 4)), jnp.float32)
    up_master = draw_up_master(jax.random.fold_in(arg_keys[23], 71), 0)
    up_first = draw_up_first(jax.random.fold_in(arg_keys[23], 71), 0)
    up_second = draw_up_second(jax.random.fold_in(arg_keys[23], 71), 0)
    up_average = scatter_about(arg_keys[14], (D, FF), D ** -0.5, 0.21875, ((0, 8), (1, 4)), jnp.float32)
    down_master = draw_down_master(jax.random.fold_in(arg_keys[23], 71), 0)
    down_first = draw_down_first(jax.random.fold_in(arg_keys[23], 71), 0)
    down_second = draw_down_second(jax.random.fold_in(arg_keys[23], 71), 0)
    down_average = scatter_about(arg_keys[18], (FF, D), FF ** -0.5, 0.109375, ((0, 8), (1, 4)), jnp.float32)
    vector_master = draw_vector_master(jax.random.fold_in(arg_keys[23], 71), 0)
    vector_first = draw_vector_first(jax.random.fold_in(arg_keys[23], 71), 0)
    vector_second = draw_vector_second(jax.random.fold_in(arg_keys[23], 71), 0)
    vector_average = scatter_about(arg_keys[22], (D, 8 + FF // D), 0.5, 3.0, ((0, 8), (1, 4)), jnp.float32)
    return dict(tokens=tokens, out_grad=out_grad, first_lengths=first_lengths, quant_scales=quant_scales, attn_quant=attn_quant, up_quant=up_quant, down_quant=down_quant, attn_master=attn_master, attn_first=attn_first, attn_second=attn_second, attn_average=attn_average, up_master=up_master, up_first=up_first, up_second=up_second, up_average=up_average, down_master=down_master, down_first=down_first, down_second=down_second, down_average=down_average, vector_master=vector_master, vector_first=vector_first, vector_second=vector_second, vector_average=vector_average)


@jax.custom_vjp
def low(v):
    return lax.optimization_barrier(v.astype(jnp.bfloat16)).astype(jnp.float32)

@jax.custom_vjp
def low_back(v):
    return v

def low_keep(v):
    return (low(v), None)

def low_pass(kept, grad):
    return (grad,)

def back_keep(v):
    return (v, None)

def back_low(kept, grad):
    return (low(grad),)
low.defvjp(low_keep, low_pass)
low_back.defvjp(back_keep, back_low)
highest = lax.Precision.HIGHEST
norm_eps = 1e-06
clip_limit = 1.0
beta_first = 0.9
beta_second = 0.999
adam_eps = 1e-08
matrix_rate = 0.08
vector_rate = 0.5
matrix_decay = 0.01
average_keep = 0.9

def product(left, right):
    return jnp.dot(left, right, precision=highest, preferred_element_type=jnp.float32)

def layer_norm(inputs, gain_row, shift_row):
    centre = inputs - lax.optimization_barrier(jnp.mean(inputs, axis=-1, keepdims=True))
    inv_std = lax.rsqrt(lax.optimization_barrier(jnp.mean(centre * centre, axis=-1, keepdims=True)) + norm_eps)
    return centre * inv_std * gain_row + shift_row

def one_buffer(tokens, segment, attn_w, up_w, down_w, vectors):
    bias_q = vectors[:, 0]
    bias_v = vectors[:, 1]
    bias_o = vectors[:, 2]
    gain_one = vectors[:, 3]
    shift_one = vectors[:, 4]
    bias_two = vectors[:, 5]
    gain_two = vectors[:, 6]
    shift_two = vectors[:, 7]
    bias_up = vectors[:, 8:].T.reshape(-1)
    row_count = tokens.shape[0]
    queries = low(low_back(product(tokens, attn_w[:, :D])) + bias_q)
    key_rows = low(low_back(product(tokens, attn_w[:, D:2 * D])))
    values = low(low_back(product(tokens, attn_w[:, 2 * D:3 * D])) + bias_v)
    q_heads = queries.reshape(row_count, HEADS, HEAD_DIM)
    k_heads = key_rows.reshape(row_count, HEADS, HEAD_DIM)
    v_heads = values.reshape(row_count, HEADS, HEAD_DIM)
    raw_scores = jnp.einsum('qhd,khd->hqk', q_heads, k_heads, precision=highest)
    scores = low_back(raw_scores) * (1.0 / math.sqrt(HEAD_DIM))
    same_seq = segment[:, None] == segment[None, :]
    scores = jnp.where(same_seq[None], scores, -1e+30)
    row_max = lax.optimization_barrier(jnp.max(scores, axis=-1, keepdims=True))
    exponent = jnp.exp(scores - row_max)
    attn_prob = exponent / lax.optimization_barrier(jnp.sum(exponent, axis=-1, keepdims=True))
    context = jnp.einsum('hqk,khd->qhd', low(attn_prob), v_heads, precision=highest).reshape(row_count, D)
    context = low(low_back(context))
    residual_one = tokens + low_back(product(context, attn_w[:, 3 * D:])) + bias_o
    norm_one = layer_norm(residual_one, gain_one, shift_one)
    hidden = low_back(product(low(norm_one), up_w)) + bias_up
    activated = low(jax.nn.gelu(hidden, approximate=True))
    residual_two = norm_one + low_back(product(activated, down_w)) + bias_two
    return layer_norm(residual_two, gain_two, shift_two)

def group_forward(inputs, segment_all, attn_w, up_w, down_w, vectors):
    slots_group = max(1, min(SLOTS, 2048 // TOK_DEV))
    grouped = inputs.reshape(SLOTS // slots_group, slots_group, TOK_DEV, D)
    seg_grouped = segment_all.reshape(SLOTS // slots_group, slots_group, TOK_DEV)

    def run_group(pair):
        part_tokens, part_segment = pair
        return jax.vmap(one_buffer, in_axes=(0, 0, None, None, None, None))(part_tokens, part_segment, attn_w, up_w, down_w, vectors)
    outputs = lax.map(jax.checkpoint(run_group), (grouped, seg_grouped))
    return outputs.reshape(TOKENS, D)

def adam_update(gradient, master, first_old, second_old, average, step_rate, decay_rate):
    first_new = beta_first * first_old + (1.0 - beta_first) * gradient
    second_new = beta_second * second_old + (1.0 - beta_second) * gradient * gradient
    first_hat = first_new / (1.0 - beta_first ** STEP)
    second_hat = second_new / (1.0 - beta_second ** STEP)
    master_new = master - step_rate * (first_hat / (jnp.sqrt(second_hat) + adam_eps) + decay_rate * master)
    average_new = average_keep * average + (1.0 - average_keep) * master_new
    return (first_new, second_new, master_new, average_new)

def reference(tokens, out_grad, first_lengths, quant_scales, attn_quant, up_quant, down_quant, attn_master, attn_first, attn_second, attn_average, up_master, up_first, up_second, up_average, down_master, down_first, down_second, down_average, vector_master, vector_first, vector_second, vector_average):
    column_scale = jnp.repeat(quant_scales[:4], D)
    attn_w = attn_quant.astype(jnp.float32) * column_scale[None, :]
    up_w = up_quant.astype(jnp.float32) * quant_scales[4]
    down_w = down_quant.astype(jnp.float32) * quant_scales[5]
    vectors = lax.optimization_barrier(vector_master.astype(jnp.bfloat16)).astype(jnp.float32)
    position = jnp.arange(TOK_DEV, dtype=jnp.int32)
    segment_all = (position[None, :] >= first_lengths[:, None]).astype(jnp.int32)
    inputs = tokens.astype(jnp.float32)

    def forward(inputs, attn_w, up_w, down_w, vectors):
        return group_forward(inputs, segment_all, attn_w, up_w, down_w, vectors)
    outputs, pullback = jax.vjp(forward, inputs, attn_w, up_w, down_w, vectors)
    grad_in, grad_attn, grad_up, grad_down, grad_vector = pullback(out_grad.astype(jnp.float32))
    squares = jnp.sum(grad_attn * grad_attn) + jnp.sum(grad_up * grad_up) + jnp.sum(grad_down * grad_down) + jnp.sum(grad_vector * grad_vector)
    grad_norm = jnp.sqrt(squares)
    factor = jnp.minimum(1.0, clip_limit / (grad_norm + norm_eps))
    attn_a, attn_b, attn_c, attn_d = adam_update(grad_attn * factor, attn_master, attn_first, attn_second, attn_average, matrix_rate, matrix_decay)
    up_a, up_b, up_c, up_d = adam_update(grad_up * factor, up_master, up_first, up_second, up_average, matrix_rate, matrix_decay)
    down_a, down_b, down_c, down_d = adam_update(grad_down * factor, down_master, down_first, down_second, down_average, matrix_rate, matrix_decay)
    vector_a, vector_b, vector_c, vector_d = adam_update(grad_vector * factor, vector_master, vector_first, vector_second, vector_average, vector_rate, 0.0)
    return (outputs.astype(jnp.bfloat16), grad_in.astype(jnp.bfloat16), grad_norm, attn_a, attn_b, attn_c, attn_d, up_a, up_b, up_c, up_d, down_a, down_b, down_c, down_d, vector_a, vector_b, vector_c, vector_d)
```

```python
import functools
import math

import jax
import jax.numpy as jnp
from jax import lax
from jax.experimental import pallas as pl
from jax.experimental.pallas import tpu as pltpu
from jax.sharding import PartitionSpec as P

HEAD_DIM = 64
STEP = 10

norm_eps = 1e-06
clip_limit = 1.0
beta_first = 0.9
beta_second = 0.999
adam_eps = 1e-08
matrix_rate = 0.08
vector_rate = 0.5
matrix_decay = 0.01
average_keep = 0.9

VMEM = 58 * 2**20
GELU_K = math.sqrt(2.0 / math.pi)
GELU_C = 0.044715
f32 = jnp.float32
bf16 = jnp.bfloat16
SDS = jax.ShapeDtypeStruct


def dot(left, right):
    return jnp.dot(left, right, preferred_element_type=f32)


def dot_last(left, right):
    return lax.dot_general(left, right, (((1,), (1,)), ((), ())), preferred_element_type=f32)


def col_sum(value):
    return jnp.sum(value, axis=0, keepdims=True)


def params(**extra):
    return pltpu.CompilerParams(vmem_limit_bytes=VMEM, **extra)


def cost(flops, moved, trans=0):
    return pl.CostEstimate(flops=int(flops), bytes_accessed=int(moved), transcendentals=int(trans))


SMEM = pl.BlockSpec(memory_space=pltpu.SMEM)


def normalize(value):
    centre = value - jnp.mean(value, axis=-1, keepdims=True)
    inv_std = lax.rsqrt(jnp.mean(centre * centre, axis=-1, keepdims=True) + norm_eps)
    return centre * inv_std, inv_std


def normalize_back(scaled, normed, inv_std):
    return inv_std * (
        scaled
        - jnp.mean(scaled, axis=-1, keepdims=True)
        - normed * jnp.mean(scaled * normed, axis=-1, keepdims=True)
    )


def attn_fwd_kernel(
    len_ref, scale_ref, x_ref, wq_ref, wk_ref, wv_ref, bq_ref, bv_ref,
    q_ref, k_ref, v_ref, c_ref, lse_ref, *, block,
):
    rows, width = q_ref.shape
    x = x_ref[...]
    q_ref[...] = (dot(x, wq_ref[...]) * scale_ref[0] + bq_ref[...]).astype(bf16)
    k_ref[...] = (dot(x, wk_ref[...]) * scale_ref[1]).astype(bf16)
    v_ref[...] = (dot(x, wv_ref[...]) * scale_ref[2] + bv_ref[...]).astype(bf16)
    lane = lax.broadcasted_iota(jnp.int32, (1, 128), 1)

    def run(span):
        step = min(block, span)
        for pair in range(width // 128):
            cols = pl.ds(pair * 128, 128)
            for start in range(0, rows, step):
                low = start // span * span
                q_rows = q_ref[start : start + step, cols]
                k_rows = k_ref[low : low + span, cols]
                v_rows = v_ref[low : low + span, cols]
                found = []
                for head in range(2):
                    own = (lane < 64) if head == 0 else (lane >= 64)
                    q_own = jnp.where(own, q_rows, jnp.zeros_like(q_rows)) * jnp.asarray(0.125, bf16)
                    v_ones = jnp.where(own, v_rows, jnp.ones_like(v_rows))
                    scores = dot_last(q_own, k_rows)
                    top = jnp.max(scores, axis=1, keepdims=True)
                    found.append((dot(jnp.exp(scores - top).astype(bf16), v_ones), top))
                (out_a, top_a), (out_b, top_b) = found
                value = jnp.where(lane < 64, out_a, out_b)
                total = jnp.where(lane < 64, pltpu.roll(out_a, 64, 1), pltpu.roll(out_b, 64, 1))
                c_ref[start : start + step, cols] = (value / total).astype(bf16)
                lse_ref[start : start + step, cols] = jnp.where(lane < 64, top_a, top_b) + jnp.log(total)

    two = len_ref[0] < rows

    @pl.when(two)
    def _():
        run(rows // 2)

    @pl.when(jnp.logical_not(two))
    def _():
        run(rows)


def attn_fwd(lengths, scales, x, w_attn, bias_q, bias_v):
    rows, width = x.shape
    group = 256
    count = width // group

    def cols(height, part=0):
        return pl.BlockSpec((height, group), lambda g: (0, part * count + g))

    return pl.pallas_call(
        functools.partial(attn_fwd_kernel, block=512),
        grid=(count,),
        in_specs=[SMEM, SMEM, pl.BlockSpec((rows, width), lambda g: (0, 0)),
                  cols(width, 0), cols(width, 1), cols(width, 2), cols(1), cols(1)],
        out_specs=[cols(rows)] * 5,
        out_shape=[SDS((rows, width), bf16)] * 4 + [SDS((rows, width), f32)],
        compiler_params=params(),
        cost_estimate=cost(20e9, 12e6, 12e6),
        name="attention_forward",
    )(lengths, scales, x, w_attn, w_attn, w_attn, bias_q, bias_v)


def attn_bwd_kernel(
    len_ref, q_ref, k_ref, v_ref, dc_ref, c_ref, lse_ref,
    dq_ref, dk_ref, dv_ref, sum_q_ref, sum_v_ref, dk_acc, dv_acc, dq_acc, *, block,
):
    rows = q_ref.shape[0]
    lane = lax.broadcasted_iota(jnp.int32, (1, 128), 1)
    masks = [lane < 64, lane >= 64]
    prod = (dc_ref[...].astype(f32) * c_ref[...].astype(f32)).T
    row_dots = [col_sum(prod[:64]), col_sum(prod[64:])]
    lse = lse_ref[...].T
    lse_rows = [lse[0:1], lse[64:65]]

    def run(span):
        step = min(block, span)
        for low in range(0, rows, span):
            k_rows = k_ref[low : low + span, :]
            v_rows = v_ref[low : low + span, :]
            k_cols = k_rows.astype(f32).T.astype(bf16)
            for start in range(low, low + span, step):
                q_rows = q_ref[start : start + step, :]
                dc_rows = dc_ref[start : start + step, :]
                probs, d_scores, q_own, dc_own, dq_parts = [], [], [], [], []
                for head in range(2):
                    q_head = jnp.where(masks[head], q_rows, jnp.zeros_like(q_rows)) * jnp.asarray(0.125, bf16)
                    dc_head = jnp.where(masks[head], dc_rows, jnp.zeros_like(dc_rows))
                    prob = jnp.exp(dot_last(k_rows, q_head) - lse_rows[head][:, start : start + step])
                    d_prob = dot_last(v_rows, dc_head)
                    d_score = (prob * (d_prob - row_dots[head][:, start : start + step])).astype(bf16)
                    probs.append(prob.astype(bf16))
                    d_scores.append(d_score)
                    q_own.append(q_head)
                    dc_own.append(dc_head)
                    dq_parts.append(dot(k_cols[head * 64 : head * 64 + 64], d_score))
                dq_acc[:, start : start + step] = jnp.concatenate(dq_parts, axis=0)
                dv = dot(jnp.concatenate(probs, axis=1), jnp.concatenate(dc_own, axis=0))
                dk = dot(jnp.concatenate(d_scores, axis=1), jnp.concatenate(q_own, axis=0))
                if start == low:
                    dv_acc[low : low + span, :] = dv
                    dk_acc[low : low + span, :] = dk
                else:
                    dv_acc[low : low + span, :] += dv
                    dk_acc[low : low + span, :] += dk

    two = len_ref[0] < rows

    @pl.when(two)
    def _():
        run(rows // 2)

    @pl.when(jnp.logical_not(two))
    def _():
        run(rows)

    dq = dq_acc[...].T * 0.125
    dq_ref[...] = dq.astype(bf16)
    dk_ref[...] = dk_acc[...].astype(bf16)
    dv_ref[...] = dv_acc[...].astype(bf16)
    sum_q_ref[...] = jnp.broadcast_to(col_sum(dq), sum_q_ref.shape)
    sum_v_ref[...] = jnp.broadcast_to(col_sum(dv_acc[...]), sum_v_ref.shape)


def attn_bwd(lengths, q, k, v, dc, c, lse):
    rows, width = q.shape
    cols = pl.BlockSpec((rows, 128), lambda g: (0, g))
    sums = pl.BlockSpec((8, 128), lambda g: (0, g))
    return pl.pallas_call(
        functools.partial(attn_bwd_kernel, block=512),
        grid=(width // 128,),
        in_specs=[SMEM] + [cols] * 6,
        out_specs=[cols] * 3 + [sums] * 2,
        out_shape=[SDS((rows, width), bf16)] * 3 + [SDS((8, width), f32)] * 2,
        scratch_shapes=[pltpu.VMEM((rows, 128), f32), pltpu.VMEM((rows, 128), f32), pltpu.VMEM((128, rows), f32)],
        compiler_params=params(),
        cost_estimate=cost(40e9, 20e6, 12e6),
        name="attention_backward",
    )(lengths, q, k, v, dc, c, lse)


def mid_fwd_kernel(scale_ref, x_ref, c_ref, wo_ref, w1_ref, vec_ref, b1_ref, n1_ref, r1_ref, y1_ref, a_ref, gp_ref, *, chunk):
    rows = x_ref.shape[0]
    residual = x_ref[...].astype(f32) + dot(c_ref[...], wo_ref[...]) * scale_ref[3] + vec_ref[2:3]
    normed, inv_std = normalize(residual)
    n1_ref[...] = normed
    r1_ref[...] = jnp.broadcast_to(inv_std, (rows, 128))
    y1 = (normed * vec_ref[3:4] + vec_ref[4:5]).astype(bf16)
    y1_ref[...] = y1
    for start in range(0, w1_ref.shape[1], chunk):
        cols = slice(start, start + chunk)
        u = dot(y1, w1_ref[:, cols]) * scale_ref[4] + b1_ref[:, cols]
        square = u * u
        half = 0.5 + 0.5 * jnp.tanh(u * (GELU_K + (GELU_K * GELU_C) * square))
        act = u * half
        a_ref[:, cols] = act.astype(bf16)
        gp_ref[:, cols] = (half + act * (1.0 - half) * (2 * GELU_K + (6 * GELU_K * GELU_C) * square)).astype(bf16)


def mid_fwd(scales, x, c, w_out, w_up, vec, bias_up):
    rows, width = x.shape
    hidden = w_up.shape[1]
    tile = 512

    def row(size):
        return pl.BlockSpec((tile, size), lambda i: (i, 0))

    def full(arr):
        return pl.BlockSpec(arr.shape, lambda i: (0, 0))

    return pl.pallas_call(
        functools.partial(mid_fwd_kernel, chunk=256),
        grid=(rows // tile,),
        in_specs=[SMEM, row(width), row(width), full(w_out), full(w_up), full(vec), full(bias_up)],
        out_specs=[row(width), row(128), row(width), row(hidden), row(hidden)],
        out_shape=[SDS((rows, width), f32), SDS((rows, 128), f32), SDS((rows, width), bf16),
                   SDS((rows, hidden), bf16), SDS((rows, hidden), bf16)],
        compiler_params=params(),
        cost_estimate=cost(12e9, 25e6, 3e6),
        name="middle_forward",
    )(scales, x, c, w_out, w_up, vec, bias_up)


def mid_bwd_kernel(
    scale_ref, n1_ref, r1_ref, a_ref, gp_ref, do_ref, w2_ref, w1_ref, wo_ref, vec_ref,
    out_ref, dz_ref, du_ref, dh_ref, dhb_ref, dc_ref, vg_ref, b1g_ref, *, chunk,
):
    @pl.when(pl.program_id(0) == 0)
    def _():
        vg_ref[...] = jnp.zeros_like(vg_ref)
        b1g_ref[...] = jnp.zeros_like(b1g_ref)

    g1, c1, b2, g2, c2 = [vec_ref[i : i + 1] for i in range(3, 8)]
    n1 = n1_ref[...]
    residual = n1 * g1 + c1 + dot_last(a_ref[...], w2_ref[...]) * scale_ref[5] + b2
    n2, r2 = normalize(residual)
    out_ref[...] = (n2 * g2 + c2).astype(bf16)
    d_out = do_ref[...].astype(f32)
    vg_ref[6:7] += col_sum(d_out * n2)
    vg_ref[7:8] += col_sum(d_out)
    dz = normalize_back(d_out * g2, n2, r2)
    vg_ref[5:6] += col_sum(dz)
    dz_low = dz.astype(bf16)
    dz_ref[...] = dz_low
    for start in range(0, w1_ref.shape[1], chunk):
        cols = slice(start, start + chunk)
        du = dot(dz_low, w2_ref[:, cols]) * scale_ref[5] * gp_ref[:, cols].astype(f32)
        b1g_ref[0:1, cols] += col_sum(du)
        du_ref[:, cols] = du.astype(bf16)
    dy = dz + dot_last(du_ref[...], w1_ref[...]) * scale_ref[4]
    vg_ref[3:4] += col_sum(dy * n1)
    vg_ref[4:5] += col_sum(dy)
    dh = normalize_back(dy * g1, n1, r1_ref[:, 0:1])
    vg_ref[2:3] += col_sum(dh)
    dh_ref[...] = dh
    dh_low = dh.astype(bf16)
    dhb_ref[...] = dh_low
    dc_ref[...] = (dot_last(dh_low, wo_ref[...]) * scale_ref[3]).astype(bf16)


def mid_bwd(scales, n1, r1, act, gelu_grad, d_out, w_down_t, w_up, w_out, vec):
    rows, width = n1.shape
    hidden = w_up.shape[1]
    tile = 256

    def row(size):
        return pl.BlockSpec((tile, size), lambda i: (i, 0))

    def full(arr):
        return pl.BlockSpec(arr.shape, lambda i: (0, 0))

    return pl.pallas_call(
        functools.partial(mid_bwd_kernel, chunk=256),
        grid=(rows // tile,),
        in_specs=[SMEM, row(width), row(128), row(hidden), row(hidden), row(width),
                  full(w_down_t), full(w_up), full(w_out), full(vec)],
        out_specs=[row(width), row(width), row(hidden), row(width), row(width), row(width),
                   pl.BlockSpec((8, width), lambda i: (0, 0)), pl.BlockSpec((8, hidden), lambda i: (0, 0))],
        out_shape=[SDS((rows, width), bf16), SDS((rows, width), bf16), SDS((rows, hidden), bf16),
                   SDS((rows, width), f32), SDS((rows, width), bf16), SDS((rows, width), bf16),
                   SDS((8, width), f32), SDS((8, hidden), f32)],
        compiler_params=params(),
        cost_estimate=cost(25e9, 45e6),
        name="middle_backward",
    )(scales, n1, r1, act, gelu_grad, d_out, w_down_t, w_up, w_out, vec)


def weight_grad_kernel(left_ref, *refs, count):
    right, outs, left_t = refs[:count], refs[count : 2 * count], refs[2 * count]

    @pl.when(pl.program_id(0) == 0)
    def _():
        left_t[...] = left_ref[...].T

    for r, o in zip(right, outs):
        o[...] = dot(left_t[...], r[...]).astype(bf16)


def weight_grad(left, rights, chunk):
    rows, width = left.shape
    size = rights[0].shape[1]
    count = len(rights)
    return pl.pallas_call(
        functools.partial(weight_grad_kernel, count=count),
        grid=(size // chunk,),
        in_specs=[pl.BlockSpec((rows, width), lambda i: (0, 0))]
        + [pl.BlockSpec((rows, chunk), lambda i: (0, i))] * count,
        out_specs=[pl.BlockSpec((width, chunk), lambda i: (0, i))] * count,
        out_shape=[SDS((width, size), bf16)] * count,
        scratch_shapes=[pltpu.VMEM((width, rows), bf16)],
        compiler_params=params(),
        cost_estimate=cost(3 * rows * width * size * count, 2 * (rows * width + count * size * (rows + width))),
        name="weight_gradient",
    )(left, *rights)


def input_grad_kernel(scale_ref, dh_ref, dq_ref, dk_ref, dv_ref, wq_ref, wk_ref, wv_ref, out_ref):
    total = dh_ref[...] + dot_last(dq_ref[...], wq_ref[...]) * scale_ref[0]
    total = total + dot_last(dk_ref[...], wk_ref[...]) * scale_ref[1]
    out_ref[...] = (total + dot_last(dv_ref[...], wv_ref[...]) * scale_ref[2]).astype(bf16)


def input_grad(scales, dh, dq, dk, dv, w_attn):
    rows, width = dh.shape
    tile = 512
    row = pl.BlockSpec((tile, width), lambda i: (i, 0))

    def part(index):
        return pl.BlockSpec((width, width), lambda i: (0, index))

    return pl.pallas_call(
        input_grad_kernel,
        grid=(rows // tile,),
        in_specs=[SMEM] + [row] * 4 + [part(i) for i in range(3)],
        out_specs=row,
        out_shape=SDS((rows, width), bf16),
        compiler_params=params(),
        cost_estimate=cost(9e9, 2 * (rows * width * 6 + 3 * width * width)),
        name="input_gradient",
    )(scales, dh, dq, dk, dv, w_attn, w_attn, w_attn)


def adam_update(gradient, master, first_old, second_old, average, step_rate, decay_rate):
    first_new = beta_first * first_old + (1.0 - beta_first) * gradient
    second_new = beta_second * second_old + (1.0 - beta_second) * gradient * gradient
    first_hat = first_new / (1.0 - beta_first**STEP)
    second_hat = second_new / (1.0 - beta_second**STEP)
    master_new = master - step_rate * (
        first_hat / (jnp.sqrt(second_hat) + adam_eps) + decay_rate * master
    )
    average_new = average_keep * average + (1.0 - average_keep) * master_new
    return (first_new, second_new, master_new, average_new)


def on_device(
    tokens, out_grad, first_lengths, quant_scales, attn_quant, up_quant, down_quant,
    attn_master, attn_first, attn_second, attn_average,
    up_master, up_first, up_second, up_average,
    down_master, down_first, down_second, down_average,
    vector_master, vector_first, vector_second, vector_average,
):
    width = tokens.shape[1]
    gather = functools.partial(lax.all_gather, tiled=True)
    scatter = functools.partial(lax.psum_scatter, tiled=True)
    vector_low = vector_master.astype(bf16)
    attn_w = gather(gather(attn_quant, "shard", axis=1), "dp", axis=0)
    vec_w = gather(gather(vector_low, "shard", axis=1), "dp", axis=0)
    up_w = gather(gather(up_quant, "shard", axis=1), "dp", axis=0)
    down_t = gather(gather(down_quant.T, "shard", axis=0), "dp", axis=1)
    vec = vec_w.astype(f32).T
    bias_up = vec[8:].reshape(1, -1)
    vec = vec[:8]

    q, k, v, c, lse = attn_fwd(first_lengths, quant_scales, tokens, attn_w, vec[0:1], vec[1:2])
    w_out = attn_w[:, 3 * width :]
    n1, r1, y1, act, gelu_grad = mid_fwd(quant_scales, tokens, c, w_out, up_w, vec, bias_up)
    layer_out, dz, du, dh, dh_low, dc, vec_grad, b1_grad = mid_bwd(
        quant_scales, n1, r1, act, gelu_grad, out_grad, down_t, up_w, w_out, vec
    )
    (grad_down_t,) = weight_grad(dz, [act], 768)
    (grad_up,) = weight_grad(y1, [du], 768)
    (grad_out_proj,) = weight_grad(c, [dh_low], 768)
    dq, dk, dv, sum_q, sum_v = attn_bwd(first_lengths, q, k, v, dc, c, lse)
    grad_qkv = weight_grad(tokens, [dq, dk, dv], 256)
    input_gradient = input_grad(quant_scales, dh, dq, dk, dv, attn_w)

    vec_rows = jnp.concatenate([sum_q[0:1], sum_v[0:1], vec_grad[2:8], b1_grad[0:1].reshape(-1, width)], axis=0)
    own_down = scatter(scatter(grad_down_t, "dp", scatter_dimension=1), "shard", scatter_dimension=0)
    own_up = scatter(scatter(grad_up, "dp", scatter_dimension=0), "shard", scatter_dimension=1)
    grad_attn = jnp.concatenate(list(grad_qkv) + [grad_out_proj], axis=1)
    own_attn = scatter(scatter(grad_attn, "dp", scatter_dimension=0), "shard", scatter_dimension=1)
    own_vector = scatter(scatter(vec_rows.T, "dp", scatter_dimension=0), "shard", scatter_dimension=1)
    own_down = own_down.astype(f32).T
    own_up = own_up.astype(f32)
    own_attn = own_attn.astype(f32)
    local_squares = (
        jnp.sum(own_attn * own_attn)
        + jnp.sum(own_up * own_up)
        + jnp.sum(own_down * own_down)
        + jnp.sum(own_vector * own_vector)
    )
    grad_norm = jnp.sqrt(lax.psum(local_squares, ("dp", "shard")))
    factor = jnp.minimum(1.0, clip_limit / (grad_norm + norm_eps))
    attn_new = adam_update(own_attn * factor, attn_master, attn_first, attn_second, attn_average, matrix_rate, matrix_decay)
    up_new = adam_update(own_up * factor, up_master, up_first, up_second, up_average, matrix_rate, matrix_decay)
    down_new = adam_update(own_down * factor, down_master, down_first, down_second, down_average, matrix_rate, matrix_decay)
    vector_new = adam_update(own_vector * factor, vector_master, vector_first, vector_second, vector_average, vector_rate, 0.0)
    return (layer_out, input_gradient, grad_norm, *attn_new, *up_new, *down_new, *vector_new)


def solution(mesh):
    rows = P(("dp", "shard"), None)
    block = P("dp", "shard")
    in_specs = (rows, rows, P(("dp", "shard")), P()) + (block,) * 19
    out_specs = (rows, rows, P()) + (block,) * 16
    return jax.shard_map(
        on_device, mesh=mesh, in_specs=in_specs, out_specs=out_specs, check_vma=False
    )
```

```python
import functools
import math

import jax
import jax.numpy as jnp
from jax import lax
from jax.experimental import pallas as pl
from jax.experimental.pallas import tpu as pltpu
from jax.sharding import PartitionSpec as P

HEAD_DIM = 64
STEP = 10

norm_eps = 1e-06
clip_limit = 1.0
beta_first = 0.9
beta_second = 0.999
adam_eps = 1e-08
matrix_rate = 0.08
vector_rate = 0.5
matrix_decay = 0.01
average_keep = 0.9

VMEM = 58 * 2**20
GELU_K = math.sqrt(2.0 / math.pi)
GELU_C = 0.044715
f32 = jnp.float32
bf16 = jnp.bfloat16
SDS = jax.ShapeDtypeStruct


def dot(left, right):
    return jnp.dot(left, right, preferred_element_type=f32)


def dot_last(left, right):
    return lax.dot_general(left, right, (((1,), (1,)), ((), ())), preferred_element_type=f32)


def col_sum(value):
    return jnp.sum(value, axis=0, keepdims=True)


def params(**extra):
    return pltpu.CompilerParams(vmem_limit_bytes=VMEM, **extra)


def cost(flops, moved, trans=0):
    return pl.CostEstimate(flops=int(flops), bytes_accessed=int(moved), transcendentals=int(trans))


SMEM = pl.BlockSpec(memory_space=pltpu.SMEM)
ANY = pl.BlockSpec(memory_space=pl.ANY)


def piece_row(place_ref, index, count):
    if count == 1:
        return 0
    half = count // 2
    return ((place_ref[1] ^ (index % half)) * 2) + (place_ref[0] ^ (index // half))


def attn_copies(place_ref, pieces, planes, dest, sems):
    count = len(pieces)
    rows, width = pieces[0].shape[1:]
    copies = []
    for at, plane in enumerate(planes):
        for index, piece in enumerate(pieces):
            row = pl.multiple_of(piece_row(place_ref, index, count) * rows, 16)
            copies.append(
                pltpu.make_async_copy(
                    piece.at[plane ^ place_ref[2]],
                    dest.at[pl.ds(row, rows), at * width : (at + 1) * width],
                    sems.at[len(copies)],
                )
            )
    return copies


def up_copies(place_ref, source, dest, sems):
    blocks, slots, rows, width = source.shape
    copies = []
    for block in range(blocks):
        for slot in range(slots):
            col = pl.multiple_of((slot ^ place_ref[2]) * width, 128)
            copies.append(
                pltpu.make_async_copy(
                    source.at[block, slot],
                    dest.at[block * rows : (block + 1) * rows, pl.ds(col, width)],
                    sems.at[len(copies)],
                )
            )
    return copies


def down_copies(place_ref, source, dest, sems):
    blocks, slots, rows, width = source.shape
    copies = []
    for block in range(blocks):
        for slot in range(slots):
            row = pl.multiple_of((slot ^ place_ref[2]) * rows, 16)
            copies.append(
                pltpu.make_async_copy(
                    source.at[block, slot],
                    dest.at[pl.ds(row, rows), block * width : (block + 1) * width],
                    sems.at[len(copies)],
                )
            )
    return copies


def start_all(copies):
    for copy in copies:
        copy.start()


def wait_all(copies):
    for copy in copies:
        copy.wait()


def normalize(value):
    centre = value - jnp.mean(value, axis=-1, keepdims=True)
    inv_std = lax.rsqrt(jnp.mean(centre * centre, axis=-1, keepdims=True) + norm_eps)
    return centre * inv_std, inv_std


def normalize_back(scaled, normed, inv_std):
    return inv_std * (
        scaled
        - jnp.mean(scaled, axis=-1, keepdims=True)
        - normed * jnp.mean(scaled * normed, axis=-1, keepdims=True)
    )


def attn_fwd_kernel(place_ref, len_ref, scale_ref, *refs, block, count):
    pieces = refs[:count]
    x_ref, bq_ref, bv_ref, q_ref, k_ref, v_ref, c_ref, lse_ref, w_ref, sems = refs[count:]
    rows, width = q_ref.shape
    total_width = x_ref.shape[1]
    group = pl.program_id(0)

    @pl.when(group == 0)
    def _():
        copies = attn_copies(place_ref, pieces, range(3), w_ref, sems)
        start_all(copies)
        wait_all(copies)

    x = x_ref[...]

    def part(index):
        return w_ref[:, pl.ds(pl.multiple_of(index * total_width + group * width, 128), width)]

    q_ref[...] = (dot(x, part(0)) * scale_ref[0] + bq_ref[...]).astype(bf16)
    k_ref[...] = (dot(x, part(1)) * scale_ref[1]).astype(bf16)
    v_ref[...] = (dot(x, part(2)) * scale_ref[2] + bv_ref[...]).astype(bf16)
    lane = lax.broadcasted_iota(jnp.int32, (1, 128), 1)

    def run(span):
        step = min(block, span)
        for pair in range(width // 128):
            cols = pl.ds(pair * 128, 128)
            for start in range(0, rows, step):
                low = start // span * span
                q_rows = q_ref[start : start + step, cols]
                k_rows = k_ref[low : low + span, cols]
                v_rows = v_ref[low : low + span, cols]
                found = []
                for head in range(2):
                    own = (lane < 64) if head == 0 else (lane >= 64)
                    q_own = jnp.where(own, q_rows, jnp.zeros_like(q_rows)) * jnp.asarray(0.125, bf16)
                    v_ones = jnp.where(own, v_rows, jnp.ones_like(v_rows))
                    scores = dot_last(q_own, k_rows)
                    top = jnp.max(scores, axis=1, keepdims=True)
                    found.append((dot(jnp.exp(scores - top).astype(bf16), v_ones), top))
                (out_a, top_a), (out_b, top_b) = found
                value = jnp.where(lane < 64, out_a, out_b)
                total = jnp.where(lane < 64, pltpu.roll(out_a, 64, 1), pltpu.roll(out_b, 64, 1))
                c_ref[start : start + step, cols] = (value / total).astype(bf16)
                lse_ref[start : start + step, cols] = jnp.where(lane < 64, top_a, top_b) + jnp.log(total)

    two = len_ref[0] < rows

    @pl.when(two)
    def _():
        run(rows // 2)

    @pl.when(jnp.logical_not(two))
    def _():
        run(rows)


def attn_fwd(place, lengths, scales, pieces, x, bias_q, bias_v):
    rows, width = x.shape
    group = 256
    count = len(pieces)

    def cols(height):
        return pl.BlockSpec((height, group), lambda g: (0, g))

    return pl.pallas_call(
        functools.partial(attn_fwd_kernel, block=512, count=count),
        grid=(width // group,),
        in_specs=[SMEM] * 3 + [ANY] * count
        + [pl.BlockSpec((rows, width), lambda g: (0, 0)), cols(1), cols(1)],
        out_specs=[cols(rows)] * 5,
        out_shape=[SDS((rows, width), bf16)] * 4 + [SDS((rows, width), f32)],
        scratch_shapes=[pltpu.VMEM((width, 3 * width), bf16), pltpu.SemaphoreType.DMA((3 * count,))],
        compiler_params=params(),
        cost_estimate=cost(20e9, 12e6, 12e6),
        name="attention_forward",
    )(place, lengths, scales, *pieces, x, bias_q, bias_v)


def order_rows(place_ref, source_t, dest):
    cores, half = dest.shape[:2]
    blocks = source_t.shape[0] * cores // half
    if cores == 1:
        dest[0] = source_t
        return
    blocks = 8
    size = source_t.shape[0] // blocks
    for block in range(blocks):
        at = pl.multiple_of(((block // 2) ^ place_ref[1]) * size, 16)
        dest[(block % 2) ^ place_ref[0], pl.ds(at, size), :] = source_t[block * size : (block + 1) * size]


def attn_bwd_kernel(
    place_ref, len_ref, q_ref, k_ref, v_ref, dc_ref, c_ref, lse_ref, x_ref, call_ref, dh_ref, *refs, block, cores,
):
    grads = refs[:cores]
    dqkv_ref, sum_q_ref, sum_v_ref, dk_acc, dv_acc, dq_acc, x_t, c_t, dqkv = refs[cores:]
    rows = q_ref.shape[0]
    pair = pl.program_id(0)
    pairs = pl.num_programs(0)
    span_cols = dqkv.shape[1] // 3
    lane = lax.broadcasted_iota(jnp.int32, (1, 128), 1)
    masks = [lane < 64, lane >= 64]

    @pl.when(pair == 0)
    def _():
        order_rows(place_ref, x_ref[...].T, x_t)
        order_rows(place_ref, call_ref[...].T, c_t)

    prod = (dc_ref[...].astype(f32) * c_ref[...].astype(f32)).T
    row_dots = [col_sum(prod[:64]), col_sum(prod[64:])]
    lse = lse_ref[...].T
    lse_rows = [lse[0:1], lse[64:65]]

    def run(span):
        step = min(block, span)
        for low in range(0, rows, span):
            k_rows = k_ref[low : low + span, :]
            v_rows = v_ref[low : low + span, :]
            k_cols = k_rows.astype(f32).T.astype(bf16)
            for start in range(low, low + span, step):
                q_rows = q_ref[start : start + step, :]
                dc_rows = dc_ref[start : start + step, :]
                probs, d_scores, q_own, dc_own, dq_parts = [], [], [], [], []
                for head in range(2):
                    q_head = jnp.where(masks[head], q_rows, jnp.zeros_like(q_rows)) * jnp.asarray(0.125, bf16)
                    dc_head = jnp.where(masks[head], dc_rows, jnp.zeros_like(dc_rows))
                    prob = jnp.exp(dot_last(k_rows, q_head) - lse_rows[head][:, start : start + step])
                    d_prob = dot_last(v_rows, dc_head)
                    d_score = (prob * (d_prob - row_dots[head][:, start : start + step])).astype(bf16)
                    probs.append(prob.astype(bf16))
                    d_scores.append(d_score)
                    q_own.append(q_head)
                    dc_own.append(dc_head)
                    dq_parts.append(dot(k_cols[head * 64 : head * 64 + 64], d_score))
                dq_acc[:, start : start + step] = jnp.concatenate(dq_parts, axis=0)
                dv = dot(jnp.concatenate(probs, axis=1), jnp.concatenate(dc_own, axis=0))
                dk = dot(jnp.concatenate(d_scores, axis=1), jnp.concatenate(q_own, axis=0))
                if start == low:
                    dv_acc[low : low + span, :] = dv
                    dk_acc[low : low + span, :] = dk
                else:
                    dv_acc[low : low + span, :] += dv
                    dk_acc[low : low + span, :] += dk

    two = len_ref[0] < rows

    @pl.when(two)
    def _():
        run(rows // 2)

    @pl.when(jnp.logical_not(two))
    def _():
        run(rows)

    dq = dq_acc[...].T * 0.125

    def put(part, value):
        dqkv[:, pl.ds(pl.multiple_of(part * span_cols + pair * 128, 128), 128)] = value.astype(bf16)

    put(0, dq)
    put(1, dk_acc[...])
    put(2, dv_acc[...])
    sum_q_ref[...] = jnp.broadcast_to(col_sum(dq), sum_q_ref.shape)
    sum_v_ref[...] = jnp.broadcast_to(col_sum(dv_acc[...]), sum_v_ref.shape)

    @pl.when(pair == pairs - 1)
    def _():
        dqkv_ref[...] = dqkv[...]
        for core in reversed(range(cores)):
            out = grads[core]
            spots, _, size, _ = out.shape
            for plane in range(4):
                left = x_t if plane < 3 else c_t
                right = dqkv[:, plane * span_cols : (plane + 1) * span_cols] if plane < 3 else dh_ref[...]
                value = dot(left[core], right).astype(bf16).reshape(spots, 1, size, span_cols)
                out[:, pl.ds(plane ^ place_ref[2], 1)] = value


def attn_bwd(place, lengths, q, k, v, dc, c, lse, x, dh_low, chunk, chunks, cores, spots):
    rows, width = q.shape
    pairs = width // 128 // chunks
    size = width // chunks
    cols = pl.BlockSpec((rows, 128), lambda g: (0, chunk * pairs + g))
    sums = pl.BlockSpec((8, 128), lambda g: (0, g))
    full = pl.BlockSpec((rows, width), lambda g: (0, 0))
    shape = (spots, 4, width // (cores * spots), size)
    return pl.pallas_call(
        functools.partial(attn_bwd_kernel, block=512, cores=cores),
        grid=(pairs,),
        in_specs=[SMEM] * 2 + [cols] * 6 + [full] * 2 + [pl.BlockSpec((rows, size), lambda g: (0, chunk))],
        out_specs=[pl.BlockSpec(shape, lambda g: (0, 0, 0, 0))] * cores
        + [pl.BlockSpec((rows, 3 * size), lambda g: (0, 0)), sums, sums],
        out_shape=[SDS(shape, bf16)] * cores + [SDS((rows, 3 * size), bf16)] + [SDS((8, size), f32)] * 2,
        scratch_shapes=[
            pltpu.VMEM((rows, 128), f32), pltpu.VMEM((rows, 128), f32), pltpu.VMEM((128, rows), f32),
            pltpu.VMEM((cores, width // cores, rows), bf16), pltpu.VMEM((cores, width // cores, rows), bf16),
            pltpu.VMEM((rows, 3 * size), bf16),
        ],
        compiler_params=params(),
        cost_estimate=cost(50e9 / chunks, 30e6 / chunks, 12e6 / chunks),
        name="attention_backward",
    )(place, lengths, q, k, v, dc, c, lse, x, c, dh_low)


def mid_fwd_kernel(place_ref, scale_ref, *refs, chunk, count):
    pieces = refs[:count]
    (up_ref, x_ref, c_ref, vec_ref, b1_ref, n1_ref, r1_ref, y1_ref, a_ref, gp_ref,
     wo_ref, w1_ref, out_sems, up_sems) = refs[count:]
    rows = x_ref.shape[0]
    first = pl.program_id(0) == 0

    @pl.when(first)
    def _():
        copies = attn_copies(place_ref, pieces, [3], wo_ref, out_sems)
        start_all(copies)
        start_all(up_copies(place_ref, up_ref, w1_ref, up_sems))
        wait_all(copies)

    residual = x_ref[...].astype(f32) + dot(c_ref[...], wo_ref[...]) * scale_ref[3] + vec_ref[2:3]
    normed, inv_std = normalize(residual)
    n1_ref[...] = normed
    r1_ref[...] = jnp.broadcast_to(inv_std, (rows, 128))
    y1 = (normed * vec_ref[3:4] + vec_ref[4:5]).astype(bf16)
    y1_ref[...] = y1

    @pl.when(first)
    def _():
        wait_all(up_copies(place_ref, up_ref, w1_ref, up_sems))

    for start in range(0, w1_ref.shape[1], chunk):
        cols = slice(start, start + chunk)
        u = dot(y1, w1_ref[:, cols]) * scale_ref[4] + b1_ref[:, cols]
        square = u * u
        half = 0.5 + 0.5 * jnp.tanh(u * (GELU_K + (GELU_K * GELU_C) * square))
        act = u * half
        a_ref[:, cols] = act.astype(bf16)
        gp_ref[:, cols] = (half + act * (1.0 - half) * (2 * GELU_K + (6 * GELU_K * GELU_C) * square)).astype(bf16)


def mid_fwd(place, scales, pieces, up, x, c, vec, bias_up):
    rows, width = x.shape
    hidden = bias_up.shape[1]
    tile = 512
    count = len(pieces)

    def row(size):
        return pl.BlockSpec((tile, size), lambda i: (i, 0))

    def full(arr):
        return pl.BlockSpec(arr.shape, lambda i: (0, 0))

    return pl.pallas_call(
        functools.partial(mid_fwd_kernel, chunk=256, count=count),
        grid=(rows // tile,),
        in_specs=[SMEM] * 2 + [ANY] * (count + 1) + [row(width), row(width), full(vec), full(bias_up)],
        out_specs=[row(width), row(128), row(width), row(hidden), row(hidden)],
        out_shape=[SDS((rows, width), f32), SDS((rows, 128), f32), SDS((rows, width), bf16),
                   SDS((rows, hidden), bf16), SDS((rows, hidden), bf16)],
        scratch_shapes=[pltpu.VMEM((width, width), bf16), pltpu.VMEM((width, hidden), bf16),
                        pltpu.SemaphoreType.DMA((count,)), pltpu.SemaphoreType.DMA((up.shape[0] * 4,))],
        compiler_params=params(),
        cost_estimate=cost(12e9, 25e6, 3e6),
        name="middle_forward",
    )(place, scales, *pieces, up, x, c, vec, bias_up)


def mid_bwd_kernel(place_ref, scale_ref, *refs, chunk, count):
    pieces = refs[:count]
    (up_ref, down_ref, n1_ref, r1_ref, a_ref, gp_ref, do_ref, vec_ref,
     out_ref, dz_ref, du_ref, dh_ref, dhb_ref, dc_ref, vg_ref, b1g_ref,
     wo_ref, w1_ref, w2_ref, out_sems, up_sems, down_sems) = refs[count:]
    first = pl.program_id(0) == 0

    @pl.when(first)
    def _():
        copies = down_copies(place_ref, down_ref, w2_ref, down_sems)
        start_all(copies)
        start_all(up_copies(place_ref, up_ref, w1_ref, up_sems))
        start_all(attn_copies(place_ref, pieces, [3], wo_ref, out_sems))
        wait_all(copies)
        vg_ref[...] = jnp.zeros_like(vg_ref)
        b1g_ref[...] = jnp.zeros_like(b1g_ref)

    g1, c1, b2, g2, c2 = [vec_ref[i : i + 1] for i in range(3, 8)]
    n1 = n1_ref[...]
    residual = n1 * g1 + c1 + dot_last(a_ref[...], w2_ref[...]) * scale_ref[5] + b2
    n2, r2 = normalize(residual)
    out_ref[...] = (n2 * g2 + c2).astype(bf16)
    d_out = do_ref[...].astype(f32)
    vg_ref[6:7] += col_sum(d_out * n2)
    vg_ref[7:8] += col_sum(d_out)
    dz = normalize_back(d_out * g2, n2, r2)
    vg_ref[5:6] += col_sum(dz)
    dz_low = dz.astype(bf16)
    dz_ref[...] = dz_low
    for start in range(0, w1_ref.shape[1], chunk):
        cols = slice(start, start + chunk)
        du = dot(dz_low, w2_ref[:, cols]) * scale_ref[5] * gp_ref[:, cols].astype(f32)
        b1g_ref[0:1, cols] += col_sum(du)
        du_ref[:, cols] = du.astype(bf16)

    @pl.when(first)
    def _():
        wait_all(up_copies(place_ref, up_ref, w1_ref, up_sems))
        wait_all(attn_copies(place_ref, pieces, [3], wo_ref, out_sems))

    dy = dz + dot_last(du_ref[...], w1_ref[...]) * scale_ref[4]
    vg_ref[3:4] += col_sum(dy * n1)
    vg_ref[4:5] += col_sum(dy)
    dh = normalize_back(dy * g1, n1, r1_ref[:, 0:1])
    vg_ref[2:3] += col_sum(dh)
    dh_ref[...] = dh
    dh_low = dh.astype(bf16)
    dhb_ref[...] = dh_low
    dc_ref[...] = (dot_last(dh_low, wo_ref[...]) * scale_ref[3]).astype(bf16)


def mid_bwd(place, scales, pieces, up, down, n1, r1, act, gelu_grad, d_out, vec):
    rows, width = n1.shape
    hidden = act.shape[1]
    tile = 256
    count = len(pieces)

    def row(size):
        return pl.BlockSpec((tile, size), lambda i: (i, 0))

    def full(arr):
        return pl.BlockSpec(arr.shape, lambda i: (0, 0))

    return pl.pallas_call(
        functools.partial(mid_bwd_kernel, chunk=256, count=count),
        grid=(rows // tile,),
        in_specs=[SMEM] * 2 + [ANY] * (count + 2)
        + [row(width), row(128), row(hidden), row(hidden), row(width), full(vec)],
        out_specs=[row(width), row(width), row(hidden), row(width), row(width), row(width),
                   pl.BlockSpec((8, width), lambda i: (0, 0)), pl.BlockSpec((8, hidden), lambda i: (0, 0))],
        out_shape=[SDS((rows, width), bf16), SDS((rows, width), bf16), SDS((rows, hidden), bf16),
                   SDS((rows, width), f32), SDS((rows, width), bf16), SDS((rows, width), bf16),
                   SDS((8, width), f32), SDS((8, hidden), f32)],
        scratch_shapes=[pltpu.VMEM((width, width), bf16), pltpu.VMEM((width, hidden), bf16),
                        pltpu.VMEM((width, hidden), bf16), pltpu.SemaphoreType.DMA((count,)),
                        pltpu.SemaphoreType.DMA((up.shape[0] * 4,)), pltpu.SemaphoreType.DMA((down.shape[0] * 4,))],
        compiler_params=params(),
        cost_estimate=cost(25e9, 45e6),
        name="middle_backward",
    )(place, scales, *pieces, up, down, n1, r1, act, gelu_grad, d_out, vec)


def up_grad_kernel(place_ref, left_ref, right_ref, *refs, cores):
    outs, left_t = refs[:cores], refs[cores]

    @pl.when(pl.program_id(0) == 0)
    def _():
        order_rows(place_ref, left_ref[...].T, left_t)

    for core in reversed(range(cores)):
        outs[core][...] = dot(left_t[core], right_ref[...]).astype(bf16).reshape(outs[core].shape)


def up_grad(place, left, right, cores, spots):
    rows, width = left.shape
    size = right.shape[1] // 4
    block = (spots, 1, width // (cores * spots), size)
    return pl.pallas_call(
        functools.partial(up_grad_kernel, cores=cores),
        grid_spec=pltpu.PrefetchScalarGridSpec(
            num_scalar_prefetch=1,
            grid=(4,),
            in_specs=[pl.BlockSpec((rows, width), lambda i, place: (0, 0)),
                      pl.BlockSpec((rows, size), lambda i, place: (0, i))],
            out_specs=[pl.BlockSpec(block, lambda i, place: (0, i ^ place[2], 0, 0))] * cores,
            scratch_shapes=[pltpu.VMEM((cores, width // cores, rows), bf16)],
        ),
        out_shape=[SDS((spots, 4) + block[2:], bf16)] * cores,
        compiler_params=params(),
        cost_estimate=cost(8e9, 14e6),
        name="up_gradient",
    )(place, left, right)


def down_grad_kernel(place_ref, left_ref, right_ref, *refs, cores):
    outs, left_t = refs[:cores], refs[cores]
    slots, size = outs[0].shape[1:3]

    @pl.when(pl.program_id(0) == 0)
    def _():
        turned = left_ref[...].T
        for slot in range(slots):
            at = pl.multiple_of((slot ^ place_ref[2]) * size, 16)
            left_t[pl.ds(at, size), :] = turned[slot * size : (slot + 1) * size]

    value = dot(left_t[...], right_ref[...]).astype(bf16)
    if cores == 1:
        outs[0][...] = value.reshape(outs[0].shape)
        return
    cols = value.shape[1] // 2
    low, high = value[:, :cols], value[:, cols:]
    even = place_ref[0] == 0
    outs[1][...] = jnp.where(even, high, low).reshape(outs[1].shape)
    outs[0][...] = jnp.where(even, low, high).reshape(outs[0].shape)


def down_grad(place, left, right, cores, spots):
    rows, width = left.shape
    size = right.shape[1] // spots
    block = (1, 4, width // 4, size // cores)
    return pl.pallas_call(
        functools.partial(down_grad_kernel, cores=cores),
        grid_spec=pltpu.PrefetchScalarGridSpec(
            num_scalar_prefetch=1,
            grid=(spots,),
            in_specs=[pl.BlockSpec((rows, width), lambda i, place: (0, 0)),
                      pl.BlockSpec((rows, size), lambda i, place: (0, i))],
            out_specs=[pl.BlockSpec(block, lambda i, place: (i ^ place[1], 0, 0, 0))] * cores,
            scratch_shapes=[pltpu.VMEM((width, rows), bf16)],
        ),
        out_shape=[SDS((spots,) + block[1:], bf16)] * cores,
        compiler_params=params(),
        cost_estimate=cost(8e9, 14e6),
        name="down_gradient",
    )(place, left, right)


def input_grad_kernel(place_ref, scale_ref, *refs, count, chunks):
    pieces = refs[:count]
    parts = refs[count : count + chunks]
    dh_ref, out_ref, w_ref, sems = refs[count + chunks :]
    width = dh_ref.shape[1]
    size = width // chunks

    @pl.when(pl.program_id(0) == 0)
    def _():
        copies = attn_copies(place_ref, pieces, range(3), w_ref, sems)
        start_all(copies)
        wait_all(copies)

    total = dh_ref[...]
    for plane in range(3):
        product = None
        for chunk, part in enumerate(parts):
            start = plane * width + chunk * size
            more = dot_last(part[:, plane * size : (plane + 1) * size], w_ref[:, start : start + size])
            product = more if product is None else product + more
        total = total + product * scale_ref[plane]
    out_ref[...] = total.astype(bf16)


def input_grad(place, scales, pieces, parts, dh):
    rows, width = dh.shape
    tile = 512
    count, chunks = len(pieces), len(parts)

    def row(size):
        return pl.BlockSpec((tile, size), lambda i: (i, 0))

    return pl.pallas_call(
        functools.partial(input_grad_kernel, count=count, chunks=chunks),
        grid=(rows // tile,),
        in_specs=[SMEM] * 2 + [ANY] * count + [row(p.shape[1]) for p in parts] + [row(width)],
        out_specs=row(width),
        out_shape=SDS((rows, width), bf16),
        scratch_shapes=[pltpu.VMEM((width, 3 * width), bf16), pltpu.SemaphoreType.DMA((3 * count,))],
        compiler_params=params(),
        cost_estimate=cost(9e9, 2 * (rows * width * 6 + 3 * width * width)),
        name="input_gradient",
    )(place, scales, *pieces, *parts, dh)


def swap(value, axis, mask):
    count = lax.axis_size(axis)
    return lax.ppermute(value, axis, [(i, i ^ mask) for i in range(count)])


def bits(axis):
    return [1 << b for b in range(lax.axis_size(axis).bit_length() - 1)]


def doubling_gather(value, axis, dim):
    index = lax.axis_index(axis)
    for bit in bits(axis):
        other = swap(value, axis, bit)
        high = (index & bit) != 0
        value = jnp.concatenate(
            [jnp.where(high, other, value), jnp.where(high, value, other)], axis=dim
        )
    return value


def doubling_sum(value):
    for axis in ("dp", "shard"):
        for bit in bits(axis):
            value = value + swap(value, axis, bit)
    return value


def shard_slots(block):
    return jnp.stack([block] + [swap(block, "shard", m) for m in (1, 2, 3)])


def scatter_sum(mine, theirs):
    got = swap(theirs, "dp", 1)
    sent = []
    for spot in (3, 2, 1):
        part = (mine[spot].astype(f32) + got[spot].astype(f32)).astype(bf16)
        sent.append(swap(part, "dp", 2 * spot))
    slots = [None] * 4
    for slot in (3, 2, 1, 0):
        total = mine[0, slot].astype(f32) + got[0, slot].astype(f32)
        for part in sent:
            total = total + part[slot].astype(f32)
        slots[slot] = total
    total = slots[0]
    for slot in (3, 2, 1):
        total = total + swap(slots[slot].astype(bf16), "shard", slot).astype(f32)
    return total


def adam_update(gradient, master, first_old, second_old, average, step_rate, decay_rate):
    first_new = beta_first * first_old + (1.0 - beta_first) * gradient
    second_new = beta_second * second_old + (1.0 - beta_second) * gradient * gradient
    first_hat = first_new / (1.0 - beta_first**STEP)
    second_hat = second_new / (1.0 - beta_second**STEP)
    master_new = master - step_rate * (
        first_hat / (jnp.sqrt(second_hat) + adam_eps) + decay_rate * master
    )
    average_new = average_keep * average + (1.0 - average_keep) * master_new
    return (first_new, second_new, master_new, average_new)


def on_device(
    tokens, out_grad, first_lengths, quant_scales, attn_quant, up_quant, down_quant,
    attn_master, attn_first, attn_second, attn_average,
    up_master, up_first, up_second, up_average,
    down_master, down_first, down_second, down_average,
    vector_master, vector_first, vector_second, vector_average,
):
    width = tokens.shape[1]
    dp_index, shard_index = lax.axis_index("dp"), lax.axis_index("shard")
    small = lax.axis_size("dp") == 8 and lax.axis_size("shard") == 4 and attn_quant.shape == (96, 768)
    gather = functools.partial(lax.all_gather, tiled=True)
    scatter = functools.partial(lax.psum_scatter, tiled=True)
    chunks = 2
    down_turned = down_quant.T
    vec_w = doubling_gather(doubling_gather(vector_master.astype(bf16), "shard", 1), "dp", 0)
    vec = vec_w.astype(f32).T
    bias_up = vec[8:].reshape(1, -1)
    vec = vec[:8]
    if small:
        cores, spots = 2, 4
        place = jnp.stack([dp_index & 1, dp_index >> 1, shard_index]).astype(jnp.int32)
        own = shard_slots(attn_quant)
        pieces = [own] + [swap(own, "dp", 2 * spot) for spot in (1, 2, 3)]
        pieces = pieces + [swap(piece, "dp", 1) for piece in pieces]
        up = lax.all_gather(shard_slots(up_quant), "dp")
        down = lax.all_gather(shard_slots(down_turned), "dp")
    else:
        cores, spots = 1, 1
        place = jnp.zeros((3,), jnp.int32)
        attn_w = gather(gather(attn_quant, "shard", axis=1), "dp", axis=0)
        up_w = gather(gather(up_quant, "shard", axis=1), "dp", axis=0)
        down_w = gather(gather(down_turned, "shard", axis=0), "dp", axis=1)
        pieces = [attn_w.reshape(width, 4, width).transpose(1, 0, 2)]
        up = up_w.reshape(1, width, 4, -1).transpose(0, 2, 1, 3)
        down = down_w.reshape(1, 4, width // 4, -1)

    q, k, v, c, lse = attn_fwd(place, first_lengths, quant_scales, pieces, tokens, vec[0:1], vec[1:2])
    n1, r1, y1, act, gelu_grad = mid_fwd(place, quant_scales, pieces, up, tokens, c, vec, bias_up)
    layer_out, dz, du, dh, dh_low, dc, vec_grad, b1_grad = mid_bwd(
        place, quant_scales, pieces, up, down, n1, r1, act, gelu_grad, out_grad, vec
    )
    down_parts = down_grad(place, dz, act, cores, spots)
    up_parts = up_grad(place, y1, du, cores, spots)
    attn_parts, d_parts, sums_q, sums_v = [], [], [], []
    for chunk in range(chunks):
        *parts, d_part, sum_q, sum_v = attn_bwd(
            place, first_lengths, q, k, v, dc, c, lse, tokens, dh_low, chunk, chunks, cores, spots
        )
        attn_parts.append(parts)
        d_parts.append(d_part)
        sums_q.append(sum_q[0:1])
        sums_v.append(sum_v[0:1])
    input_gradient = input_grad(place, quant_scales, pieces, d_parts, dh)

    vec_rows = jnp.concatenate(
        [jnp.concatenate(sums_q, axis=1), jnp.concatenate(sums_v, axis=1), vec_grad[2:8], b1_grad[0:1].reshape(-1, width)],
        axis=0,
    )
    vec_total = doubling_sum(vec_rows)
    rows_own, cols_own = vector_master.shape
    own_vector = lax.dynamic_slice(vec_total, (shard_index * cols_own, dp_index * rows_own), (cols_own, rows_own)).T
    if small:
        own_down = scatter_sum(*down_parts)
        own_up = scatter_sum(*up_parts)
        own_attn = jnp.concatenate([scatter_sum(*parts) for parts in attn_parts], axis=1)
    else:
        grad_down = down_parts[0].reshape(width, -1)
        grad_up = up_parts[0][0].transpose(1, 0, 2).reshape(width, -1)
        grad_attn = jnp.concatenate([parts[0][0] for parts in attn_parts], axis=2)
        grad_attn = grad_attn.transpose(1, 0, 2).reshape(width, -1)
        own_down = scatter(scatter(grad_down, "dp", scatter_dimension=1), "shard", scatter_dimension=0).astype(f32)
        own_up = scatter(scatter(grad_up, "dp", scatter_dimension=0), "shard", scatter_dimension=1).astype(f32)
        own_attn = scatter(scatter(grad_attn, "dp", scatter_dimension=0), "shard", scatter_dimension=1).astype(f32)
    own_down = own_down.T
    local_squares = (
        jnp.sum(own_attn * own_attn)
        + jnp.sum(own_up * own_up)
        + jnp.sum(own_down * own_down)
        + jnp.sum(own_vector * own_vector)
    )
    grad_norm = jnp.sqrt(doubling_sum(jnp.broadcast_to(local_squares, (8, 128)))[0, 0])
    factor = jnp.minimum(1.0, clip_limit / (grad_norm + norm_eps))
    attn_new = adam_update(own_attn * factor, attn_master, attn_first, attn_second, attn_average, matrix_rate, matrix_decay)
    up_new = adam_update(own_up * factor, up_master, up_first, up_second, up_average, matrix_rate, matrix_decay)
    down_new = adam_update(own_down * factor, down_master, down_first, down_second, down_average, matrix_rate, matrix_decay)
    vector_new = adam_update(own_vector * factor, vector_master, vector_first, vector_second, vector_average, vector_rate, 0.0)
    return (layer_out, input_gradient, grad_norm, *attn_new, *up_new, *down_new, *vector_new)


def solution(mesh):
    rows = P(("dp", "shard"), None)
    block = P("dp", "shard")
    in_specs = (rows, rows, P(("dp", "shard")), P()) + (block,) * 19
    out_specs = (rows, rows, P()) + (block,) * 16
    return jax.shard_map(
        on_device, mesh=mesh, in_specs=in_specs, out_specs=out_specs, check_vma=False
    )
```

```python
import functools
import math

import jax
import jax.numpy as jnp
from jax import lax
from jax.experimental import pallas as pl
from jax.experimental.pallas import tpu as pltpu
from jax.sharding import PartitionSpec as P

HEAD_DIM = 64
STEP = 10

norm_eps = 1e-06
clip_limit = 1.0
beta_first = 0.9
beta_second = 0.999
adam_eps = 1e-08
matrix_rate = 0.08
vector_rate = 0.5
matrix_decay = 0.01
average_keep = 0.9

VMEM = 58 * 2**20
GELU_K = math.sqrt(2.0 / math.pi)
GELU_C = 0.044715
f32 = jnp.float32
bf16 = jnp.bfloat16
SDS = jax.ShapeDtypeStruct


def dot(left, right):
    return jnp.dot(left, right, preferred_element_type=f32)


def dot_last(left, right):
    return lax.dot_general(left, right, (((1,), (1,)), ((), ())), preferred_element_type=f32)


def col_sum(value):
    return jnp.sum(value, axis=0, keepdims=True)


def params(**extra):
    return pltpu.CompilerParams(vmem_limit_bytes=VMEM, **extra)


def cost(flops, moved, trans=0):
    return pl.CostEstimate(flops=int(flops), bytes_accessed=int(moved), transcendentals=int(trans))


SMEM = pl.BlockSpec(memory_space=pltpu.SMEM)
ANY = pl.BlockSpec(memory_space=pl.ANY)


def piece_row(place_ref, index, count):
    if count == 1:
        return 0
    half = count // 2
    return ((place_ref[1] ^ (index % half)) * 2) + (place_ref[0] ^ (index // half))


def block_copies(place_ref, pieces, blocks, dest, sems):
    count = len(pieces)
    rows, width = dest.shape[0] // count, pieces[0].shape[1]
    copies = []
    for at, block in enumerate(blocks):
        for index, piece in enumerate(pieces):
            row = pl.multiple_of(piece_row(place_ref, index, count) * rows, 16)
            copies.append(
                pltpu.make_async_copy(
                    piece.at[block * rows : (block + 1) * rows],
                    dest.at[pl.ds(row, rows), at * width : (at + 1) * width],
                    sems.at[len(copies)],
                )
            )
    return copies


def down_copies(source, dest, sems):
    blocks, slots, rows, width = source.shape
    copies = []
    for block in range(blocks):
        for slot in range(slots):
            copies.append(
                pltpu.make_async_copy(
                    source.at[block, slot],
                    dest.at[slot * rows : (slot + 1) * rows, block * width : (block + 1) * width],
                    sems.at[len(copies)],
                )
            )
    return copies


def start_all(copies):
    for copy in copies:
        copy.start()


def wait_all(copies):
    for copy in copies:
        copy.wait()


def normalize(value):
    centre = value - jnp.mean(value, axis=-1, keepdims=True)
    inv_std = lax.rsqrt(jnp.mean(centre * centre, axis=-1, keepdims=True) + norm_eps)
    return centre * inv_std, inv_std


def normalize_back(scaled, normed, inv_std):
    return inv_std * (
        scaled
        - jnp.mean(scaled, axis=-1, keepdims=True)
        - normed * jnp.mean(scaled * normed, axis=-1, keepdims=True)
    )


def attn_stack_kernel(place_ref, *refs):
    blocks, qkv_ref, out_ref = refs[:4], refs[4], refs[5]
    rows = out_ref.shape[0]
    vectors = None
    for slot, block in enumerate(blocks):
        plane = slot ^ place_ref[2]
        more = pltpu.roll(block[rows:, :].astype(f32), 3 * plane, 0)
        vectors = more if vectors is None else vectors + more

        @pl.when(plane < 3)
        def _():
            qkv_ref[pl.ds(pl.multiple_of(plane * rows, 16), rows), :] = block[:rows, :]

        @pl.when(plane == 3)
        def _():
            out_ref[...] = block[:rows, :]

    qkv_ref[3 * rows :, :] = vectors.astype(bf16)


def attn_stack(place, blocks):
    rows, width = blocks[0].shape
    rows -= 16
    return pl.pallas_call(
        attn_stack_kernel,
        in_specs=[SMEM] + [pl.BlockSpec(memory_space=pltpu.VMEM)] * 4,
        out_specs=[pl.BlockSpec(memory_space=pltpu.VMEM)] * 2,
        out_shape=[SDS((3 * rows + 16, width), bf16), SDS((rows, width), bf16)],
        compiler_params=params(),
        cost_estimate=cost(1e6, 1e6),
        name="attention_weight_order",
    )(place, *blocks)


def stack_kernel(place_ref, *refs, which, extra):
    blocks, out_ref = refs[:4], refs[-1]
    rows = blocks[0].shape[0]
    for slot, block in enumerate(blocks):
        at = pl.multiple_of((slot ^ place_ref[which]) * rows, 16)
        out_ref[pl.ds(at, rows), :] = block[...]
    if extra:
        out_ref[4 * rows :, :] = refs[4][...]


def stack(place, blocks, which, *extra, deps=()):
    rows, width = blocks[0].shape
    return pl.pallas_call(
        functools.partial(stack_kernel, which=which, extra=len(extra)),
        in_specs=[SMEM] + [pl.BlockSpec(memory_space=pltpu.VMEM)] * (4 + len(extra)) + [ANY] * len(deps),
        out_specs=pl.BlockSpec(memory_space=pltpu.VMEM),
        out_shape=SDS((rows * (4 + len(extra)), width), bf16),
        compiler_params=params(),
        cost_estimate=cost(1e6, 1e6),
        name="weight_order",
    )(place, *blocks, *extra, *deps)


def attn_fwd_kernel(place_ref, len_ref, scale_ref, *refs, block, count, deps):
    pieces = refs[:count]
    refs = refs[:count] + refs[count + deps :]
    x_ref, q_ref, k_ref, v_ref, c_ref, lse_ref, vec_ref, w_ref, packed, sems, vec_sems = refs[count:]
    rows, width = q_ref.shape
    total_width = x_ref.shape[1]
    group = pl.program_id(0)

    @pl.when(group == 0)
    def _():
        copies = block_copies(place_ref, pieces, range(3), w_ref, sems)
        top = pieces[0].shape[0] - 16
        for index, piece in enumerate(pieces):
            copies.append(pltpu.make_async_copy(piece.at[top : top + 16], packed.at[index], vec_sems.at[index]))
        start_all(copies)
        wait_all(copies)
        vectors = None
        for index in range(count):
            shift = piece_row(place_ref, index, count) * (total_width // count)
            more = packed[index].astype(f32)
            more = more if count == 1 else pltpu.roll(more, shift, 1)
            vectors = more if vectors is None else vectors + more
        vec_ref[...] = vectors

    x = x_ref[...]

    def part(index):
        return w_ref[:, pl.ds(pl.multiple_of(index * total_width + group * width, 128), width)]

    cols = pl.ds(pl.multiple_of(group * width, 128), width)
    q_ref[...] = (dot(x, part(0)) * scale_ref[0] + vec_ref[0:1, cols]).astype(bf16)
    k_ref[...] = (dot(x, part(1)) * scale_ref[1]).astype(bf16)
    v_ref[...] = (dot(x, part(2)) * scale_ref[2] + vec_ref[1:2, cols]).astype(bf16)
    lane = lax.broadcasted_iota(jnp.int32, (1, 128), 1)

    def run(span):
        step = min(block, span)
        for pair in range(width // 128):
            cols = pl.ds(pair * 128, 128)
            for start in range(0, rows, step):
                low = start // span * span
                q_rows = q_ref[start : start + step, cols]
                k_rows = k_ref[low : low + span, cols]
                v_rows = v_ref[low : low + span, cols]
                found = []
                for head in range(2):
                    own = (lane < 64) if head == 0 else (lane >= 64)
                    q_own = jnp.where(own, q_rows, jnp.zeros_like(q_rows)) * jnp.asarray(0.125, bf16)
                    v_ones = jnp.where(own, v_rows, jnp.ones_like(v_rows))
                    scores = dot_last(q_own, k_rows)
                    top = jnp.max(scores, axis=1, keepdims=True)
                    found.append((dot(jnp.exp(scores - top).astype(bf16), v_ones), top))
                (out_a, top_a), (out_b, top_b) = found
                value = jnp.where(lane < 64, out_a, out_b)
                total = jnp.where(lane < 64, pltpu.roll(out_a, 64, 1), pltpu.roll(out_b, 64, 1))
                c_ref[start : start + step, cols] = (value / total).astype(bf16)
                lse_ref[start : start + step, cols] = jnp.where(lane < 64, top_a, top_b) + jnp.log(total)

    two = len_ref[0] < rows

    @pl.when(two)
    def _():
        run(rows // 2)

    @pl.when(jnp.logical_not(two))
    def _():
        run(rows)


def attn_fwd(place, lengths, scales, pieces, x, deps):
    rows, width = x.shape
    group = 256
    count = len(pieces)
    cols = pl.BlockSpec((rows, group), lambda g: (0, g))
    return pl.pallas_call(
        functools.partial(attn_fwd_kernel, block=512, count=count, deps=len(deps)),
        grid=(width // group,),
        in_specs=[SMEM] * 3 + [ANY] * (count + len(deps)) + [pl.BlockSpec((rows, width), lambda g: (0, 0))],
        out_specs=[cols] * 5 + [pl.BlockSpec((16, width), lambda g: (0, 0))],
        out_shape=[SDS((rows, width), bf16)] * 4 + [SDS((rows, width), f32), SDS((16, width), f32)],
        scratch_shapes=[pltpu.VMEM((width, 3 * width), bf16), pltpu.VMEM((count, 16, width), bf16),
                        pltpu.SemaphoreType.DMA((3 * count,)), pltpu.SemaphoreType.DMA((count,))],
        compiler_params=params(),
        cost_estimate=cost(20e9, 12e6, 12e6),
        name="attention_forward",
    )(place, lengths, scales, *pieces, *deps, x)


def order_rows(place_ref, source_t, dest):
    cores = dest.shape[0]
    if cores == 1:
        dest[0] = source_t
        return
    blocks = 8
    size = source_t.shape[0] // blocks
    for block in range(blocks):
        at = pl.multiple_of(((block // 2) ^ place_ref[1]) * size, 16)
        dest[(block % 2) ^ place_ref[0], pl.ds(at, size), :] = source_t[block * size : (block + 1) * size]


def attn_bwd_kernel(
    place_ref, len_ref, q_ref, k_ref, v_ref, dc_ref, c_ref, lse_ref, x_ref, call_ref, dh_ref, *refs, block, cores, last, deps,
):
    refs = refs[deps:]
    if last:
        before_a_ref, before_b_ref, vg_ref, b1g_ref, *refs = refs
    grads = refs[:cores]
    dqkv_ref, sum_ref, dk_acc, dv_acc, dq_acc, x_t, c_t = refs[cores:]
    rows = q_ref.shape[0]
    pair = pl.program_id(0)
    pairs = pl.num_programs(0)
    span_cols = dqkv_ref.shape[1] // 3
    total_width = x_ref.shape[1]
    lane = lax.broadcasted_iota(jnp.int32, (1, 128), 1)
    masks = [lane < 64, lane >= 64]

    @pl.when(pair == 0)
    def _():
        order_rows(place_ref, x_ref[...].T, x_t)
        order_rows(place_ref, call_ref[...].T, c_t)

    prod = (dc_ref[...].astype(f32) * c_ref[...].astype(f32)).T
    row_dots = [col_sum(prod[:64]), col_sum(prod[64:])]
    lse = lse_ref[...].T
    lse_rows = [lse[0:1], lse[64:65]]

    def run(span):
        step = min(block, span)
        for low in range(0, rows, span):
            k_rows = k_ref[low : low + span, :]
            v_rows = v_ref[low : low + span, :]
            k_cols = k_rows.astype(f32).T.astype(bf16)
            for start in range(low, low + span, step):
                q_rows = q_ref[start : start + step, :]
                dc_rows = dc_ref[start : start + step, :]
                probs, d_scores, q_own, dc_own, dq_parts = [], [], [], [], []
                for head in range(2):
                    q_head = jnp.where(masks[head], q_rows, jnp.zeros_like(q_rows)) * jnp.asarray(0.125, bf16)
                    dc_head = jnp.where(masks[head], dc_rows, jnp.zeros_like(dc_rows))
                    prob = jnp.exp(dot_last(k_rows, q_head) - lse_rows[head][:, start : start + step])
                    d_prob = dot_last(v_rows, dc_head)
                    d_score = (prob * (d_prob - row_dots[head][:, start : start + step])).astype(bf16)
                    probs.append(prob.astype(bf16))
                    d_scores.append(d_score)
                    q_own.append(q_head)
                    dc_own.append(dc_head)
                    dq_parts.append(dot(k_cols[head * 64 : head * 64 + 64], d_score))
                dq_acc[:, start : start + step] = jnp.concatenate(dq_parts, axis=0)
                dv = dot(jnp.concatenate(probs, axis=1), jnp.concatenate(dc_own, axis=0))
                dk = dot(jnp.concatenate(d_scores, axis=1), jnp.concatenate(q_own, axis=0))
                if start == low:
                    dv_acc[low : low + span, :] = dv
                    dk_acc[low : low + span, :] = dk
                else:
                    dv_acc[low : low + span, :] += dv
                    dk_acc[low : low + span, :] += dk

    two = len_ref[0] < rows

    @pl.when(two)
    def _():
        run(rows // 2)

    @pl.when(jnp.logical_not(two))
    def _():
        run(rows)

    dq = dq_acc[...].T * 0.125

    def put(part, value):
        at = pl.multiple_of(part * span_cols + pair * 128, 128)
        dqkv_ref[:, pl.ds(at, 128)] = value.astype(bf16)

    put(0, dq)
    put(1, dk_acc[...])
    put(2, dv_acc[...])
    low = total_width - span_cols if last else 0
    here = pl.ds(pl.multiple_of(low + pair * 128, 128), 128)
    if last:
        @pl.when(pair == 0)
        def _():
            sum_ref[0:2, : low // 2] = before_a_ref[0:2, :]
            sum_ref[0:2, low // 2 : low] = before_b_ref[0:2, :]
            sum_ref[2:8, :] = vg_ref[2:8, :]
            for row in range(b1g_ref.shape[1] // total_width):
                sum_ref[8 + row : 9 + row, :] = b1g_ref[0:1, row * total_width : (row + 1) * total_width]

    sum_ref[0:1, here] = col_sum(dq)
    sum_ref[1:2, here] = col_sum(dv_acc[...])

    @pl.when(pair == pairs - 1)
    def _():
        for core in reversed(range(cores)):
            out = grads[core]
            spots, _, size, _ = out.shape
            size = x_t.shape[1] // spots
            for plane in range(4):
                left = x_t if plane < 3 else c_t
                right = dqkv_ref[:, plane * span_cols : (plane + 1) * span_cols] if plane < 3 else dh_ref[...]
                value = dot(left[core], right).astype(bf16).reshape(spots, 1, size, span_cols)
                out[:, pl.ds(plane ^ place_ref[2], 1), :size] = value
        if last and cores == 2:
            row = lax.broadcasted_iota(jnp.int32, (16, span_cols), 0)
            col = lax.broadcasted_iota(jnp.int32, (16, span_cols), 1)
            kept = (row < 3) & (col < size)
            even = place_ref[0] == 0
            for plane in range(4):
                rows_here = sum_ref[...] if plane == 0 else pltpu.roll(sum_ref[...], 16 - 3 * plane, 0)
                for spot in range(4):
                    tiles = []
                    for core in range(2):
                        start = (2 * spot + core) * size
                        turned = rows_here if start == 0 else pltpu.roll(rows_here, total_width - start, 1)
                        tiles.append(jnp.where(kept, turned[:, :span_cols], 0.0).astype(bf16))
                    for core in range(2):
                        tile = jnp.where(even, tiles[core], tiles[1 - core])
                        grads[core][spot ^ place_ref[1], plane ^ place_ref[2], size:, :] = tile


def attn_bwd(place, lengths, q, k, v, dc, c, lse, x, dh_low, first, pairs, cores, spots, deps, before=None):
    rows, width = q.shape
    last = before is not None
    size = pairs * 128
    cols = pl.BlockSpec((rows, 128), lambda g: (0, first + g))
    full = pl.BlockSpec((rows, width), lambda g: (0, 0))

    def whole(shape):
        return pl.BlockSpec(shape, lambda g: (0,) * len(shape))

    depth = width // (cores * spots)
    shape = (spots, 4, depth + (16 if last and cores == 2 else 0), size)
    sums = (16, width if last else size)
    more = list(before) if last else []
    return pl.pallas_call(
        functools.partial(attn_bwd_kernel, block=512, cores=cores, last=last, deps=len(deps)),
        grid=(pairs,),
        in_specs=[SMEM] * 2 + [cols] * 6 + [full] * 2
        + [pl.BlockSpec((rows, size), lambda g: (0, first // pairs))] + [ANY] * len(deps) + [whole(m.shape) for m in more],
        out_specs=[whole(shape)] * cores + [whole((rows, 3 * size)), whole(sums)],
        out_shape=[SDS(shape, bf16)] * cores + [SDS((rows, 3 * size), bf16), SDS(sums, f32)],
        scratch_shapes=[
            pltpu.VMEM((rows, 128), f32), pltpu.VMEM((rows, 128), f32), pltpu.VMEM((128, rows), f32),
            pltpu.VMEM((cores, width // cores, rows), bf16), pltpu.VMEM((cores, width // cores, rows), bf16),
        ],
        compiler_params=params(),
        cost_estimate=cost(50e9 * size / width, 30e6 * size / width, 12e6 * size / width),
        name="attention_backward",
    )(place, lengths, q, k, v, dc, c, lse, x, c, dh_low, *deps, *more)


def mid_fwd_kernel(place_ref, scale_ref, *refs, chunk, count):
    pieces = refs[:count]
    (x_ref, c_ref, vec_ref, n1_ref, r1_ref, y1_ref, a_ref, gp_ref,
     wo_ref, w1_ref, out_sems, up_sems) = refs[count:]
    rows = x_ref.shape[0]
    first = pl.program_id(0) == 0

    @pl.when(first)
    def _():
        copies = block_copies(place_ref, pieces, [4], wo_ref, out_sems)
        start_all(copies)
        start_all(block_copies(place_ref, pieces, range(4), w1_ref, up_sems))
        wait_all(copies)

    residual = x_ref[...].astype(f32) + dot(c_ref[...], wo_ref[...]) * scale_ref[3] + vec_ref[2:3]
    normed, inv_std = normalize(residual)
    n1_ref[...] = normed
    r1_ref[...] = jnp.broadcast_to(inv_std, (rows, 128))
    y1 = (normed * vec_ref[3:4] + vec_ref[4:5]).astype(bf16)
    y1_ref[...] = y1

    @pl.when(first)
    def _():
        wait_all(block_copies(place_ref, pieces, range(4), w1_ref, up_sems))

    for start in range(0, w1_ref.shape[1], chunk):
        cols = slice(start, start + chunk)
        block, at = divmod(start, x_ref.shape[1])
        bias = vec_ref[8 + block : 9 + block, at : at + chunk]
        u = dot(y1, w1_ref[:, cols]) * scale_ref[4] + bias
        square = u * u
        half = 0.5 + 0.5 * jnp.tanh(u * (GELU_K + (GELU_K * GELU_C) * square))
        act = u * half
        a_ref[:, cols] = act.astype(bf16)
        gp_ref[:, cols] = (half + act * (1.0 - half) * (2 * GELU_K + (6 * GELU_K * GELU_C) * square)).astype(bf16)


def mid_fwd(place, scales, pieces, x, c, vec):
    rows, width = x.shape
    hidden = 4 * pieces[0].shape[1]
    tile = 512
    count = len(pieces)

    def row(size):
        return pl.BlockSpec((tile, size), lambda i: (i, 0))

    def full(arr):
        return pl.BlockSpec(arr.shape, lambda i: (0, 0))

    return pl.pallas_call(
        functools.partial(mid_fwd_kernel, chunk=256, count=count),
        grid=(rows // tile,),
        in_specs=[SMEM] * 2 + [ANY] * count + [row(width), row(width), full(vec)],
        out_specs=[row(width), row(128), row(width), row(hidden), row(hidden)],
        out_shape=[SDS((rows, width), f32), SDS((rows, 128), f32), SDS((rows, width), bf16),
                   SDS((rows, hidden), bf16), SDS((rows, hidden), bf16)],
        scratch_shapes=[pltpu.VMEM((width, width), bf16), pltpu.VMEM((width, hidden), bf16),
                        pltpu.SemaphoreType.DMA((count,)), pltpu.SemaphoreType.DMA((4 * count,))],
        compiler_params=params(),
        cost_estimate=cost(12e9, 25e6, 3e6),
        name="middle_forward",
    )(place, scales, *pieces, x, c, vec)


def second_norm_kernel(
    scale_ref, down_ref, n1_ref, a_ref, do_ref, vec_ref, out_ref, dz_ref, dzb_ref, vg_ref, w2_ref, down_sems
):

    @pl.when(pl.program_id(0) == 0)
    def _():
        copies = down_copies(down_ref, w2_ref, down_sems)
        start_all(copies)
        vg_ref[...] = jnp.zeros_like(vg_ref)
        wait_all(copies)

    g1, c1, b2, g2, c2 = [vec_ref[i : i + 1] for i in range(3, 8)]
    residual = n1_ref[...] * g1 + c1 + dot_last(a_ref[...], w2_ref[...]) * scale_ref[5] + b2
    n2, r2 = normalize(residual)
    out_ref[...] = (n2 * g2 + c2).astype(bf16)
    d_out = do_ref[...].astype(f32)
    vg_ref[6:7] += col_sum(d_out * n2)
    vg_ref[7:8] += col_sum(d_out)
    dz = normalize_back(d_out * g2, n2, r2)
    vg_ref[5:6] += col_sum(dz)
    dz_ref[...] = dz
    dzb_ref[...] = dz.astype(bf16)


def second_norm(scales, down, n1, act, d_out, vec):
    rows, width = n1.shape
    hidden = act.shape[1]
    tile = 256

    def row(size):
        return pl.BlockSpec((tile, size), lambda i: (i, 0))

    return pl.pallas_call(
        second_norm_kernel,
        grid=(rows // tile,),
        in_specs=[SMEM, ANY]
        + [row(width), row(hidden), row(width), pl.BlockSpec(vec.shape, lambda i: (0, 0))],
        out_specs=[row(width)] * 3 + [pl.BlockSpec((8, width), lambda i: (0, 0))],
        out_shape=[SDS((rows, width), bf16), SDS((rows, width), f32), SDS((rows, width), bf16), SDS((8, width), f32)],
        scratch_shapes=[pltpu.VMEM((width, hidden), bf16),
                        pltpu.SemaphoreType.DMA((4 * down.shape[0],))],
        compiler_params=params(),
        cost_estimate=cost(8e9, 20e6),
        name="second_norm",
    )(scales, down, n1, act, d_out, vec)


def mid_bwd_kernel(place_ref, scale_ref, down_ref, *refs, chunk, count, deps):
    pieces = refs[:count]
    (n1_ref, r1_ref, gp_ref, dz_ref, dzb_ref, vec_ref, du_ref, dh_ref, dhb_ref, dc_ref, vg_ref, b1g_ref,
     wo_ref, w1_ref, w2_ref, out_sems, up_sems, down_sems) = refs[count + deps :]
    first = pl.program_id(0) == 0

    @pl.when(first)
    def _():
        copies = down_copies(down_ref, w2_ref, down_sems)
        start_all(copies)
        start_all(block_copies(place_ref, pieces, range(4), w1_ref, up_sems))
        start_all(block_copies(place_ref, pieces, [4], wo_ref, out_sems))
        vg_ref[...] = jnp.zeros_like(vg_ref)
        b1g_ref[...] = jnp.zeros_like(b1g_ref)
        wait_all(copies)

    g1 = vec_ref[3:4]
    n1 = n1_ref[...]
    dz_low = dzb_ref[...]
    for start in range(0, w1_ref.shape[1], chunk):
        cols = slice(start, start + chunk)
        du = dot(dz_low, w2_ref[:, cols]) * scale_ref[5] * gp_ref[:, cols].astype(f32)
        b1g_ref[0:1, cols] += col_sum(du)
        du_ref[:, cols] = du.astype(bf16)

    @pl.when(first)
    def _():
        wait_all(block_copies(place_ref, pieces, range(4), w1_ref, up_sems))
        wait_all(block_copies(place_ref, pieces, [4], wo_ref, out_sems))

    dy = dz_ref[...] + dot_last(du_ref[...], w1_ref[...]) * scale_ref[4]
    vg_ref[3:4] += col_sum(dy * n1)
    vg_ref[4:5] += col_sum(dy)
    dh = normalize_back(dy * g1, n1, r1_ref[:, 0:1])
    vg_ref[2:3] += col_sum(dh)
    dh_ref[...] = dh
    dh_low = dh.astype(bf16)
    dhb_ref[...] = dh_low
    dc_ref[...] = (dot_last(dh_low, wo_ref[...]) * scale_ref[3]).astype(bf16)


def mid_bwd(place, scales, pieces, down, n1, r1, gelu_grad, dz, dz_low, vec, deps):
    rows, width = n1.shape
    hidden = gelu_grad.shape[1]
    tile = 256
    count = len(pieces)

    def row(size):
        return pl.BlockSpec((tile, size), lambda i: (i, 0))

    return pl.pallas_call(
        functools.partial(mid_bwd_kernel, chunk=256, count=count, deps=len(deps)),
        grid=(rows // tile,),
        in_specs=[SMEM] * 2 + [ANY] * (count + 1 + len(deps))
        + [row(width), row(128), row(hidden), row(width), row(width), pl.BlockSpec(vec.shape, lambda i: (0, 0))],
        out_specs=[row(hidden), row(width), row(width), row(width),
                   pl.BlockSpec((8, width), lambda i: (0, 0)), pl.BlockSpec((8, hidden), lambda i: (0, 0))],
        out_shape=[SDS((rows, hidden), bf16), SDS((rows, width), f32), SDS((rows, width), bf16),
                   SDS((rows, width), bf16), SDS((8, width), f32), SDS((8, hidden), f32)],
        scratch_shapes=[pltpu.VMEM((width, width), bf16), pltpu.VMEM((width, hidden), bf16),
                        pltpu.VMEM((width, hidden), bf16), pltpu.SemaphoreType.DMA((count,)),
                        pltpu.SemaphoreType.DMA((4 * count,)),
                        pltpu.SemaphoreType.DMA((4 * down.shape[0],))],
        compiler_params=params(),
        cost_estimate=cost(20e9, 40e6),
        name="middle_backward",
    )(place, scales, down, *pieces, *deps, n1, r1, gelu_grad, dz, dz_low, vec)


def up_grad_kernel(place_ref, left_ref, right_ref, *refs, cores, deps):
    outs, left_t = refs[deps : deps + cores], refs[deps + cores]

    @pl.when(pl.program_id(0) == 0)
    def _():
        order_rows(place_ref, left_ref[...].T, left_t)

    for core in reversed(range(cores)):
        outs[core][...] = dot(left_t[core], right_ref[...]).astype(bf16).reshape(outs[core].shape)


def up_grad(place, left, right, cores, spots, deps):
    rows, width = left.shape
    size = right.shape[1] // 4
    block = (spots, 1, width // (cores * spots), size)
    return pl.pallas_call(
        functools.partial(up_grad_kernel, cores=cores, deps=len(deps)),
        grid_spec=pltpu.PrefetchScalarGridSpec(
            num_scalar_prefetch=1,
            grid=(4,),
            in_specs=[pl.BlockSpec((rows, width), lambda i, place: (0, 0)),
                      pl.BlockSpec((rows, size), lambda i, place: (0, i))] + [ANY] * len(deps),
            out_specs=[pl.BlockSpec(block, lambda i, place: (0, i, 0, 0))] * cores,
            scratch_shapes=[pltpu.VMEM((cores, width // cores, rows), bf16)],
        ),
        out_shape=[SDS((spots, 4) + block[2:], bf16)] * cores,
        compiler_params=params(),
        cost_estimate=cost(8e9, 14e6),
        name="up_gradient",
    )(place, left, right, *deps)


def down_grad_kernel(left_ref, right_ref, out_ref, left_t):
    @pl.when(pl.program_id(0) == 0)
    def _():
        left_t[...] = left_ref[...].T

    value = dot(left_t[...], right_ref[...]).astype(bf16)
    blocks, slots, size, cols = out_ref.shape
    for block in range(blocks):
        out_ref[block] = value[:, block * cols : (block + 1) * cols].reshape(slots, size, cols)


def down_grad(left, right, blocks):
    rows, width = left.shape
    size = right.shape[1] // blocks
    step = min(2, blocks)
    block = (step, 4, width // 4, size)
    return pl.pallas_call(
        down_grad_kernel,
        grid=(blocks // step,),
        in_specs=[pl.BlockSpec((rows, width), lambda i: (0, 0)),
                  pl.BlockSpec((rows, step * size), lambda i: (0, i))],
        out_specs=pl.BlockSpec(block, lambda i: (i, 0, 0, 0)),
        out_shape=SDS((blocks,) + block[1:], bf16),
        scratch_shapes=[pltpu.VMEM((width, rows), bf16)],
        compiler_params=params(),
        cost_estimate=cost(8e9, 14e6),
        name="down_gradient",
    )(left, right)


def input_grad_kernel(place_ref, scale_ref, *refs, count, chunks, deps):
    pieces = refs[:count]
    parts = refs[count : count + chunks]
    dh_ref, out_ref, w_ref, sems = refs[count + chunks + deps :]
    width = dh_ref.shape[1]

    @pl.when(pl.program_id(0) == 0)
    def _():
        copies = block_copies(place_ref, pieces, range(3), w_ref, sems)
        start_all(copies)
        wait_all(copies)

    total = dh_ref[...]
    for plane in range(3):
        product = None
        start = plane * width
        for part in parts:
            size = part.shape[1] // 3
            more = dot_last(part[:, plane * size : (plane + 1) * size], w_ref[:, start : start + size])
            product = more if product is None else product + more
            start += size
        total = total + product * scale_ref[plane]
    out_ref[...] = total.astype(bf16)


def input_grad(place, scales, pieces, parts, dh, deps):
    rows, width = dh.shape
    tile = 512
    count, chunks = len(pieces), len(parts)

    def row(size):
        return pl.BlockSpec((tile, size), lambda i: (i, 0))

    return pl.pallas_call(
        functools.partial(input_grad_kernel, count=count, chunks=chunks, deps=len(deps)),
        grid=(rows // tile,),
        in_specs=[SMEM] * 2 + [ANY] * count + [row(p.shape[1]) for p in parts] + [ANY] * len(deps) + [row(width)],
        out_specs=row(width),
        out_shape=SDS((rows, width), bf16),
        scratch_shapes=[pltpu.VMEM((width, 3 * width), bf16), pltpu.SemaphoreType.DMA((3 * count,))],
        compiler_params=params(),
        cost_estimate=cost(9e9, 2 * (rows * width * 6 + 3 * width * width)),
        name="input_gradient",
    )(place, scales, *pieces, *parts, *deps, dh)


def swap(value, axis, mask):
    count = lax.axis_size(axis)
    return lax.ppermute(value, axis, [(i, i ^ mask) for i in range(count)])


def bits(axis):
    return [1 << b for b in range(lax.axis_size(axis).bit_length() - 1)]


def doubling_gather(value, axis, dim):
    index = lax.axis_index(axis)
    for bit in bits(axis):
        other = swap(value, axis, bit)
        high = (index & bit) != 0
        value = jnp.concatenate(
            [jnp.where(high, other, value), jnp.where(high, value, other)], axis=dim
        )
    return value


def doubling_sum(value):
    for axis in ("dp", "shard"):
        for bit in bits(axis):
            value = value + swap(value, axis, bit)
    return value


def total_sum(value):
    value = value + swap(value, "dp", 1)
    for axis, masks in (("dp", (6, 4, 2)), ("shard", (3, 2, 1))):
        others = [swap(value, axis, mask) for mask in masks]
        value = (value + others[0]) + (others[1] + others[2])
    return value


def four(block, axis, unit):
    return [block] + [swap(block, axis, unit * m) for m in (1, 2, 3)]


def core_sum_kernel(*refs, sizes, deps):
    count = len(sizes)
    outs = refs[2 * count + deps :]
    at = 0
    for index, (depth, width) in enumerate(sizes):
        mine, got = refs[2 * index : 2 * index + 2]
        for spot, out in enumerate(outs):
            total = mine[spot, 0].astype(f32) + got[spot, 0].astype(f32)
            out[0, :depth, at : at + width] = total.astype(bf16)
            if depth < out.shape[1]:
                out[0, depth:, at : at + width] = jnp.zeros((out.shape[1] - depth, width), bf16)
        at += width


def core_sum(pairs, deps=()):
    spots, slots = pairs[0][0].shape[:2]
    sizes = [mine.shape[2:] for mine, _ in pairs]
    rows, width = max(s[0] for s in sizes), sum(s[1] for s in sizes)
    specs = []
    for mine, got in pairs:
        specs += [pl.BlockSpec((spots, 1) + mine.shape[2:], lambda i: (0, i, 0, 0))] * 2
    return pl.pallas_call(
        functools.partial(core_sum_kernel, sizes=sizes, deps=len(deps)),
        grid=(slots,),
        in_specs=specs + [ANY] * len(deps),
        out_specs=[pl.BlockSpec((1, rows, width), lambda i: (i, 0, 0))] * spots,
        out_shape=[SDS((slots, rows, width), bf16)] * spots,
        compiler_params=params(),
        cost_estimate=cost(1e6, 6 * spots * slots * rows * width),
        name="core_sum",
    )(*[part for pair in pairs for part in pair], *deps)


def plane_sum_kernel(*refs, count, deps):
    outs = refs[4 * count + deps :]
    at = 0
    for index in range(count):
        parts = refs[4 * index : 4 * index + 4]
        depth, width = parts[0].shape[1:]
        for slot in range(parts[0].shape[0]):
            total = parts[0][slot].astype(f32) + parts[1][slot].astype(f32)
            total = total + (parts[2][slot].astype(f32) + parts[3][slot].astype(f32))
            out = outs[0].at[slot] if len(outs) == 1 else outs[slot]
            out[:depth, at : at + width] = total.astype(out.dtype)
            if depth < out.shape[0]:
                out[depth:, at : at + width] = jnp.zeros((out.shape[0] - depth, width), out.dtype)
        at += width


def plane_sum(groups, split, deps=()):
    slots = groups[0][0].shape[0]
    rows = max(parts[0].shape[1] for parts in groups)
    width = sum(parts[0].shape[2] for parts in groups)
    vmem = pl.BlockSpec(memory_space=pltpu.VMEM)
    shapes = [SDS((rows, width), f32)] + [SDS((rows, width), bf16)] * (slots - 1)
    if not split:
        shapes = [SDS((slots, rows, width), bf16)]
    return pl.pallas_call(
        functools.partial(plane_sum_kernel, count=len(groups), deps=len(deps)),
        in_specs=[vmem] * (4 * len(groups)) + [ANY] * len(deps),
        out_specs=[vmem] * len(shapes),
        out_shape=shapes,
        compiler_params=params(),
        cost_estimate=cost(1e6, 4 * slots * rows * width),
        name="plane_sum",
    )(*[part for parts in groups for part in parts], *deps)


def to_plane(parts):
    return [parts[0]] + [swap(parts[spot], "dp", 2 * spot) for spot in (1, 2, 3)]


def to_shards(slots):
    total = slots[0]
    for slot in (1, 2, 3):
        total = total + swap(slots[slot], "shard", slot).astype(f32)
    return total


def after(value, *others):
    return lax.optimization_barrier((value,) + others)[0]

def adam_update(gradient, master, first_old, second_old, average, step_rate, decay_rate):
    first_new = beta_first * first_old + (1.0 - beta_first) * gradient
    second_new = beta_second * second_old + (1.0 - beta_second) * gradient * gradient
    first_hat = first_new / (1.0 - beta_first**STEP)
    second_hat = second_new / (1.0 - beta_second**STEP)
    master_new = master - step_rate * (
        first_hat / (jnp.sqrt(second_hat) + adam_eps) + decay_rate * master
    )
    average_new = average_keep * average + (1.0 - average_keep) * master_new
    return (first_new, second_new, master_new, average_new)


def on_device(
    tokens, out_grad, first_lengths, quant_scales, attn_quant, up_quant, down_quant,
    attn_master, attn_first, attn_second, attn_average,
    up_master, up_first, up_second, up_average,
    down_master, down_first, down_second, down_average,
    vector_master, vector_first, vector_second, vector_average,
):
    width = tokens.shape[1]
    dp_index, shard_index = lax.axis_index("dp"), lax.axis_index("shard")
    small = lax.axis_size("dp") == 8 and lax.axis_size("shard") == 4 and attn_quant.shape == (96, 768)
    gather = functools.partial(lax.all_gather, tiled=True)
    scatter = functools.partial(lax.psum_scatter, tiled=True)
    down_turned = down_quant.T
    vector_low = vector_master.astype(bf16)
    if small:
        cores, spots = 2, 4
        place = jnp.stack([dp_index & 1, dp_index >> 1, shard_index]).astype(jnp.int32)
        packed = jnp.pad(vector_low.T, ((0, 13), (0, width - 96)))
        blocks = four(jnp.concatenate([attn_quant, packed]), "shard", 1)
        qkv, w_out = attn_stack(place, blocks)
        pieces = four(qkv, "dp", 2)
        up_blocks = four(after(up_quant, qkv), "shard", 1)
        down = lax.all_gather(after(down_turned, *pieces[1:], *up_blocks), ("dp", "shard")).reshape(8, 4, 192, -1)
        up = stack(place, up_blocks, 2, w_out, deps=pieces[1:])
        ups = four(up, "dp", 2)
        pieces = pieces + [swap(after(piece, *up_blocks), "dp", 1) for piece in pieces]
        early = [up]
    else:
        cores, spots = 1, 1
        place = jnp.zeros((3,), jnp.int32)
        vec_w = doubling_gather(doubling_gather(vector_low, "shard", 1), "dp", 0)
        attn_w = gather(gather(attn_quant, "shard", axis=1), "dp", axis=0)
        up_w = gather(gather(up_quant, "shard", axis=1), "dp", axis=0)
        down_w = gather(gather(down_turned, "shard", axis=0), "dp", axis=1)
        planes = [attn_w[:, i * width : (i + 1) * width] for i in range(4)]
        pieces = [jnp.concatenate(planes[:3] + [jnp.pad(vec_w.T, ((0, 4), (0, 0)))])]
        ups = [jnp.concatenate([up_w[:, i * width : (i + 1) * width] for i in range(4)] + planes[3:])]
        down = down_w.reshape(1, 4, width // 4, -1)
        early = []

    q, k, v, c, lse, vec = attn_fwd(place, first_lengths, quant_scales, pieces, tokens, early)
    if small:
        ups = [ups[0]] + [after(piece, c) for piece in ups[1:]]
        ups = ups + [swap(piece, "dp", 1) for piece in ups]
    n1, r1, y1, act, gelu_grad = mid_fwd(place, quant_scales, ups, tokens, c, vec)
    layer_out, dz, dz_low, vec_second = second_norm(quant_scales, down, n1, act, out_grad, vec)
    grad_down = down_grad(dz_low, act, cores * spots)
    du, dh, dh_low, dc, vec_first, b1_grad = mid_bwd(
        place, quant_scales, ups, down, n1, r1, gelu_grad, dz, dz_low, vec, [grad_down]
    )
    vec_grad = jnp.concatenate([vec_first[:5], vec_second[5:]])
    attn = functools.partial(
        attn_bwd, place, first_lengths, q, k, v, dc, c, lse, tokens, dh_low, cores=cores, spots=spots
    )
    if small:
        own_down = lax.psum_scatter(grad_down, "dp", scatter_dimension=0)
        up_parts = up_grad(place, y1, du, cores, spots, [])
        up_got = swap(up_parts[1], "dp", 1)
        *parts_a, d_a, sums_a = attn(first=0, pairs=2, deps=up_parts[1:])
        up_plane = core_sum([(up_parts[0], up_got)], [d_a])
        got_a = swap(after(parts_a[1], up_plane), "dp", 1)
        up_plane = to_plane(up_plane)
        *parts_b, d_b, sums_b = attn(first=2, pairs=2, deps=[up_plane[0]])
        got_b = swap(parts_b[1], "dp", 1)
        own_down = lax.psum_scatter(own_down, "shard", scatter_dimension=0).astype(f32)
        *parts_c, d_c, sums = attn(first=4, pairs=2, deps=[d_b], before=(sums_a, sums_b, vec_grad, b1_grad))
        plane_a = core_sum([(parts_a[0], got_a), (parts_b[0], got_b)], [d_c])
        got_c = swap(parts_c[1], "dp", 1)
        plane_a = to_plane(plane_a)
        (up_shards,) = plane_sum([up_plane], False, [plane_a[0]])
        own_up = lax.psum_scatter(up_shards, "shard", scatter_dimension=0).astype(f32)
        plane_c = to_plane(core_sum([(parts_c[0], got_c)], [plane_a[0]]))
        input_gradient = input_grad(place, quant_scales, pieces, [d_a, d_b, d_c], dh, [up_shards, plane_c[0]])
        own_all = to_shards(plane_sum([plane_a, plane_c], True, [input_gradient]))
    else:
        up_parts = up_grad(place, y1, du, cores, spots, [])
        parts_a, d_a, sums_a = attn(first=0, pairs=2, deps=[])
        parts_b, d_b, sums_b = attn(first=2, pairs=2, deps=[])
        parts_c, d_c, sums = attn(first=4, pairs=2, deps=[], before=(sums_a, sums_b, vec_grad, b1_grad))
        attn_parts = [[parts_a], [parts_b], [parts_c]]
        input_gradient = input_grad(place, quant_scales, pieces, [d_a, d_b, d_c], dh, [])

    rows_own, cols_own = vector_master.shape
    if small:
        own_attn = own_all[:rows_own]
        own_vector = own_all[rows_own : rows_own + cols_own, width - 256 : width - 256 + rows_own].T
        total = total_sum
    else:
        vec_total = doubling_sum(sums[:12])
        own_vector = lax.dynamic_slice(vec_total, (shard_index * cols_own, dp_index * rows_own), (cols_own, rows_own)).T
        grad_down = grad_down.reshape(width, -1)
        grad_up = up_parts[0][0].transpose(1, 0, 2).reshape(width, -1)
        grad_attn = jnp.concatenate([parts[0][0] for parts in attn_parts], axis=2)
        grad_attn = grad_attn.transpose(1, 0, 2).reshape(width, -1)
        own_down = scatter(scatter(grad_down, "dp", scatter_dimension=1), "shard", scatter_dimension=0).astype(f32)
        own_up = scatter(scatter(grad_up, "dp", scatter_dimension=0), "shard", scatter_dimension=1).astype(f32)
        own_attn = scatter(scatter(grad_attn, "dp", scatter_dimension=0), "shard", scatter_dimension=1).astype(f32)
        total = doubling_sum
    own_down = own_down.T
    local_squares = (
        jnp.sum(own_attn * own_attn)
        + jnp.sum(own_up * own_up)
        + jnp.sum(own_down * own_down)
        + jnp.sum(own_vector * own_vector)
    )
    grad_norm = jnp.sqrt(total(jnp.broadcast_to(local_squares, (8, 128)))[0, 0])
    factor = jnp.minimum(1.0, clip_limit / (grad_norm + norm_eps))
    attn_new = adam_update(own_attn * factor, attn_master, attn_first, attn_second, attn_average, matrix_rate, matrix_decay)
    up_new = adam_update(own_up * factor, up_master, up_first, up_second, up_average, matrix_rate, matrix_decay)
    down_new = adam_update(own_down * factor, down_master, down_first, down_second, down_average, matrix_rate, matrix_decay)
    vector_new = adam_update(own_vector * factor, vector_master, vector_first, vector_second, vector_average, vector_rate, 0.0)
    return (layer_out, input_gradient, grad_norm, *attn_new, *up_new, *down_new, *vector_new)


def solution(mesh):
    rows = P(("dp", "shard"), None)
    block = P("dp", "shard")
    in_specs = (rows, rows, P(("dp", "shard")), P()) + (block,) * 19
    out_specs = (rows, rows, P()) + (block,) * 16
    return jax.shard_map(
        on_device, mesh=mesh, in_specs=in_specs, out_specs=out_specs, check_vma=False
    )
```

```python
import functools
import math

import jax
import jax.numpy as jnp
from jax import lax
from jax.experimental import pallas as pl
from jax.experimental.pallas import tpu as pltpu
from jax.sharding import PartitionSpec as P

HEAD_DIM = 64
STEP = 10

norm_eps = 1e-06
clip_limit = 1.0
beta_first = 0.9
beta_second = 0.999
adam_eps = 1e-08
matrix_rate = 0.08
vector_rate = 0.5
matrix_decay = 0.01
average_keep = 0.9

VMEM = 58 * 2**20
GELU_K = math.sqrt(2.0 / math.pi)
GELU_C = 0.044715
f32 = jnp.float32
bf16 = jnp.bfloat16
SDS = jax.ShapeDtypeStruct


def dot(left, right):
    return jnp.dot(left, right, preferred_element_type=f32)


def dot_last(left, right):
    return lax.dot_general(left, right, (((1,), (1,)), ((), ())), preferred_element_type=f32)


def col_sum(value):
    return jnp.sum(value, axis=0, keepdims=True)


def params(**extra):
    return pltpu.CompilerParams(vmem_limit_bytes=VMEM, **extra)


def cost(flops, moved, trans=0):
    return pl.CostEstimate(flops=int(flops), bytes_accessed=int(moved), transcendentals=int(trans))


SMEM = pl.BlockSpec(memory_space=pltpu.SMEM)
ANY = pl.BlockSpec(memory_space=pl.ANY)


def piece_row(place_ref, index, count):
    if count == 1:
        return 0
    half = count // 2
    return ((place_ref[1] ^ (index % half)) * 2) + (place_ref[0] ^ (index // half))


def block_copies(place_ref, pieces, blocks, dest, sems):
    count = len(pieces)
    rows, width = dest.shape[0] // count, pieces[0].shape[1]
    copies = []
    for at, block in enumerate(blocks):
        for index, piece in enumerate(pieces):
            row = pl.multiple_of(piece_row(place_ref, index, count) * rows, 16)
            copies.append(
                pltpu.make_async_copy(
                    piece.at[block * rows : (block + 1) * rows],
                    dest.at[pl.ds(row, rows), at * width : (at + 1) * width],
                    sems.at[len(copies)],
                )
            )
    return copies


def down_copies(place_ref, sources, dest, sems):
    copies = []
    for core, source in enumerate(sources):
        slots, spots, rows, width = source.shape
        for slot in range(slots):
            for spot in range(spots):
                col = (spot * len(sources) + (place_ref[0] ^ core)) * width
                copies.append(
                    pltpu.make_async_copy(
                        source.at[slot, spot],
                        dest.at[slot * rows : (slot + 1) * rows, pl.ds(pl.multiple_of(col, 128), width)],
                        sems.at[len(copies)],
                    )
                )
    return copies


def start_all(copies):
    for copy in copies:
        copy.start()


def wait_all(copies):
    for copy in copies:
        copy.wait()


def normalize(value):
    centre = value - jnp.mean(value, axis=-1, keepdims=True)
    inv_std = lax.rsqrt(jnp.mean(centre * centre, axis=-1, keepdims=True) + norm_eps)
    return centre * inv_std, inv_std


def normalize_back(scaled, normed, inv_std):
    return inv_std * (
        scaled
        - jnp.mean(scaled, axis=-1, keepdims=True)
        - normed * jnp.mean(scaled * normed, axis=-1, keepdims=True)
    )


def attn_stack_kernel(place_ref, *refs):
    blocks, qkv_ref, out_ref = refs[:4], refs[4], refs[5]
    rows = out_ref.shape[0]
    vectors = None
    for slot, block in enumerate(blocks):
        plane = slot ^ place_ref[2]
        more = pltpu.roll(block[rows:, :].astype(f32), 3 * plane, 0)
        vectors = more if vectors is None else vectors + more

        @pl.when(plane < 3)
        def _():
            qkv_ref[pl.ds(pl.multiple_of(plane * rows, 16), rows), :] = block[:rows, :]

        @pl.when(plane == 3)
        def _():
            out_ref[...] = block[:rows, :]

    qkv_ref[3 * rows :, :] = vectors.astype(bf16)


def attn_stack(place, blocks):
    rows, width = blocks[0].shape
    rows -= 16
    return pl.pallas_call(
        attn_stack_kernel,
        in_specs=[SMEM] + [pl.BlockSpec(memory_space=pltpu.VMEM)] * 4,
        out_specs=[pl.BlockSpec(memory_space=pltpu.VMEM)] * 2,
        out_shape=[SDS((3 * rows + 16, width), bf16), SDS((rows, width), bf16)],
        compiler_params=params(),
        cost_estimate=cost(1e6, 1e6),
        name="attention_weight_order",
    )(place, *blocks)


def stack_kernel(place_ref, *refs, which, extra):
    blocks, out_ref = refs[:4], refs[-1]
    rows = blocks[0].shape[0]
    for slot, block in enumerate(blocks):
        at = pl.multiple_of((slot ^ place_ref[which]) * rows, 16)
        out_ref[pl.ds(at, rows), :] = block[...]
    if extra:
        out_ref[4 * rows :, :] = refs[4][...]


def stack(place, blocks, which, *extra, deps=()):
    rows, width = blocks[0].shape
    return pl.pallas_call(
        functools.partial(stack_kernel, which=which, extra=len(extra)),
        in_specs=[SMEM] + [pl.BlockSpec(memory_space=pltpu.VMEM)] * (4 + len(extra)) + [ANY] * len(deps),
        out_specs=pl.BlockSpec(memory_space=pltpu.VMEM),
        out_shape=SDS((rows * (4 + len(extra)), width), bf16),
        compiler_params=params(),
        cost_estimate=cost(1e6, 1e6),
        name="weight_order",
    )(place, *blocks, *extra, *deps)


def attn_fwd_kernel(place_ref, len_ref, scale_ref, *refs, block, count, deps):
    pieces = refs[:count]
    refs = refs[:count] + refs[count + deps :]
    x_ref, q_ref, k_ref, v_ref, c_ref, lse_ref, vec_ref, w_ref, packed, sems, vec_sems = refs[count:]
    rows, width = q_ref.shape
    total_width = x_ref.shape[1]
    group = pl.program_id(0)

    @pl.when(group == 0)
    def _():
        copies = block_copies(place_ref, pieces, range(3), w_ref, sems)
        top = pieces[0].shape[0] - 16
        for index, piece in enumerate(pieces):
            copies.append(pltpu.make_async_copy(piece.at[top : top + 16], packed.at[index], vec_sems.at[index]))
        start_all(copies)
        wait_all(copies)
        vectors = None
        for index in range(count):
            shift = piece_row(place_ref, index, count) * (total_width // count)
            more = packed[index].astype(f32)
            more = more if count == 1 else pltpu.roll(more, shift, 1)
            vectors = more if vectors is None else vectors + more
        vec_ref[...] = vectors

    x = x_ref[...]

    def part(index):
        return w_ref[:, pl.ds(pl.multiple_of(index * total_width + group * width, 128), width)]

    cols = pl.ds(pl.multiple_of(group * width, 128), width)
    q_ref[...] = (dot(x, part(0)) * scale_ref[0] + vec_ref[0:1, cols]).astype(bf16)
    k_ref[...] = (dot(x, part(1)) * scale_ref[1]).astype(bf16)
    v_ref[...] = (dot(x, part(2)) * scale_ref[2] + vec_ref[1:2, cols]).astype(bf16)
    lane = lax.broadcasted_iota(jnp.int32, (1, 128), 1)

    def run(span):
        step = min(block, span)
        for pair in range(width // 128):
            cols = pl.ds(pair * 128, 128)
            for start in range(0, rows, step):
                low = start // span * span
                q_rows = q_ref[start : start + step, cols]
                k_rows = k_ref[low : low + span, cols]
                v_rows = v_ref[low : low + span, cols]
                found = []
                for head in range(2):
                    own = (lane < 64) if head == 0 else (lane >= 64)
                    q_own = jnp.where(own, q_rows, jnp.zeros_like(q_rows)) * jnp.asarray(0.125, bf16)
                    v_ones = jnp.where(own, v_rows, jnp.ones_like(v_rows))
                    scores = dot_last(q_own, k_rows)
                    top = jnp.max(scores, axis=1, keepdims=True)
                    found.append((dot(jnp.exp(scores - top).astype(bf16), v_ones), top))
                (out_a, top_a), (out_b, top_b) = found
                value = jnp.where(lane < 64, out_a, out_b)
                total = jnp.where(lane < 64, pltpu.roll(out_a, 64, 1), pltpu.roll(out_b, 64, 1))
                c_ref[start : start + step, cols] = (value / total).astype(bf16)
                lse_ref[start : start + step, cols] = jnp.where(lane < 64, top_a, top_b) + jnp.log(total)

    two = len_ref[0] < rows

    @pl.when(two)
    def _():
        run(rows // 2)

    @pl.when(jnp.logical_not(two))
    def _():
        run(rows)


def attn_fwd(place, lengths, scales, pieces, x, deps):
    rows, width = x.shape
    group = 256
    count = len(pieces)
    cols = pl.BlockSpec((rows, group), lambda g: (0, g))
    return pl.pallas_call(
        functools.partial(attn_fwd_kernel, block=512, count=count, deps=len(deps)),
        grid=(width // group,),
        in_specs=[SMEM] * 3 + [ANY] * (count + len(deps)) + [pl.BlockSpec((rows, width), lambda g: (0, 0))],
        out_specs=[cols] * 5 + [pl.BlockSpec((16, width), lambda g: (0, 0))],
        out_shape=[SDS((rows, width), bf16)] * 4 + [SDS((rows, width), f32), SDS((16, width), f32)],
        scratch_shapes=[pltpu.VMEM((width, 3 * width), bf16), pltpu.VMEM((count, 16, width), bf16),
                        pltpu.SemaphoreType.DMA((3 * count,)), pltpu.SemaphoreType.DMA((count,))],
        compiler_params=params(),
        cost_estimate=cost(20e9, 12e6, 12e6),
        name="attention_forward",
    )(place, lengths, scales, *pieces, *deps, x)


def order_rows(place_ref, source_t, dest):
    cores = dest.shape[0]
    if cores == 1:
        dest[0] = source_t
        return
    blocks = 8
    size = source_t.shape[0] // blocks
    for block in range(blocks):
        at = pl.multiple_of(((block // 2) ^ place_ref[1]) * size, 16)
        dest[(block % 2) ^ place_ref[0], pl.ds(at, size), :] = source_t[block * size : (block + 1) * size]


def attn_bwd_kernel(
    place_ref, len_ref, q_ref, k_ref, v_ref, dc_ref, c_ref, lse_ref, x_ref, call_ref, dh_ref, *refs, block, cores, last, shard_first, deps,
):
    refs = refs[deps:]
    if last:
        before_a_ref, before_b_ref, vg_ref, b1g_ref, *refs = refs
    grads = refs[:cores]
    dqkv_ref, sum_ref, dk_acc, dv_acc, dq_acc, x_t, c_t = refs[cores:]
    rows = q_ref.shape[0]
    pair = pl.program_id(0)
    pairs = pl.num_programs(0)
    span_cols = dqkv_ref.shape[1] // 3
    total_width = x_ref.shape[1]
    lane = lax.broadcasted_iota(jnp.int32, (1, 128), 1)
    masks = [lane < 64, lane >= 64]

    @pl.when(pair == 0)
    def _():
        order_rows(place_ref, x_ref[...].T, x_t)
        order_rows(place_ref, call_ref[...].T, c_t)

    prod = (dc_ref[...].astype(f32) * c_ref[...].astype(f32)).T
    row_dots = [col_sum(prod[:64]), col_sum(prod[64:])]
    lse = lse_ref[...].T
    lse_rows = [lse[0:1], lse[64:65]]

    def run(span):
        step = min(block, span)
        for low in range(0, rows, span):
            k_rows = k_ref[low : low + span, :]
            v_rows = v_ref[low : low + span, :]
            k_cols = k_rows.astype(f32).T.astype(bf16)
            for start in range(low, low + span, step):
                q_rows = q_ref[start : start + step, :]
                dc_rows = dc_ref[start : start + step, :]
                probs, d_scores, q_own, dc_own, dq_parts = [], [], [], [], []
                for head in range(2):
                    q_head = jnp.where(masks[head], q_rows, jnp.zeros_like(q_rows)) * jnp.asarray(0.125, bf16)
                    dc_head = jnp.where(masks[head], dc_rows, jnp.zeros_like(dc_rows))
                    prob = jnp.exp(dot_last(k_rows, q_head) - lse_rows[head][:, start : start + step])
                    d_prob = dot_last(v_rows, dc_head)
                    d_score = (prob * (d_prob - row_dots[head][:, start : start + step])).astype(bf16)
                    probs.append(prob.astype(bf16))
                    d_scores.append(d_score)
                    q_own.append(q_head)
                    dc_own.append(dc_head)
                    dq_parts.append(dot(k_cols[head * 64 : head * 64 + 64], d_score))
                dq_acc[:, start : start + step] = jnp.concatenate(dq_parts, axis=0)
                dv = dot(jnp.concatenate(probs, axis=1), jnp.concatenate(dc_own, axis=0))
                dk = dot(jnp.concatenate(d_scores, axis=1), jnp.concatenate(q_own, axis=0))
                if start == low:
                    dv_acc[low : low + span, :] = dv
                    dk_acc[low : low + span, :] = dk
                else:
                    dv_acc[low : low + span, :] += dv
                    dk_acc[low : low + span, :] += dk

    two = len_ref[0] < rows

    @pl.when(two)
    def _():
        run(rows // 2)

    @pl.when(jnp.logical_not(two))
    def _():
        run(rows)

    dq = dq_acc[...].T * 0.125

    def put(part, value):
        at = pl.multiple_of(part * span_cols + pair * 128, 128)
        dqkv_ref[:, pl.ds(at, 128)] = value.astype(bf16)

    put(0, dq)
    put(1, dk_acc[...])
    put(2, dv_acc[...])
    low = total_width - span_cols if last else 0
    here = pl.ds(pl.multiple_of(low + pair * 128, 128), 128)
    if last:
        @pl.when(pair == 0)
        def _():
            sum_ref[0:2, : before_a_ref.shape[1]] = before_a_ref[0:2, :]
            sum_ref[0:2, before_a_ref.shape[1] : low] = before_b_ref[0:2, :]
            sum_ref[2:8, :] = vg_ref[2:8, :]
            for row in range(b1g_ref.shape[1] // total_width):
                sum_ref[8 + row : 9 + row, :] = b1g_ref[0:1, row * total_width : (row + 1) * total_width]

    sum_ref[0:1, here] = col_sum(dq)
    sum_ref[1:2, here] = col_sum(dv_acc[...])

    @pl.when(pair == pairs - 1)
    def _():
        for core in reversed(range(cores)):
            out = grads[core]
            spots = out.shape[1 if shard_first else 0]
            size = x_t.shape[1] // spots
            for plane in range(4):
                left = x_t if plane < 3 else c_t
                right = dqkv_ref[:, plane * span_cols : (plane + 1) * span_cols] if plane < 3 else dh_ref[...]
                value = dot(left[core], right).astype(bf16)
                if shard_first:
                    out[plane] = value.reshape(spots, size, span_cols)
                else:
                    out[:, pl.ds(plane ^ place_ref[2], 1), :size] = value.reshape(spots, 1, size, span_cols)
        if last and cores == 2:
            row = lax.broadcasted_iota(jnp.int32, (16, span_cols), 0)
            col = lax.broadcasted_iota(jnp.int32, (16, span_cols), 1)
            kept = (row < 3) & (col < size)
            even = place_ref[0] == 0
            for plane in range(4):
                rows_here = sum_ref[...] if plane == 0 else pltpu.roll(sum_ref[...], 16 - 3 * plane, 0)
                for spot in range(4):
                    tiles = []
                    for core in range(2):
                        start = (2 * spot + core) * size
                        turned = rows_here if start == 0 else pltpu.roll(rows_here, total_width - start, 1)
                        tiles.append(jnp.where(kept, turned[:, :span_cols], 0.0).astype(bf16))
                    for core in range(2):
                        tile = jnp.where(even, tiles[core], tiles[1 - core])
                        grads[core][spot ^ place_ref[1], plane ^ place_ref[2], size:, :] = tile


def attn_bwd(place, lengths, q, k, v, dc, c, lse, x, dh_low, first, pairs, cores, spots, deps, before=None, shard_first=False):
    rows, width = q.shape
    last = before is not None
    size = pairs * 128
    cols = pl.BlockSpec((rows, 128), lambda g: (0, first + g))
    full = pl.BlockSpec((rows, width), lambda g: (0, 0))

    def whole(shape):
        return pl.BlockSpec(shape, lambda g: (0,) * len(shape))

    depth = width // (cores * spots)
    shape = (spots, 4, depth + (16 if last and cores == 2 else 0), size)
    shape = (shape[1], shape[0]) + shape[2:] if shard_first else shape
    sums = (16, width if last else size)
    more = list(before) if last else []
    return pl.pallas_call(
        functools.partial(attn_bwd_kernel, block=512, cores=cores, last=last, shard_first=shard_first, deps=len(deps)),
        grid=(pairs,),
        in_specs=[SMEM] * 2 + [cols] * 6 + [full] * 2
        + [pl.BlockSpec((rows, size), lambda g: (0, first // pairs))] + [ANY] * len(deps) + [whole(m.shape) for m in more],
        out_specs=[whole(shape)] * cores + [whole((rows, 3 * size)), whole(sums)],
        out_shape=[SDS(shape, bf16)] * cores + [SDS((rows, 3 * size), bf16), SDS(sums, f32)],
        scratch_shapes=[
            pltpu.VMEM((rows, 128), f32), pltpu.VMEM((rows, 128), f32), pltpu.VMEM((128, rows), f32),
            pltpu.VMEM((cores, width // cores, rows), bf16), pltpu.VMEM((cores, width // cores, rows), bf16),
        ],
        compiler_params=params(),
        cost_estimate=cost(50e9 * size / width, 30e6 * size / width, 12e6 * size / width),
        name="attention_backward",
    )(place, lengths, q, k, v, dc, c, lse, x, c, dh_low, *deps, *more)


def mid_fwd_kernel(place_ref, scale_ref, *refs, chunk, count):
    pieces = refs[:count]
    (x_ref, c_ref, vec_ref, n1_ref, r1_ref, y1_ref, a_ref, gp_ref,
     wo_ref, w1_ref, out_sems, up_sems) = refs[count:]
    rows = x_ref.shape[0]
    first = pl.program_id(0) == 0

    @pl.when(first)
    def _():
        copies = block_copies(place_ref, pieces, [4], wo_ref, out_sems)
        start_all(copies)
        start_all(block_copies(place_ref, pieces, range(4), w1_ref, up_sems))
        wait_all(copies)

    residual = x_ref[...].astype(f32) + dot(c_ref[...], wo_ref[...]) * scale_ref[3] + vec_ref[2:3]
    normed, inv_std = normalize(residual)
    n1_ref[...] = normed
    r1_ref[...] = jnp.broadcast_to(inv_std, (rows, 128))
    y1 = (normed * vec_ref[3:4] + vec_ref[4:5]).astype(bf16)
    y1_ref[...] = y1

    @pl.when(first)
    def _():
        wait_all(block_copies(place_ref, pieces, range(4), w1_ref, up_sems))

    for start in range(0, w1_ref.shape[1], chunk):
        cols = slice(start, start + chunk)
        block, at = divmod(start, x_ref.shape[1])
        bias = vec_ref[8 + block : 9 + block, at : at + chunk]
        u = dot(y1, w1_ref[:, cols]) * scale_ref[4] + bias
        square = u * u
        half = 0.5 + 0.5 * jnp.tanh(u * (GELU_K + (GELU_K * GELU_C) * square))
        act = u * half
        a_ref[:, cols] = act.astype(bf16)
        gp_ref[:, cols] = (half + act * (1.0 - half) * (2 * GELU_K + (6 * GELU_K * GELU_C) * square)).astype(bf16)


def mid_fwd(place, scales, pieces, x, c, vec):
    rows, width = x.shape
    hidden = 4 * pieces[0].shape[1]
    tile = 512
    count = len(pieces)

    def row(size):
        return pl.BlockSpec((tile, size), lambda i: (i, 0))

    def full(arr):
        return pl.BlockSpec(arr.shape, lambda i: (0, 0))

    return pl.pallas_call(
        functools.partial(mid_fwd_kernel, chunk=256, count=count),
        grid=(rows // tile,),
        in_specs=[SMEM] * 2 + [ANY] * count + [row(width), row(width), full(vec)],
        out_specs=[row(width), row(128), row(width), row(hidden), row(hidden)],
        out_shape=[SDS((rows, width), f32), SDS((rows, 128), f32), SDS((rows, width), bf16),
                   SDS((rows, hidden), bf16), SDS((rows, hidden), bf16)],
        scratch_shapes=[pltpu.VMEM((width, width), bf16), pltpu.VMEM((width, hidden), bf16),
                        pltpu.SemaphoreType.DMA((count,)), pltpu.SemaphoreType.DMA((4 * count,))],
        compiler_params=params(),
        cost_estimate=cost(12e9, 25e6, 3e6),
        name="middle_forward",
    )(place, scales, *pieces, x, c, vec)


def second_norm_kernel(place_ref, scale_ref, *refs, cores):
    downs = refs[:cores]
    n1_ref, a_ref, do_ref, vec_ref, out_ref, dz_ref, dzb_ref, vg_ref, w2_ref, down_sems = refs[cores:]


    @pl.when(pl.program_id(0) == 0)
    def _():
        copies = down_copies(place_ref, downs, w2_ref, down_sems)
        start_all(copies)
        vg_ref[...] = jnp.zeros_like(vg_ref)
        wait_all(copies)

    g1, c1, b2, g2, c2 = [vec_ref[i : i + 1] for i in range(3, 8)]
    residual = n1_ref[...] * g1 + c1 + dot_last(a_ref[...], w2_ref[...]) * scale_ref[5] + b2
    n2, r2 = normalize(residual)
    out_ref[...] = (n2 * g2 + c2).astype(bf16)
    d_out = do_ref[...].astype(f32)
    vg_ref[6:7] += col_sum(d_out * n2)
    vg_ref[7:8] += col_sum(d_out)
    dz = normalize_back(d_out * g2, n2, r2)
    vg_ref[5:6] += col_sum(dz)
    dz_ref[...] = dz
    dzb_ref[...] = dz.astype(bf16)


def second_norm(place, scales, downs, n1, act, d_out, vec):
    rows, width = n1.shape
    hidden = act.shape[1]
    tile = 256

    def row(size):
        return pl.BlockSpec((tile, size), lambda i: (i, 0))

    return pl.pallas_call(
        functools.partial(second_norm_kernel, cores=len(downs)),
        grid=(rows // tile,),
        in_specs=[SMEM] * 2 + [ANY] * len(downs)
        + [row(width), row(hidden), row(width), pl.BlockSpec(vec.shape, lambda i: (0, 0))],
        out_specs=[row(width)] * 3 + [pl.BlockSpec((8, width), lambda i: (0, 0))],
        out_shape=[SDS((rows, width), bf16), SDS((rows, width), f32), SDS((rows, width), bf16), SDS((8, width), f32)],
        scratch_shapes=[pltpu.VMEM((width, hidden), bf16),
                        pltpu.SemaphoreType.DMA((4 * downs[0].shape[1] * len(downs),))],
        compiler_params=params(),
        cost_estimate=cost(8e9, 20e6),
        name="second_norm",
    )(place, scales, *downs, n1, act, d_out, vec)


def mid_bwd_kernel(place_ref, scale_ref, *refs, chunk, count, cores, deps):
    downs, pieces, refs = refs[:cores], refs[cores : cores + count], refs[cores:]
    (n1_ref, r1_ref, gp_ref, dz_ref, dzb_ref, vec_ref, du_ref, dh_ref, dhb_ref, dc_ref, vg_ref, b1g_ref,
     wo_ref, w1_ref, w2_ref, out_sems, up_sems, down_sems) = refs[count + deps :]
    first = pl.program_id(0) == 0

    @pl.when(first)
    def _():
        copies = down_copies(place_ref, downs, w2_ref, down_sems)
        start_all(copies)
        start_all(block_copies(place_ref, pieces, range(4), w1_ref, up_sems))
        start_all(block_copies(place_ref, pieces, [4], wo_ref, out_sems))
        vg_ref[...] = jnp.zeros_like(vg_ref)
        b1g_ref[...] = jnp.zeros_like(b1g_ref)
        wait_all(copies)

    g1 = vec_ref[3:4]
    n1 = n1_ref[...]
    dz_low = dzb_ref[...]
    for start in range(0, w1_ref.shape[1], chunk):
        cols = slice(start, start + chunk)
        du = dot(dz_low, w2_ref[:, cols]) * scale_ref[5] * gp_ref[:, cols].astype(f32)
        b1g_ref[0:1, cols] += col_sum(du)
        du_ref[:, cols] = du.astype(bf16)

    @pl.when(first)
    def _():
        wait_all(block_copies(place_ref, pieces, range(4), w1_ref, up_sems))
        wait_all(block_copies(place_ref, pieces, [4], wo_ref, out_sems))

    dy = dz_ref[...] + dot_last(du_ref[...], w1_ref[...]) * scale_ref[4]
    vg_ref[3:4] += col_sum(dy * n1)
    vg_ref[4:5] += col_sum(dy)
    dh = normalize_back(dy * g1, n1, r1_ref[:, 0:1])
    vg_ref[2:3] += col_sum(dh)
    dh_ref[...] = dh
    dh_low = dh.astype(bf16)
    dhb_ref[...] = dh_low
    dc_ref[...] = (dot_last(dh_low, wo_ref[...]) * scale_ref[3]).astype(bf16)


def mid_bwd(place, scales, pieces, downs, n1, r1, gelu_grad, dz, dz_low, vec, deps):
    rows, width = n1.shape
    hidden = gelu_grad.shape[1]
    tile = 256
    count = len(pieces)

    def row(size):
        return pl.BlockSpec((tile, size), lambda i: (i, 0))

    return pl.pallas_call(
        functools.partial(mid_bwd_kernel, chunk=256, count=count, cores=len(downs), deps=len(deps)),
        grid=(rows // tile,),
        in_specs=[SMEM] * 2 + [ANY] * (count + len(downs) + len(deps))
        + [row(width), row(128), row(hidden), row(width), row(width), pl.BlockSpec(vec.shape, lambda i: (0, 0))],
        out_specs=[row(hidden), row(width), row(width), row(width),
                   pl.BlockSpec((8, width), lambda i: (0, 0)), pl.BlockSpec((8, hidden), lambda i: (0, 0))],
        out_shape=[SDS((rows, hidden), bf16), SDS((rows, width), f32), SDS((rows, width), bf16),
                   SDS((rows, width), bf16), SDS((8, width), f32), SDS((8, hidden), f32)],
        scratch_shapes=[pltpu.VMEM((width, width), bf16), pltpu.VMEM((width, hidden), bf16),
                        pltpu.VMEM((width, hidden), bf16), pltpu.SemaphoreType.DMA((count,)),
                        pltpu.SemaphoreType.DMA((4 * count,)),
                        pltpu.SemaphoreType.DMA((4 * downs[0].shape[1] * len(downs),))],
        compiler_params=params(),
        cost_estimate=cost(20e9, 40e6),
        name="middle_backward",
    )(place, scales, *downs, *pieces, *deps, n1, r1, gelu_grad, dz, dz_low, vec)


def up_grad_kernel(place_ref, left_ref, right_ref, *refs, cores, deps):
    outs, left_t = refs[deps : deps + cores], refs[deps + cores]

    @pl.when(pl.program_id(0) == 0)
    def _():
        order_rows(place_ref, left_ref[...].T, left_t)

    for core in reversed(range(cores)):
        outs[core][...] = dot(left_t[core], right_ref[...]).astype(bf16).reshape(outs[core].shape)


def up_grad(place, left, right, cores, spots, deps):
    rows, width = left.shape
    size = right.shape[1] // 4
    block = (spots, 1, width // (cores * spots), size)
    return pl.pallas_call(
        functools.partial(up_grad_kernel, cores=cores, deps=len(deps)),
        grid_spec=pltpu.PrefetchScalarGridSpec(
            num_scalar_prefetch=1,
            grid=(4,),
            in_specs=[pl.BlockSpec((rows, width), lambda i, place: (0, 0)),
                      pl.BlockSpec((rows, size), lambda i, place: (0, i))] + [ANY] * len(deps),
            out_specs=[pl.BlockSpec(block, lambda i, place: (0, i, 0, 0))] * cores,
            scratch_shapes=[pltpu.VMEM((cores, width // cores, rows), bf16)],
        ),
        out_shape=[SDS((spots, 4) + block[2:], bf16)] * cores,
        compiler_params=params(),
        cost_estimate=cost(8e9, 14e6),
        name="up_gradient",
    )(place, left, right, *deps)


def down_grad_kernel(left_ref, right_ref, out_ref, left_t):
    @pl.when(pl.program_id(0) == 0)
    def _():
        left_t[...] = left_ref[...].T

    value = dot(left_t[...], right_ref[...]).astype(bf16)
    blocks, slots, size, cols = out_ref.shape
    for block in range(blocks):
        out_ref[block] = value[:, block * cols : (block + 1) * cols].reshape(slots, size, cols)


def down_grad(left, right, blocks):
    rows, width = left.shape
    size = right.shape[1] // blocks
    step = min(2, blocks)
    block = (step, 4, width // 4, size)
    return pl.pallas_call(
        down_grad_kernel,
        grid=(blocks // step,),
        in_specs=[pl.BlockSpec((rows, width), lambda i: (0, 0)),
                  pl.BlockSpec((rows, step * size), lambda i: (0, i))],
        out_specs=pl.BlockSpec(block, lambda i: (i, 0, 0, 0)),
        out_shape=SDS((blocks,) + block[1:], bf16),
        scratch_shapes=[pltpu.VMEM((width, rows), bf16)],
        compiler_params=params(),
        cost_estimate=cost(8e9, 14e6),
        name="down_gradient",
    )(left, right)


def input_grad_kernel(place_ref, scale_ref, *refs, count, chunks, deps):
    pieces = refs[:count]
    parts = refs[count : count + chunks]
    dh_ref, out_ref, w_ref, sems = refs[count + chunks + deps :]
    width = dh_ref.shape[1]

    @pl.when(pl.program_id(0) == 0)
    def _():
        copies = block_copies(place_ref, pieces, range(3), w_ref, sems)
        start_all(copies)
        wait_all(copies)

    total = dh_ref[...]
    for plane in range(3):
        product = None
        start = plane * width
        for part in parts:
            size = part.shape[1] // 3
            more = dot_last(part[:, plane * size : (plane + 1) * size], w_ref[:, start : start + size])
            product = more if product is None else product + more
            start += size
        total = total + product * scale_ref[plane]
    out_ref[...] = total.astype(bf16)


def input_grad(place, scales, pieces, parts, dh, deps):
    rows, width = dh.shape
    tile = 512
    count, chunks = len(pieces), len(parts)

    def row(size):
        return pl.BlockSpec((tile, size), lambda i: (i, 0))

    return pl.pallas_call(
        functools.partial(input_grad_kernel, count=count, chunks=chunks, deps=len(deps)),
        grid=(rows // tile,),
        in_specs=[SMEM] * 2 + [ANY] * count + [row(p.shape[1]) for p in parts] + [ANY] * len(deps) + [row(width)],
        out_specs=row(width),
        out_shape=SDS((rows, width), bf16),
        scratch_shapes=[pltpu.VMEM((width, 3 * width), bf16), pltpu.SemaphoreType.DMA((3 * count,))],
        compiler_params=params(),
        cost_estimate=cost(9e9, 2 * (rows * width * 6 + 3 * width * width)),
        name="input_gradient",
    )(place, scales, *pieces, *parts, *deps, dh)


def swap(value, axis, mask):
    count = lax.axis_size(axis)
    return lax.ppermute(value, axis, [(i, i ^ mask) for i in range(count)])


def bits(axis):
    return [1 << b for b in range(lax.axis_size(axis).bit_length() - 1)]


def doubling_gather(value, axis, dim):
    index = lax.axis_index(axis)
    for bit in bits(axis):
        other = swap(value, axis, bit)
        high = (index & bit) != 0
        value = jnp.concatenate(
            [jnp.where(high, other, value), jnp.where(high, value, other)], axis=dim
        )
    return value


def doubling_sum(value):
    for axis in ("dp", "shard"):
        for bit in bits(axis):
            value = value + swap(value, axis, bit)
    return value


def total_sum(value):
    value = value + swap(value, "dp", 1)
    for axis, masks in (("dp", (6, 4, 2)), ("shard", (3, 2, 1))):
        others = [swap(value, axis, mask) for mask in masks]
        value = (value + others[0]) + (others[1] + others[2])
    return value


def four(block, axis, unit):
    return [block] + [swap(block, axis, unit * m) for m in (1, 2, 3)]


def core_sum_kernel(*refs, sizes, deps):
    count = len(sizes)
    outs = refs[2 * count + deps :]
    at = 0
    for index, (depth, width) in enumerate(sizes):
        mine, got = refs[2 * index : 2 * index + 2]
        for spot, out in enumerate(outs):
            total = mine[spot, 0].astype(f32) + got[spot, 0].astype(f32)
            out[0, :depth, at : at + width] = total.astype(bf16)
            if depth < out.shape[1]:
                out[0, depth:, at : at + width] = jnp.zeros((out.shape[1] - depth, width), bf16)
        at += width


def core_sum(pairs, deps=()):
    spots, slots = pairs[0][0].shape[:2]
    sizes = [mine.shape[2:] for mine, _ in pairs]
    rows, width = max(s[0] for s in sizes), sum(s[1] for s in sizes)
    specs = []
    for mine, got in pairs:
        specs += [pl.BlockSpec((spots, 1) + mine.shape[2:], lambda i: (0, i, 0, 0))] * 2
    return pl.pallas_call(
        functools.partial(core_sum_kernel, sizes=sizes, deps=len(deps)),
        grid=(slots,),
        in_specs=specs + [ANY] * len(deps),
        out_specs=[pl.BlockSpec((1, rows, width), lambda i: (i, 0, 0))] * spots,
        out_shape=[SDS((slots, rows, width), bf16)] * spots,
        compiler_params=params(),
        cost_estimate=cost(1e6, 6 * spots * slots * rows * width),
        name="core_sum",
    )(*[part for pair in pairs for part in pair], *deps)


def pair_sum_kernel(mine_ref, got_ref, *refs):
    refs[-1][...] = (mine_ref[...].astype(f32) + got_ref[...].astype(f32)).astype(bf16)


def pair_sum(mine, got, deps=()):
    block = pl.BlockSpec((1,) + mine.shape[1:], lambda i: (i, 0, 0, 0))
    return pl.pallas_call(
        pair_sum_kernel,
        grid=mine.shape[:1],
        in_specs=[block, block] + [ANY] * len(deps),
        out_specs=block,
        out_shape=SDS(mine.shape, bf16),
        compiler_params=params(),
        cost_estimate=cost(1e6, 6 * mine.size),
        name="pair_sum",
    )(mine, got, *deps)


def plane_sum_kernel(*refs, count, deps):
    outs = refs[4 * count + deps :]
    at = 0
    for index in range(count):
        parts = refs[4 * index : 4 * index + 4]
        depth, width = parts[0].shape[1:]
        for slot in range(parts[0].shape[0]):
            total = parts[0][slot].astype(f32) + parts[1][slot].astype(f32)
            total = total + (parts[2][slot].astype(f32) + parts[3][slot].astype(f32))
            out = outs[0].at[slot] if len(outs) == 1 else outs[slot]
            out[:depth, at : at + width] = total.astype(out.dtype)
            if depth < out.shape[0]:
                out[depth:, at : at + width] = jnp.zeros((out.shape[0] - depth, width), out.dtype)
        at += width


def plane_sum(groups, split, deps=()):
    slots = groups[0][0].shape[0]
    rows = max(parts[0].shape[1] for parts in groups)
    width = sum(parts[0].shape[2] for parts in groups)
    vmem = pl.BlockSpec(memory_space=pltpu.VMEM)
    shapes = [SDS((rows, width), f32)] + [SDS((rows, width), bf16)] * (slots - 1)
    if not split:
        shapes = [SDS((slots, rows, width), bf16)]
    return pl.pallas_call(
        functools.partial(plane_sum_kernel, count=len(groups), deps=len(deps)),
        in_specs=[vmem] * (4 * len(groups)) + [ANY] * len(deps),
        out_specs=[vmem] * len(shapes),
        out_shape=shapes,
        compiler_params=params(),
        cost_estimate=cost(1e6, 4 * slots * rows * width),
        name="plane_sum",
    )(*[part for parts in groups for part in parts], *deps)


def exchange(parts, axis, unit):
    return [parts[0]] + [swap(parts[m], axis, unit * m) for m in (1, 2, 3)]


def after(value, *others):
    return lax.optimization_barrier((value,) + others)[0]

def adam_update(gradient, master, first_old, second_old, average, step_rate, decay_rate):
    first_new = beta_first * first_old + (1.0 - beta_first) * gradient
    second_new = beta_second * second_old + (1.0 - beta_second) * gradient * gradient
    first_hat = first_new / (1.0 - beta_first**STEP)
    second_hat = second_new / (1.0 - beta_second**STEP)
    master_new = master - step_rate * (
        first_hat / (jnp.sqrt(second_hat) + adam_eps) + decay_rate * master
    )
    average_new = average_keep * average + (1.0 - average_keep) * master_new
    return (first_new, second_new, master_new, average_new)


def own_sums_kernel(*refs):
    firsts, lasts, (up_ref, down_ref, attn_ref, vec_ref, square_ref) = refs[:4], refs[4:8], refs[8:]
    rows = attn_ref.shape[0]
    first, last = [
        (parts[0][...].astype(f32) + parts[1][...].astype(f32)) + (parts[2][...].astype(f32) + parts[3][...].astype(f32))
        for parts in (firsts, lasts)
    ]
    attn_ref[:, : first.shape[1]] = first
    attn_ref[:, first.shape[1] :] = last[:rows]
    at = 128
    vec_ref[...] = last[rows:, at : at + 128]
    total = jnp.sum(first * first) + jnp.sum(last * last)
    for ref in (up_ref, down_ref):
        value = ref[...].astype(f32)
        total = total + jnp.sum(value * value)
    square_ref[...] = jnp.full(square_ref.shape, total, f32)


def own_sums(firsts, lasts, own_up, own_down):
    vmem = pl.BlockSpec(memory_space=pltpu.VMEM)
    rows, width = firsts[0].shape[0], firsts[0].shape[1] + lasts[0].shape[1]
    return pl.pallas_call(
        own_sums_kernel,
        in_specs=[vmem] * 10,
        out_specs=[vmem] * 3,
        out_shape=[SDS((rows, width), f32), SDS((16, 128), f32), SDS((8, 128), f32)],
        compiler_params=params(),
        cost_estimate=cost(1e6, 2e6),
        name="own_sums",
    )(*firsts, *lasts, own_up, own_down)


def update_kernel(square_ref, attn_ref, up_ref, down_ref, vec_ref, *refs):
    states, news, norm_ref = refs[:16], refs[16:32], refs[32]
    norm = jnp.sqrt(square_ref[...])
    norm_ref[0, 0] = jnp.max(norm)
    factor = jnp.minimum(1.0, clip_limit / (norm + norm_eps))[0:1, 0:1]
    rows, cols = states[12].shape
    grads = (
        attn_ref[...],
        up_ref[...].astype(f32),
        down_ref[...].astype(f32),
        vec_ref[:rows, :cols],
    )
    for index, grad in enumerate(grads):
        rates = (vector_rate, 0.0) if index == 3 else (matrix_rate, matrix_decay)
        old = [ref[...] for ref in states[4 * index : 4 * index + 4]]
        for ref, new in zip(news[4 * index : 4 * index + 4], adam_update(grad * factor, *old, *rates)):
            ref[...] = new


def update(squares, own_attn, own_up, own_down, own_vector, states):
    vmem = pl.BlockSpec(memory_space=pltpu.VMEM)
    states = list(states[:8]) + [state.T for state in states[8:]]
    *news, norm = pl.pallas_call(
        update_kernel,
        in_specs=[vmem] * 21,
        out_specs=[vmem] * 16 + [SMEM],
        out_shape=[SDS(state.shape, f32) for state in states] + [SDS((1, 1), f32)],
        compiler_params=params(),
        cost_estimate=cost(1e7, 8e6),
        name="state_update",
    )(squares, own_attn, own_up, own_down, own_vector, *states)
    return news[:8] + [new.T for new in news[8:]], norm


def on_device(
    tokens, out_grad, first_lengths, quant_scales, attn_quant, up_quant, down_quant,
    attn_master, attn_first, attn_second, attn_average,
    up_master, up_first, up_second, up_average,
    down_master, down_first, down_second, down_average,
    vector_master, vector_first, vector_second, vector_average,
):
    width = tokens.shape[1]
    dp_index, shard_index = lax.axis_index("dp"), lax.axis_index("shard")
    small = lax.axis_size("dp") == 8 and lax.axis_size("shard") == 4 and attn_quant.shape == (96, 768)
    gather = functools.partial(lax.all_gather, tiled=True)
    scatter = functools.partial(lax.psum_scatter, tiled=True)
    down_turned = down_quant.T
    vector_low = vector_master.astype(bf16)
    if small:
        cores, spots = 2, 4
        place = jnp.stack([dp_index & 1, dp_index >> 1, shard_index]).astype(jnp.int32)
        packed = jnp.pad(vector_low.T, ((0, 13), (0, width - 96)))
        blocks = four(jnp.concatenate([attn_quant, packed]), "shard", 1)
        qkv, w_out = attn_stack(place, blocks)
        pieces = four(qkv, "dp", 2)
        up_blocks = four(after(up_quant, qkv), "shard", 1)
        down = after(lax.all_gather(down_turned, "dp"), pieces[1]).reshape(4, 2, 192, -1)
        down = lax.dynamic_index_in_dim(down, dp_index & 1, 1, keepdims=False)
        down = lax.all_gather(after(down, *pieces[1:], *up_blocks), "shard")
        up = stack(place, up_blocks, 2, w_out, deps=pieces[1:2])
        ups = four(up, "dp", 2)
        pieces = pieces + [swap(after(piece, *up_blocks), "dp", 1) for piece in pieces]
        early = [up]
    else:
        cores, spots = 1, 1
        place = jnp.zeros((3,), jnp.int32)
        vec_w = doubling_gather(doubling_gather(vector_low, "shard", 1), "dp", 0)
        attn_w = gather(gather(attn_quant, "shard", axis=1), "dp", axis=0)
        up_w = gather(gather(up_quant, "shard", axis=1), "dp", axis=0)
        down_w = gather(gather(down_turned, "shard", axis=0), "dp", axis=1)
        planes = [attn_w[:, i * width : (i + 1) * width] for i in range(4)]
        pieces = [jnp.concatenate(planes[:3] + [jnp.pad(vec_w.T, ((0, 4), (0, 0)))])]
        ups = [jnp.concatenate([up_w[:, i * width : (i + 1) * width] for i in range(4)] + planes[3:])]
        downs = [down_w.reshape(4, 1, width // 4, -1)]
        early = []

    q, k, v, c, lse, vec = attn_fwd(place, first_lengths, quant_scales, pieces, tokens, early)
    if small:
        ups = [ups[0]] + [after(piece, c) for piece in ups[1:]]
        ups = ups + [swap(piece, "dp", 1) for piece in ups]
    n1, r1, y1, act, gelu_grad = mid_fwd(place, quant_scales, ups, tokens, c, vec)
    if small:
        downs = [down, swap(after(down, act), "dp", 1)]
    layer_out, dz, dz_low, vec_second = second_norm(place, quant_scales, downs, n1, act, out_grad, vec)
    grad_down = down_grad(dz_low, act, cores * spots)
    du, dh, dh_low, dc, vec_first, b1_grad = mid_bwd(
        place, quant_scales, ups, downs, n1, r1, gelu_grad, dz, dz_low, vec, [grad_down]
    )
    vec_grad = jnp.concatenate([vec_first[:5], vec_second[5:]])
    attn = functools.partial(
        attn_bwd, place, first_lengths, q, k, v, dc, c, lse, tokens, dh_low, cores=cores, spots=spots
    )
    if small:
        own_down = lax.psum_scatter(grad_down, "dp", scatter_dimension=0)
        up_parts = up_grad(place, y1, du, cores, spots, [])
        up_got = swap(up_parts[1], "dp", 1)
        *parts_p, d_p, sums_p = attn(first=3, pairs=1, deps=up_parts[1:])
        up_plane = core_sum([(up_parts[0], up_got)], [d_p])
        got_p = swap(after(parts_p[1], up_plane[0]), "dp", 1)
        up_plane = exchange(up_plane, "dp", 2)
        *parts_q, d_q, sums_q = attn(first=0, pairs=3, deps=up_plane[:1], shard_first=True)
        own_down = lax.psum_scatter(own_down, "shard", scatter_dimension=0)
        (up_shards,) = plane_sum([up_plane], False, [d_q, own_down])
        own_up = lax.psum_scatter(up_shards, "shard", scatter_dimension=0)
        got_q = swap(after(parts_q[1], up_shards), "dp", 1)
        *parts_r, d_r, sums = attn(first=4, pairs=2, deps=[up_shards], before=(sums_q, sums_p, vec_grad, b1_grad))
        got_r = swap(parts_r[1], "dp", 1)
        plane_pr = core_sum([(parts_p[0], got_p), (parts_r[0], got_r)], [d_r])
        sum_q = pair_sum(parts_q[0], got_q, [plane_pr[0], own_up])
        plane_pr = exchange(plane_pr, "dp", 2)
        spots_q = lax.psum_scatter(sum_q, "shard", scatter_dimension=0)
        spots_q = exchange(after(spots_q, plane_pr[1]), "dp", 2)
        input_gradient = input_grad(place, quant_scales, pieces, [d_q, d_p, d_r], dh, [plane_pr[0]])
        slots_pr = exchange(plane_sum([plane_pr], True, [input_gradient]), "shard", 1)
    else:
        up_parts = up_grad(place, y1, du, cores, spots, [])
        parts_p, d_p, sums_p = attn(first=3, pairs=1, deps=[])
        parts_q, d_q, sums_q = attn(first=0, pairs=3, deps=[])
        parts_r, d_r, sums = attn(first=4, pairs=2, deps=[], before=(sums_q, sums_p, vec_grad, b1_grad))
        attn_parts = [[parts_q], [parts_p], [parts_r]]
        input_gradient = input_grad(place, quant_scales, pieces, [d_q, d_p, d_r], dh, [])

    rows_own, cols_own = vector_master.shape
    states = (
        attn_master, attn_first, attn_second, attn_average,
        up_master, up_first, up_second, up_average,
        down_master, down_first, down_second, down_average,
        vector_master, vector_first, vector_second, vector_average,
    )
    if small:
        own_attn, own_vector, squares = own_sums(spots_q, slots_pr, own_up, own_down)
        news, grad_norm = update(total_sum(squares), own_attn, own_up, own_down, own_vector, states)
        return (layer_out, input_gradient, grad_norm.reshape(()), *news)
    vec_total = doubling_sum(sums[:12])
    own_vector = lax.dynamic_slice(vec_total, (shard_index * cols_own, dp_index * rows_own), (cols_own, rows_own)).T
    grad_down = grad_down.reshape(width, -1)
    grad_up = up_parts[0][0].transpose(1, 0, 2).reshape(width, -1)
    grad_attn = jnp.concatenate([parts[0][0] for parts in attn_parts], axis=2)
    grad_attn = grad_attn.transpose(1, 0, 2).reshape(width, -1)
    own_down = scatter(scatter(grad_down, "dp", scatter_dimension=1), "shard", scatter_dimension=0).astype(f32).T
    own_up = scatter(scatter(grad_up, "dp", scatter_dimension=0), "shard", scatter_dimension=1).astype(f32)
    own_attn = scatter(scatter(grad_attn, "dp", scatter_dimension=0), "shard", scatter_dimension=1).astype(f32)
    grads = (own_attn, own_up, own_down, own_vector)
    squares = sum(jnp.sum(grad * grad) for grad in grads)
    grad_norm = jnp.sqrt(doubling_sum(jnp.broadcast_to(squares, (8, 128)))[0, 0])
    factor = jnp.minimum(1.0, clip_limit / (grad_norm + norm_eps))
    news = []
    for index, grad in enumerate(grads):
        rates = (vector_rate, 0.0) if index == 3 else (matrix_rate, matrix_decay)
        news += adam_update(grad * factor, *states[4 * index : 4 * index + 4], *rates)
    return (layer_out, input_gradient, grad_norm, *news)


def solution(mesh):
    rows = P(("dp", "shard"), None)
    block = P("dp", "shard")
    in_specs = (rows, rows, P(("dp", "shard")), P()) + (block,) * 19
    out_specs = (rows, rows, P()) + (block,) * 16
    return jax.shard_map(
        on_device, mesh=mesh, in_specs=in_specs, out_specs=out_specs, check_vma=False
    )
```

```python
import functools
import math

import jax
import jax.numpy as jnp
from jax import lax
from jax.experimental import pallas as pl
from jax.experimental.pallas import tpu as pltpu
from jax.sharding import PartitionSpec as P

HEAD_DIM = 64
STEP = 10

norm_eps = 1e-06
clip_limit = 1.0
beta_first = 0.9
beta_second = 0.999
adam_eps = 1e-08
matrix_rate = 0.08
vector_rate = 0.5
matrix_decay = 0.01
average_keep = 0.9

VMEM = 62 * 2**20
GELU_K = math.sqrt(2.0 / math.pi)
GELU_C = 0.044715
f32 = jnp.float32
bf16 = jnp.bfloat16
SDS = jax.ShapeDtypeStruct


def dot(left, right):
    return jnp.dot(left, right, preferred_element_type=f32)


def dot_last(left, right):
    return lax.dot_general(left, right, (((1,), (1,)), ((), ())), preferred_element_type=f32)


def col_sum(value):
    return jnp.sum(value, axis=0, keepdims=True)


def params(**extra):
    return pltpu.CompilerParams(vmem_limit_bytes=VMEM, **extra)


def cost(flops, moved, trans=0):
    return pl.CostEstimate(flops=int(flops), bytes_accessed=int(moved), transcendentals=int(trans))


SMEM = pl.BlockSpec(memory_space=pltpu.SMEM)
ANY = pl.BlockSpec(memory_space=pl.ANY)


def piece_row(place_ref, index, count):
    if count == 1:
        return 0
    half = count // 2
    return ((place_ref[1] ^ (index % half)) * 2) + (place_ref[0] ^ (index // half))


def block_copies(place_ref, pieces, blocks, dest, sems):
    count = len(pieces)
    rows, width = dest.shape[0] // count, pieces[0].shape[1]

    def copy(at, block, index):
        def make():
            row = pl.multiple_of(piece_row(place_ref, index, count) * rows, 16)
            return pltpu.make_async_copy(
                pieces[index].at[block * rows : (block + 1) * rows],
                dest.at[pl.ds(row, rows), at * width : (at + 1) * width],
                sems.at[at * count + index],
            )

        return make

    return [copy(at, block, index) for at, block in enumerate(blocks) for index in range(count)]


def some_copies(copies, part, parts):
    size = len(copies) // parts
    return copies[part * size : (part + 1) * size]


def down_copies(place_ref, sources, dest, sems):
    slots, spots, rows, width = sources[0].shape
    count = len(sources)

    def copy(spot, core, slot):
        def make():
            col = (spot * count + (place_ref[0] ^ core)) * width
            return pltpu.make_async_copy(
                sources[core].at[slot, spot],
                dest.at[slot * rows : (slot + 1) * rows, pl.ds(pl.multiple_of(col, 128), width)],
                sems.at[(spot * count + core) * slots + slot],
            )

        return make

    return [copy(spot, core, slot) for spot in range(spots) for core in range(count) for slot in range(slots)]


def start_all(copies):
    for copy in copies:
        copy().start()


def wait_all(copies):
    for copy in copies:
        copy().wait()


def normalize(value):
    centre = value - jnp.mean(value, axis=-1, keepdims=True)
    inv_std = lax.rsqrt(jnp.mean(centre * centre, axis=-1, keepdims=True) + norm_eps)
    return centre * inv_std, inv_std


def normalize_back(scaled, normed, inv_std):
    return inv_std * (
        scaled
        - jnp.mean(scaled, axis=-1, keepdims=True)
        - normed * jnp.mean(scaled * normed, axis=-1, keepdims=True)
    )


def attn_stack_kernel(place_ref, *refs):
    blocks, qkv_ref, out_ref = refs[:4], refs[-2], refs[-1]
    rows = out_ref.shape[0]
    vectors = None
    for slot, block in enumerate(blocks):
        plane = slot ^ place_ref[2]
        more = pltpu.roll(block[rows:, :].astype(f32), 3 * plane, 0)
        vectors = more if vectors is None else vectors + more

        @pl.when(plane < 3)
        def _():
            qkv_ref[pl.ds(pl.multiple_of(plane * rows, 16), rows), :] = block[:rows, :]

        @pl.when(plane == 3)
        def _():
            out_ref[...] = block[:rows, :]

    qkv_ref[3 * rows :, :] = vectors.astype(bf16)


def attn_stack(place, blocks, deps):
    rows, width = blocks[0].shape
    rows -= 16
    return pl.pallas_call(
        attn_stack_kernel,
        in_specs=[SMEM] + [pl.BlockSpec(memory_space=pltpu.VMEM)] * 4 + [ANY] * len(deps),
        out_specs=[pl.BlockSpec(memory_space=pltpu.VMEM)] * 2,
        out_shape=[SDS((3 * rows + 16, width), bf16), SDS((rows, width), bf16)],
        compiler_params=params(),
        cost_estimate=cost(1e6, 1e6),
        name="attention_weight_order",
    )(place, *blocks, *deps)


def stack_kernel(place_ref, *refs, which, extra):
    blocks, out_ref = refs[:4], refs[-1]
    rows = blocks[0].shape[0]
    for slot, block in enumerate(blocks):
        at = pl.multiple_of((slot ^ place_ref[which]) * rows, 16)
        out_ref[pl.ds(at, rows), :] = block[...]
    if extra:
        out_ref[4 * rows :, :] = refs[4][...]


def stack(place, blocks, which, *extra, deps=()):
    rows, width = blocks[0].shape
    return pl.pallas_call(
        functools.partial(stack_kernel, which=which, extra=len(extra)),
        in_specs=[SMEM] + [pl.BlockSpec(memory_space=pltpu.VMEM)] * (4 + len(extra)) + [ANY] * len(deps),
        out_specs=pl.BlockSpec(memory_space=pltpu.VMEM),
        out_shape=SDS((rows * (4 + len(extra)), width), bf16),
        compiler_params=params(),
        cost_estimate=cost(1e6, 1e6),
        name="weight_order",
    )(place, *blocks, *extra, *deps)


def attn_fwd_kernel(place_ref, len_ref, scale_ref, *refs, block, count, deps):
    pieces = refs[:count]
    refs = refs[:count] + refs[count + deps :]
    x_ref, q_ref, k_ref, v_ref, c_ref, lse_ref, vec_ref, w_ref, packed, sems, vec_sems = refs[count:]
    rows, width = q_ref.shape
    total_width = x_ref.shape[1]
    group = pl.program_id(0)
    weights = block_copies(place_ref, pieces, range(3), w_ref, sems)

    @pl.when(group == 0)
    def _():
        top = pieces[0].shape[0] - 16
        vec_copies = [
            pltpu.make_async_copy(piece.at[top : top + 16], packed.at[index], vec_sems.at[index])
            for index, piece in enumerate(pieces)
        ]
        for copy in vec_copies:
            copy.start()
        start_all(weights)
        for copy in vec_copies:
            copy.wait()
        vectors = None
        for index in range(count):
            shift = piece_row(place_ref, index, count) * (total_width // count)
            more = packed[index].astype(f32)
            more = more if count == 1 else pltpu.roll(more, shift, 1)
            vectors = more if vectors is None else vectors + more
        vec_ref[...] = vectors
        wait_all(weights)

    x = x_ref[...]
    cols = pl.ds(pl.multiple_of(group * width, 128), width)
    for index, out in enumerate((q_ref, k_ref, v_ref)):
        part = w_ref[:, pl.ds(pl.multiple_of(index * total_width + group * width, 128), width)]
        value = dot(x, part) * scale_ref[index]
        if index != 1:
            value = value + vec_ref[index // 2 : index // 2 + 1, cols]
        out[...] = value.astype(bf16)
    lane = lax.broadcasted_iota(jnp.int32, (1, 128), 1)

    def run(span):
        step = min(block, span)
        for pair in range(width // 128):
            cols = pl.ds(pair * 128, 128)
            for start in range(0, rows, step):
                low = start // span * span
                q_rows = q_ref[start : start + step, cols]
                k_rows = k_ref[low : low + span, cols]
                v_rows = v_ref[low : low + span, cols]
                found = []
                for head in range(2):
                    own = (lane < 64) if head == 0 else (lane >= 64)
                    q_own = jnp.where(own, q_rows, jnp.zeros_like(q_rows)) * jnp.asarray(0.125, bf16)
                    v_ones = jnp.where(own, v_rows, jnp.ones_like(v_rows))
                    scores = dot_last(q_own, k_rows)
                    top = jnp.max(scores, axis=1, keepdims=True)
                    found.append((dot(jnp.exp(scores - top).astype(bf16), v_ones), top))
                (out_a, top_a), (out_b, top_b) = found
                value = jnp.where(lane < 64, out_a, out_b)
                total = jnp.where(lane < 64, pltpu.roll(out_a, 64, 1), pltpu.roll(out_b, 64, 1))
                c_ref[start : start + step, cols] = (value / total).astype(bf16)
                lse_ref[start : start + step, cols] = jnp.where(lane < 64, top_a, top_b) + jnp.log(total)

    two = len_ref[0] < rows

    @pl.when(two)
    def _():
        run(rows // 2)

    @pl.when(jnp.logical_not(two))
    def _():
        run(rows)


def attn_fwd(place, lengths, scales, pieces, x, deps):
    rows, width = x.shape
    group = 256
    count = len(pieces)
    cols = pl.BlockSpec((rows, group), lambda g: (0, g))
    return pl.pallas_call(
        functools.partial(attn_fwd_kernel, block=512, count=count, deps=len(deps)),
        grid=(width // group,),
        in_specs=[SMEM] * 3 + [ANY] * (count + len(deps)) + [pl.BlockSpec((rows, width), lambda g: (0, 0))],
        out_specs=[cols] * 5 + [pl.BlockSpec((16, width), lambda g: (0, 0))],
        out_shape=[SDS((rows, width), bf16)] * 4 + [SDS((rows, width), f32), SDS((16, width), f32)],
        scratch_shapes=[pltpu.VMEM((width, 3 * width), bf16), pltpu.VMEM((count, 16, width), bf16),
                        pltpu.SemaphoreType.DMA((3 * count,)), pltpu.SemaphoreType.DMA((count,))],
        compiler_params=params(),
        cost_estimate=cost(20e9, 12e6, 12e6),
        name="attention_forward",
    )(place, lengths, scales, *pieces, *deps, x)


def order_rows(place_ref, source_t, dest):
    cores = dest.shape[0]
    if cores == 1:
        dest[0] = source_t
        return
    blocks = 8
    size = source_t.shape[0] // blocks
    for block in range(blocks):
        at = pl.multiple_of(((block // 2) ^ place_ref[1]) * size, 16)
        dest[(block % 2) ^ place_ref[0], pl.ds(at, size), :] = source_t[block * size : (block + 1) * size]


def turn_kernel(place_ref, source_ref, out_ref):
    order_rows(place_ref, source_ref[...].T, out_ref)


def turn(place, source, cores):
    rows, width = source.shape
    vmem = pl.BlockSpec(memory_space=pltpu.VMEM)
    return pl.pallas_call(
        turn_kernel,
        in_specs=[SMEM, vmem],
        out_specs=vmem,
        out_shape=SDS((cores, width // cores, rows), bf16),
        compiler_params=params(),
        cost_estimate=cost(1e6, 3e6),
        name="turn",
    )(place, source)


def attn_bwd_kernel(
    place_ref, len_ref, q_ref, k_ref, v_ref, dc_ref, c_ref, lse_ref, x_hbm, c_hbm, dh_ref, *refs, block, cores, last, shard_first, deps,
):
    refs = refs[deps:]
    if last:
        before_a_ref, before_b_ref, vg_ref, b1g_ref, *refs = refs
    grads = refs[:cores]
    dqkv_ref, sum_ref, dk_acc, dv_acc, dq_acc, x_t, c_t, sems = refs[cores:]
    rows = q_ref.shape[0]
    pair = pl.program_id(0)
    pairs = pl.num_programs(0)
    span_cols = dqkv_ref.shape[1] // 3
    total_width = x_t.shape[0] * x_t.shape[1]
    lane = lax.broadcasted_iota(jnp.int32, (1, 128), 1)
    masks = [lane < 64, lane >= 64]

    turned_copies = [
        pltpu.make_async_copy(x_hbm, x_t, sems.at[0]),
        pltpu.make_async_copy(c_hbm, c_t, sems.at[1]),
    ]

    @pl.when(pair == 0)
    def _():
        for copy in turned_copies:
            copy.start()

    prod = (dc_ref[...].astype(f32) * c_ref[...].astype(f32)).T
    row_dots = [col_sum(prod[:64]), col_sum(prod[64:])]
    lse = lse_ref[...].T
    lse_rows = [lse[0:1], lse[64:65]]

    def run(span):
        step = min(block, span)
        for low in range(0, rows, span):
            k_rows = k_ref[low : low + span, :]
            v_rows = v_ref[low : low + span, :]
            k_cols = k_rows.astype(f32).T.astype(bf16)
            for start in range(low, low + span, step):
                q_rows = q_ref[start : start + step, :]
                dc_rows = dc_ref[start : start + step, :]
                probs, d_scores, q_own, dc_own, dq_parts = [], [], [], [], []
                for head in range(2):
                    q_head = jnp.where(masks[head], q_rows, jnp.zeros_like(q_rows)) * jnp.asarray(0.125, bf16)
                    dc_head = jnp.where(masks[head], dc_rows, jnp.zeros_like(dc_rows))
                    prob = jnp.exp(dot_last(k_rows, q_head) - lse_rows[head][:, start : start + step])
                    d_prob = dot_last(v_rows, dc_head)
                    d_score = (prob * (d_prob - row_dots[head][:, start : start + step])).astype(bf16)
                    probs.append(prob.astype(bf16))
                    d_scores.append(d_score)
                    q_own.append(q_head)
                    dc_own.append(dc_head)
                    dq_parts.append(dot(k_cols[head * 64 : head * 64 + 64], d_score))
                dq_acc[:, start : start + step] = jnp.concatenate(dq_parts, axis=0)
                dv = dot(jnp.concatenate(probs, axis=1), jnp.concatenate(dc_own, axis=0))
                dk = dot(jnp.concatenate(d_scores, axis=1), jnp.concatenate(q_own, axis=0))
                if start == low:
                    dv_acc[low : low + span, :] = dv
                    dk_acc[low : low + span, :] = dk
                else:
                    dv_acc[low : low + span, :] += dv
                    dk_acc[low : low + span, :] += dk

    two = len_ref[0] < rows

    @pl.when(two)
    def _():
        run(rows // 2)

    @pl.when(jnp.logical_not(two))
    def _():
        run(rows)

    dq = dq_acc[...].T * 0.125

    def put(part, value):
        at = pl.multiple_of(part * span_cols + pair * 128, 128)
        dqkv_ref[:, pl.ds(at, 128)] = value.astype(bf16)

    put(0, dq)
    put(1, dk_acc[...])
    put(2, dv_acc[...])
    low = before_a_ref.shape[1] if last else 0
    here = pl.ds(pl.multiple_of(low + pair * 128, 128), 128)
    if last:
        @pl.when(pair == 0)
        def _():
            sum_ref[0:2, : before_a_ref.shape[1]] = before_a_ref[0:2, :]
            sum_ref[0:2, low + span_cols :] = before_b_ref[0:2, :]
            sum_ref[2:8, :] = vg_ref[2:8, :]
            for row in range(b1g_ref.shape[1] // total_width):
                sum_ref[8 + row : 9 + row, :] = b1g_ref[0:1, row * total_width : (row + 1) * total_width]

    sum_ref[0:1, here] = col_sum(dq)
    sum_ref[1:2, here] = col_sum(dv_acc[...])

    @pl.when(pair == pairs - 1)
    def _():
        for copy in turned_copies:
            copy.wait()
        for core in reversed(range(cores)):
            out = grads[core]
            spots = out.shape[1 if shard_first else 0]
            size = x_t.shape[1] // spots
            for plane in range(4):
                left = x_t if plane < 3 else c_t
                right = dqkv_ref[:, plane * span_cols : (plane + 1) * span_cols] if plane < 3 else dh_ref[...]
                value = dot(left[core], right).astype(bf16)
                if shard_first:
                    out[plane] = value.reshape(spots, size, span_cols)
                else:
                    out[:, pl.ds(plane ^ place_ref[2], 1), :size] = value.reshape(spots, 1, size, span_cols)
        if last and cores == 2:
            row = lax.broadcasted_iota(jnp.int32, (16, span_cols), 0)
            col = lax.broadcasted_iota(jnp.int32, (16, span_cols), 1)
            kept = (row < 3) & (col < size)
            even = place_ref[0] == 0
            for plane in range(4):
                rows_here = sum_ref[...] if plane == 0 else pltpu.roll(sum_ref[...], 16 - 3 * plane, 0)
                for spot in range(4):
                    tiles = []
                    for core in range(2):
                        start = (2 * spot + core) * size
                        turned = rows_here if start == 0 else pltpu.roll(rows_here, total_width - start, 1)
                        tiles.append(jnp.where(kept, turned[:, :span_cols], 0.0).astype(bf16))
                    for core in range(2):
                        tile = jnp.where(even, tiles[core], tiles[1 - core])
                        grads[core][spot ^ place_ref[1], plane ^ place_ref[2], size:, :] = tile


def attn_bwd(place, lengths, q, k, v, dc, c, lse, x_turned, c_turned, dh_low, first, pairs, cores, spots, deps, before=None, shard_first=False):
    rows, width = q.shape
    last = before is not None
    size = pairs * 128
    cols = pl.BlockSpec((rows, 128), lambda g: (0, first + g))

    def whole(shape):
        return pl.BlockSpec(shape, lambda g: (0,) * len(shape))

    depth = width // (cores * spots)
    shape = (spots, 4, depth + (16 if last and cores == 2 else 0), size)
    shape = (shape[1], shape[0]) + shape[2:] if shard_first else shape
    sums = (16, width if last else size)
    more = list(before) if last else []
    return pl.pallas_call(
        functools.partial(attn_bwd_kernel, block=512, cores=cores, last=last, shard_first=shard_first, deps=len(deps)),
        grid=(pairs,),
        in_specs=[SMEM] * 2 + [cols] * 6 + [ANY] * 2
        + [pl.BlockSpec((rows, size), lambda g: (0, first // pairs))] + [ANY] * len(deps) + [whole(m.shape) for m in more],
        out_specs=[whole(shape)] * cores + [whole((rows, 3 * size)), whole(sums)],
        out_shape=[SDS(shape, bf16)] * cores + [SDS((rows, 3 * size), bf16), SDS(sums, f32)],
        scratch_shapes=[
            pltpu.VMEM((rows, 128), f32), pltpu.VMEM((rows, 128), f32), pltpu.VMEM((128, rows), f32),
            pltpu.VMEM((cores, width // cores, rows), bf16), pltpu.VMEM((cores, width // cores, rows), bf16),
            pltpu.SemaphoreType.DMA((2,)),
        ],
        compiler_params=params(),
        cost_estimate=cost(50e9 * size / width, 30e6 * size / width, 12e6 * size / width),
        name="attention_backward",
    )(place, lengths, q, k, v, dc, c, lse, x_turned, c_turned, dh_low, *deps, *more)


def mid_fwd_kernel(place_ref, scale_ref, *refs, chunk, count, deps):
    pieces = refs[:count]
    refs = refs[:count] + refs[count + deps :]
    (x_ref, c_ref, vec_ref, n1_ref, r1_ref, y1_ref, a_ref, gp_ref,
     wo_ref, w1_ref, out_sems, up_sems) = refs[count:]
    rows, width = x_ref.shape
    first = pl.program_id(0) == 0
    out_copies = block_copies(place_ref, pieces, [4], wo_ref, out_sems)
    up_copies = block_copies(place_ref, pieces, range(4), w1_ref, up_sems)

    @pl.when(first)
    def _():
        start_all(out_copies)
        start_all(up_copies)
        wait_all(out_copies)

    residual = x_ref[...].astype(f32) + dot(c_ref[...], wo_ref[...]) * scale_ref[3] + vec_ref[2:3]
    normed, inv_std = normalize(residual)
    n1_ref[...] = normed
    r1_ref[...] = jnp.broadcast_to(inv_std, (rows, 128))
    y1 = (normed * vec_ref[3:4] + vec_ref[4:5]).astype(bf16)
    y1_ref[...] = y1

    @pl.when(first)
    def _():
        wait_all(up_copies)

    for start in range(0, w1_ref.shape[1], chunk):
        block, at = divmod(start, width)
        cols = slice(start, start + chunk)
        bias = vec_ref[8 + block : 9 + block, at : at + chunk]
        u = dot(y1, w1_ref[:, cols]) * scale_ref[4] + bias
        square = u * u
        half = 0.5 + 0.5 * jnp.tanh(u * (GELU_K + (GELU_K * GELU_C) * square))
        act = u * half
        a_ref[:, cols] = act.astype(bf16)
        gp_ref[:, cols] = (half + act * (1.0 - half) * (2 * GELU_K + (6 * GELU_K * GELU_C) * square)).astype(bf16)


def mid_fwd(place, scales, pieces, x, c, vec, deps):
    rows, width = x.shape
    hidden = 4 * pieces[0].shape[1]
    tile = 512
    count = len(pieces)

    def row(size):
        return pl.BlockSpec((tile, size), lambda i: (i, 0))

    def full(arr):
        return pl.BlockSpec(arr.shape, lambda i: (0, 0))

    return pl.pallas_call(
        functools.partial(mid_fwd_kernel, chunk=256, count=count, deps=len(deps)),
        grid=(rows // tile,),
        in_specs=[SMEM] * 2 + [ANY] * (count + len(deps)) + [row(width), row(width), full(vec)],
        out_specs=[row(width), row(128), row(width), row(hidden), row(hidden)],
        out_shape=[SDS((rows, width), f32), SDS((rows, 128), f32), SDS((rows, width), bf16),
                   SDS((rows, hidden), bf16), SDS((rows, hidden), bf16)],
        scratch_shapes=[pltpu.VMEM((width, width), bf16), pltpu.VMEM((width, hidden), bf16),
                        pltpu.SemaphoreType.DMA((count,)), pltpu.SemaphoreType.DMA((4 * count,))],
        compiler_params=params(),
        cost_estimate=cost(12e9, 25e6, 3e6),
        name="middle_forward",
    )(place, scales, *pieces, *deps, x, c, vec)


def second_norm_kernel(place_ref, scale_ref, *refs, cores, tiles):
    downs = refs[:cores]
    (act_ref, n1_ref, do_ref, vec_ref, out_ref, dz_ref, dzb_ref, vg_ref, grad_ref,
     w2_ref, act, dz_all, left_t, down_sems, act_sems) = refs[cores:]
    step = pl.program_id(0)
    tile = n1_ref.shape[0]

    def act_copy(index):
        rows = pl.ds(pl.multiple_of(index * tile, tile), tile)
        return pltpu.make_async_copy(act_ref.at[rows], act.at[rows], act_sems.at[index])

    copies = down_copies(place_ref, downs, w2_ref, down_sems)
    spots = downs[0].shape[1]
    size = w2_ref.shape[1] // spots

    def body(arriving):
        if arriving:
            act_copy(0).start()
            start_all(copies)
            for index in range(1, tiles):
                act_copy(index).start()
            vg_ref[...] = jnp.zeros_like(vg_ref)
        act_copy(step).wait()
        rows = pl.ds(pl.multiple_of(step * tile, tile), tile)
        g1, c1, b2, g2, c2 = [vec_ref[i : i + 1] for i in range(3, 8)]
        if arriving:
            product = None
            for spot in range(spots):
                wait_all(some_copies(copies, spot, spots))
                cols = slice(spot * size, (spot + 1) * size)
                more = dot_last(act[rows, cols], w2_ref[:, cols])
                product = more if product is None else product + more
        else:
            product = dot_last(act[rows, :], w2_ref[...])
        residual = n1_ref[...] * g1 + c1 + product * scale_ref[5] + b2
        n2, r2 = normalize(residual)
        out_ref[...] = (n2 * g2 + c2).astype(bf16)
        d_out = do_ref[...].astype(f32)
        vg_ref[6:7] += col_sum(d_out * n2)
        vg_ref[7:8] += col_sum(d_out)
        dz = normalize_back(d_out * g2, n2, r2)
        vg_ref[5:6] += col_sum(dz)
        dz_ref[...] = dz
        dz_low = dz.astype(bf16)
        dzb_ref[...] = dz_low
        dz_all[rows, :] = dz_low

    @pl.when(step == 0)
    def _():
        body(True)

    @pl.when((step > 0) & (step < tiles))
    def _():
        body(False)

    @pl.when(step == tiles)
    def _():
        left_t[...] = dz_all[...].T

    @pl.when(step >= tiles)
    def _():
        blocks, slots, size, cols = grad_ref.shape
        wide = blocks * cols
        start = pl.multiple_of((step - tiles) * wide, 128)
        value = dot(left_t[...], act[:, pl.ds(start, wide)]).astype(bf16)
        for block in range(blocks):
            grad_ref[block] = value[:, block * cols : (block + 1) * cols].reshape(slots, size, cols)


def second_norm(place, scales, downs, n1, act, d_out, vec, blocks):
    rows, width = n1.shape
    hidden = act.shape[1]
    tile = 256
    tiles = rows // tile
    some = min(2, blocks)
    block = (some, 4, width // 4, hidden // blocks)

    def row(size):
        return pl.BlockSpec((tile, size), lambda i: (jnp.minimum(i, tiles - 1), 0))

    return pl.pallas_call(
        functools.partial(second_norm_kernel, cores=len(downs), tiles=tiles),
        grid=(tiles + blocks // some,),
        in_specs=[SMEM] * 2 + [ANY] * (len(downs) + 1)
        + [row(width), row(width), pl.BlockSpec(vec.shape, lambda i: (0, 0))],
        out_specs=[row(width)] * 3 + [pl.BlockSpec((8, width), lambda i: (0, 0)),
                                      pl.BlockSpec(block, lambda i: (jnp.maximum(i - tiles, 0), 0, 0, 0))],
        out_shape=[SDS((rows, width), bf16), SDS((rows, width), f32), SDS((rows, width), bf16), SDS((8, width), f32),
                   SDS((blocks,) + block[1:], bf16)],
        scratch_shapes=[pltpu.VMEM((width, hidden), bf16), pltpu.VMEM((rows, hidden), bf16),
                        pltpu.VMEM((rows, width), bf16), pltpu.VMEM((width, rows), bf16),
                        pltpu.SemaphoreType.DMA((4 * downs[0].shape[1] * len(downs),)),
                        pltpu.SemaphoreType.DMA((tiles,))],
        compiler_params=params(),
        cost_estimate=cost(16e9, 30e6),
        name="second_norm",
    )(place, scales, *downs, act, n1, d_out, vec)


def mid_bwd_kernel(place_ref, scale_ref, *refs, chunk, count, cores, outs, tiles, deps):
    downs, pieces, refs = refs[:cores], refs[cores : cores + count], refs[cores + count + deps :]
    y1_hbm, n1_ref, r1_ref, gp_ref, dz_ref, dzb_ref, vec_ref = refs[:7]
    dh_ref, dhb_ref, dc_ref, vg_ref, b1g_ref = refs[7:12]
    grads = refs[12 : 12 + outs]
    wo_ref, w1_ref, w2_ref, du_all, y1, left_t, out_sems, up_sems, down_sems, y1_sem = refs[12 + outs :]
    step = pl.program_id(0)
    tile, width = n1_ref.shape
    first = step == 0
    y1_copy = pltpu.make_async_copy(y1_hbm, y1, y1_sem.at[0])

    w2_copies = down_copies(place_ref, downs, w2_ref, down_sems)
    w1_copies = block_copies(place_ref, pieces, range(4), w1_ref, up_sems)
    wo_copies = block_copies(place_ref, pieces, [4], wo_ref, out_sems)
    spots = downs[0].shape[1]

    def body(arriving):
        if arriving:
            start_all(w2_copies)
            start_all(w1_copies)
            start_all(wo_copies)
            y1_copy.start()
            vg_ref[...] = jnp.zeros_like(vg_ref)
            b1g_ref[...] = jnp.zeros_like(b1g_ref)
        rows = pl.ds(pl.multiple_of(step * tile, tile), tile)
        g1 = vec_ref[3:4]
        n1 = n1_ref[...]
        dz_low = dzb_ref[...]
        for start in range(0, w1_ref.shape[1], chunk):
            spot, rest = divmod(start * spots, w1_ref.shape[1])
            if arriving and rest == 0:
                wait_all(some_copies(w2_copies, spot, spots))
            cols = slice(start, start + chunk)
            du = dot(dz_low, w2_ref[:, cols]) * scale_ref[5] * gp_ref[:, cols].astype(f32)
            b1g_ref[0:1, cols] += col_sum(du)
            du_all[rows, cols] = du.astype(bf16)
        if arriving:
            wait_all(w1_copies)
            wait_all(wo_copies)
        dy = dz_ref[...] + dot_last(du_all[rows, :], w1_ref[...]) * scale_ref[4]
        vg_ref[3:4] += col_sum(dy * n1)
        vg_ref[4:5] += col_sum(dy)
        dh = normalize_back(dy * g1, n1, r1_ref[:, 0:1])
        vg_ref[2:3] += col_sum(dh)
        dh_ref[...] = dh
        dh_low = dh.astype(bf16)
        dhb_ref[...] = dh_low
        dc_ref[...] = (dot_last(dh_low, wo_ref[...]) * scale_ref[3]).astype(bf16)

    @pl.when(first)
    def _():
        body(True)

    @pl.when((step > 0) & (step < tiles))
    def _():
        body(False)

    @pl.when(step == tiles)
    def _():
        y1_copy.wait()
        order_rows(place_ref, y1[...].T, left_t)

    @pl.when(step >= tiles)
    def _():
        cols = pl.ds(pl.multiple_of((step - tiles) * width, 128), width)
        for core in reversed(range(outs)):
            grads[core][...] = dot(left_t[core], du_all[:, cols]).astype(bf16).reshape(grads[core].shape)


def mid_bwd(place, scales, pieces, downs, n1, r1, y1, gelu_grad, dz, dz_low, vec, cores, spots, deps):
    rows, width = n1.shape
    hidden = gelu_grad.shape[1]
    tile = 256
    tiles = rows // tile
    count = len(pieces)
    block = (spots, 1, width // (cores * spots), width)

    def row(size):
        return pl.BlockSpec((tile, size), lambda i: (jnp.minimum(i, tiles - 1), 0))

    def whole(shape):
        return pl.BlockSpec(shape, lambda i: (0,) * len(shape))

    return pl.pallas_call(
        functools.partial(
            mid_bwd_kernel, chunk=256, count=count, cores=len(downs), outs=cores, tiles=tiles, deps=len(deps)
        ),
        grid=(tiles + 4,),
        in_specs=[SMEM] * 2 + [ANY] * (count + len(downs) + len(deps) + 1)
        + [row(width), row(128), row(hidden), row(width), row(width), whole(vec.shape)],
        out_specs=[row(width), row(width), row(width), whole((8, width)), whole((8, hidden))]
        + [pl.BlockSpec(block, lambda i: (0, jnp.maximum(i - tiles, 0), 0, 0))] * cores,
        out_shape=[SDS((rows, width), f32), SDS((rows, width), bf16), SDS((rows, width), bf16),
                   SDS((8, width), f32), SDS((8, hidden), f32)]
        + [SDS((spots, 4) + block[2:], bf16)] * cores,
        scratch_shapes=[pltpu.VMEM((width, width), bf16), pltpu.VMEM((width, hidden), bf16),
                        pltpu.VMEM((width, hidden), bf16), pltpu.VMEM((rows, hidden), bf16),
                        pltpu.VMEM((rows, width), bf16), pltpu.VMEM((cores, width // cores, rows), bf16),
                        pltpu.SemaphoreType.DMA((count,)), pltpu.SemaphoreType.DMA((4 * count,)),
                        pltpu.SemaphoreType.DMA((4 * downs[0].shape[1] * len(downs),)),
                        pltpu.SemaphoreType.DMA((1,))],
        compiler_params=params(),
        cost_estimate=cost(28e9, 40e6),
        name="middle_backward",
    )(place, scales, *downs, *pieces, *deps, y1, n1, r1, gelu_grad, dz, dz_low, vec)


def input_grad_kernel(place_ref, scale_ref, *refs, count, chunks, deps):
    pieces = refs[:count]
    parts = refs[count : count + chunks]
    dh_ref, out_ref, w_ref, sems = refs[count + chunks + deps :]
    width = dh_ref.shape[1]

    @pl.when(pl.program_id(0) == 0)
    def _():
        copies = block_copies(place_ref, pieces, range(3), w_ref, sems)
        start_all(copies)
        wait_all(copies)

    total = dh_ref[...]
    for plane in range(3):
        product = None
        start = plane * width
        for part in parts:
            size = part.shape[1] // 3
            more = dot_last(part[:, plane * size : (plane + 1) * size], w_ref[:, start : start + size])
            product = more if product is None else product + more
            start += size
        total = total + product * scale_ref[plane]
    out_ref[...] = total.astype(bf16)


def input_grad(place, scales, pieces, parts, dh, deps):
    rows, width = dh.shape
    tile = 512
    count, chunks = len(pieces), len(parts)

    def row(size):
        return pl.BlockSpec((tile, size), lambda i: (i, 0))

    return pl.pallas_call(
        functools.partial(input_grad_kernel, count=count, chunks=chunks, deps=len(deps)),
        grid=(rows // tile,),
        in_specs=[SMEM] * 2 + [ANY] * count + [row(p.shape[1]) for p in parts] + [ANY] * len(deps) + [row(width)],
        out_specs=row(width),
        out_shape=SDS((rows, width), bf16),
        scratch_shapes=[pltpu.VMEM((width, 3 * width), bf16), pltpu.SemaphoreType.DMA((3 * count,))],
        compiler_params=params(),
        cost_estimate=cost(9e9, 2 * (rows * width * 6 + 3 * width * width)),
        name="input_gradient",
    )(place, scales, *pieces, *parts, *deps, dh)


def swap(value, axis, mask):
    count = lax.axis_size(axis)
    return lax.ppermute(value, axis, [(i, i ^ mask) for i in range(count)])


def bits(axis):
    return [1 << b for b in range(lax.axis_size(axis).bit_length() - 1)]


def doubling_gather(value, axis, dim):
    index = lax.axis_index(axis)
    for bit in bits(axis):
        other = swap(value, axis, bit)
        high = (index & bit) != 0
        value = jnp.concatenate(
            [jnp.where(high, other, value), jnp.where(high, value, other)], axis=dim
        )
    return value


def doubling_sum(value):
    for axis in ("dp", "shard"):
        for bit in bits(axis):
            value = value + swap(value, axis, bit)
    return value


def total_sum(value):
    value = value + swap(value, "dp", 1)
    for axis, masks in (("dp", (6, 4, 2)), ("shard", (3, 2, 1))):
        others = [swap(value, axis, mask) for mask in masks]
        value = (value + others[0]) + (others[1] + others[2])
    return value


def four(block, axis, unit):
    return [block] + [swap(block, axis, unit * m) for m in (1, 2, 3)]


def core_sum_kernel(*refs, sizes, deps):
    count = len(sizes)
    outs = refs[2 * count + deps :]
    at = 0
    for index, (depth, width) in enumerate(sizes):
        mine, got = refs[2 * index : 2 * index + 2]
        for spot, out in enumerate(outs):
            total = mine[spot, 0].astype(f32) + got[spot, 0].astype(f32)
            out[0, :depth, at : at + width] = total.astype(bf16)
            if depth < out.shape[1]:
                out[0, depth:, at : at + width] = jnp.zeros((out.shape[1] - depth, width), bf16)
        at += width


def core_sum(pairs, deps=()):
    spots, slots = pairs[0][0].shape[:2]
    sizes = [mine.shape[2:] for mine, _ in pairs]
    rows, width = max(s[0] for s in sizes), sum(s[1] for s in sizes)
    specs = []
    for mine, got in pairs:
        specs += [pl.BlockSpec((spots, 1) + mine.shape[2:], lambda i: (0, i, 0, 0))] * 2
    return pl.pallas_call(
        functools.partial(core_sum_kernel, sizes=sizes, deps=len(deps)),
        grid=(slots,),
        in_specs=specs + [ANY] * len(deps),
        out_specs=[pl.BlockSpec((1, rows, width), lambda i: (i, 0, 0))] * spots,
        out_shape=[SDS((slots, rows, width), bf16)] * spots,
        compiler_params=params(),
        cost_estimate=cost(1e6, 6 * spots * slots * rows * width),
        name="core_sum",
    )(*[part for pair in pairs for part in pair], *deps)


def pair_sum_kernel(mine_ref, got_ref, *refs):
    refs[-1][...] = (mine_ref[...].astype(f32) + got_ref[...].astype(f32)).astype(bf16)


def pair_sum(mine, got, deps=()):
    block = pl.BlockSpec((1,) + mine.shape[1:], lambda i: (i, 0, 0, 0))
    return pl.pallas_call(
        pair_sum_kernel,
        grid=mine.shape[:1],
        in_specs=[block, block] + [ANY] * len(deps),
        out_specs=block,
        out_shape=SDS(mine.shape, bf16),
        compiler_params=params(),
        cost_estimate=cost(1e6, 6 * mine.size),
        name="pair_sum",
    )(mine, got, *deps)


def plane_sum_kernel(*refs, count, deps):
    outs = refs[4 * count + deps :]
    at = 0
    for index in range(count):
        parts = refs[4 * index : 4 * index + 4]
        depth, width = parts[0].shape[1:]
        for slot in range(parts[0].shape[0]):
            total = parts[0][slot].astype(f32) + parts[1][slot].astype(f32)
            total = total + (parts[2][slot].astype(f32) + parts[3][slot].astype(f32))
            out = outs[0].at[slot] if len(outs) == 1 else outs[slot]
            out[:depth, at : at + width] = total.astype(out.dtype)
            if depth < out.shape[0]:
                out[depth:, at : at + width] = jnp.zeros((out.shape[0] - depth, width), out.dtype)
        at += width


def plane_sum(groups, split, deps=()):
    slots = groups[0][0].shape[0]
    rows = max(parts[0].shape[1] for parts in groups)
    width = sum(parts[0].shape[2] for parts in groups)
    vmem = pl.BlockSpec(memory_space=pltpu.VMEM)
    shapes = [SDS((rows, width), f32)] + [SDS((rows, width), bf16)] * (slots - 1)
    if not split:
        shapes = [SDS((slots, rows, width), bf16)]
    return pl.pallas_call(
        functools.partial(plane_sum_kernel, count=len(groups), deps=len(deps)),
        in_specs=[vmem] * (4 * len(groups)) + [ANY] * len(deps),
        out_specs=[vmem] * len(shapes),
        out_shape=shapes,
        compiler_params=params(),
        cost_estimate=cost(1e6, 4 * slots * rows * width),
        name="plane_sum",
    )(*[part for parts in groups for part in parts], *deps)


def exchange(parts, axis, unit):
    return [parts[0]] + [swap(parts[m], axis, unit * m) for m in (1, 2, 3)]


def after(value, *others):
    return lax.optimization_barrier((value,) + others)[0]

def adam_update(gradient, master, first_old, second_old, average, step_rate, decay_rate):
    first_new = beta_first * first_old + (1.0 - beta_first) * gradient
    second_new = beta_second * second_old + (1.0 - beta_second) * gradient * gradient
    first_hat = first_new / (1.0 - beta_first**STEP)
    second_hat = second_new / (1.0 - beta_second**STEP)
    master_new = master - step_rate * (
        first_hat / (jnp.sqrt(second_hat) + adam_eps) + decay_rate * master
    )
    average_new = average_keep * average + (1.0 - average_keep) * master_new
    return (first_new, second_new, master_new, average_new)


def own_sums_kernel(*refs):
    firsts, lasts, (up_ref, down_ref, attn_ref, vec_ref, square_ref) = refs[:4], refs[4:8], refs[8:]
    rows = attn_ref.shape[0]
    first, last = [
        (parts[0][...].astype(f32) + parts[1][...].astype(f32)) + (parts[2][...].astype(f32) + parts[3][...].astype(f32))
        for parts in (firsts, lasts)
    ]
    attn_ref[:, : first.shape[1]] = first
    attn_ref[:, first.shape[1] :] = last[:rows]
    at = 0
    vec_ref[...] = last[rows:, at : at + 128]
    total = jnp.sum(first * first) + jnp.sum(last * last)
    for ref in (up_ref, down_ref):
        value = ref[...].astype(f32)
        total = total + jnp.sum(value * value)
    square_ref[...] = jnp.full(square_ref.shape, total, f32)


def own_sums(firsts, lasts, own_up, own_down):
    vmem = pl.BlockSpec(memory_space=pltpu.VMEM)
    rows, width = firsts[0].shape[0], firsts[0].shape[1] + lasts[0].shape[1]
    return pl.pallas_call(
        own_sums_kernel,
        in_specs=[vmem] * 10,
        out_specs=[vmem] * 3,
        out_shape=[SDS((rows, width), f32), SDS((16, 128), f32), SDS((8, 128), f32)],
        compiler_params=params(),
        cost_estimate=cost(1e6, 2e6),
        name="own_sums",
    )(*firsts, *lasts, own_up, own_down)


def update_kernel(square_ref, attn_ref, up_ref, down_ref, vec_ref, *refs):
    states, news, norm_ref = refs[:16], refs[16:32], refs[32]
    norm = jnp.sqrt(square_ref[...])
    norm_ref[0, 0] = jnp.max(norm)
    factor = jnp.minimum(1.0, clip_limit / (norm + norm_eps))[0:1, 0:1]
    rows, cols = states[12].shape
    grads = (
        attn_ref[...],
        up_ref[...].astype(f32),
        down_ref[...].astype(f32),
        vec_ref[:rows, :cols],
    )
    for index, grad in enumerate(grads):
        rates = (vector_rate, 0.0) if index == 3 else (matrix_rate, matrix_decay)
        old = [ref[...] for ref in states[4 * index : 4 * index + 4]]
        for ref, new in zip(news[4 * index : 4 * index + 4], adam_update(grad * factor, *old, *rates)):
            ref[...] = new


def update(squares, own_attn, own_up, own_down, own_vector, states):
    vmem = pl.BlockSpec(memory_space=pltpu.VMEM)
    states = list(states[:8]) + [state.T for state in states[8:]]
    *news, norm = pl.pallas_call(
        update_kernel,
        in_specs=[vmem] * 21,
        out_specs=[vmem] * 16 + [SMEM],
        out_shape=[SDS(state.shape, f32) for state in states] + [SDS((1, 1), f32)],
        compiler_params=params(),
        cost_estimate=cost(1e7, 8e6),
        name="state_update",
    )(squares, own_attn, own_up, own_down, own_vector, *states)
    return news[:8] + [new.T for new in news[8:]], norm


def on_device(
    tokens, out_grad, first_lengths, quant_scales, attn_quant, up_quant, down_quant,
    attn_master, attn_first, attn_second, attn_average,
    up_master, up_first, up_second, up_average,
    down_master, down_first, down_second, down_average,
    vector_master, vector_first, vector_second, vector_average,
):
    width = tokens.shape[1]
    dp_index, shard_index = lax.axis_index("dp"), lax.axis_index("shard")
    small = lax.axis_size("dp") == 8 and lax.axis_size("shard") == 4 and attn_quant.shape == (96, 768)
    gather = functools.partial(lax.all_gather, tiled=True)
    scatter = functools.partial(lax.psum_scatter, tiled=True)
    down_turned = down_quant.T
    vector_low = vector_master.astype(bf16)
    if small:
        cores, spots = 2, 4
        place = jnp.stack([dp_index & 1, dp_index >> 1, shard_index]).astype(jnp.int32)
        packed = jnp.pad(vector_low.T, ((0, 13), (0, width - 96)))
        blocks = four(jnp.concatenate([attn_quant, packed]), "shard", 1)
        x_turned = turn(place, tokens, cores)
        qkv, w_out = attn_stack(place, blocks, [x_turned])
        pieces = four(qkv, "dp", 2)
        up_blocks = four(after(up_quant, qkv), "shard", 1)
        down = after(lax.all_gather(down_turned, "dp"), pieces[1]).reshape(4, 2, 192, -1)
        down = lax.dynamic_index_in_dim(down, dp_index & 1, 1, keepdims=False)
        half = down
        down = lax.all_gather(after(down, *pieces[1:], *up_blocks), "shard")
        up = stack(place, up_blocks, 2, w_out, deps=pieces[1:2])
        ups = four(up, "dp", 2)
        pieces = pieces + [swap(after(piece, up, half), "dp", 1) for piece in pieces]
        early = [up]
    else:
        cores, spots = 1, 1
        place = jnp.zeros((3,), jnp.int32)
        x_turned = turn(place, tokens, cores)
        vec_w = doubling_gather(doubling_gather(vector_low, "shard", 1), "dp", 0)
        attn_w = gather(gather(attn_quant, "shard", axis=1), "dp", axis=0)
        up_w = gather(gather(up_quant, "shard", axis=1), "dp", axis=0)
        down_w = gather(gather(down_turned, "shard", axis=0), "dp", axis=1)
        planes = [attn_w[:, i * width : (i + 1) * width] for i in range(4)]
        pieces = [jnp.concatenate(planes[:3] + [jnp.pad(vec_w.T, ((0, 4), (0, 0)))])]
        ups = [jnp.concatenate([up_w[:, i * width : (i + 1) * width] for i in range(4)] + planes[3:])]
        downs = [down_w.reshape(4, 1, width // 4, -1)]
        early = []

    q, k, v, c, lse, vec = attn_fwd(place, first_lengths, quant_scales, pieces, tokens, early)
    c_turned = turn(place, c, cores)
    if small:
        ups = [ups[0]] + [after(piece, c_turned) for piece in ups[1:]]
        ups = ups + [swap(piece, "dp", 1) for piece in ups]
    n1, r1, y1, act, gelu_grad = mid_fwd(place, quant_scales, ups, tokens, c, vec, [c_turned])
    if small:
        downs = [down, swap(after(down, act), "dp", 1)]
    layer_out, dz, dz_low, vec_second, grad_down = second_norm(
        place, quant_scales, downs, n1, act, out_grad, vec, cores * spots
    )
    dh, dh_low, dc, vec_first, b1_grad, *up_parts = mid_bwd(
        place, quant_scales, ups, downs, n1, r1, y1, gelu_grad, dz, dz_low, vec, cores, spots, [grad_down]
    )
    vec_grad = jnp.concatenate([vec_first[:5], vec_second[5:]])
    attn = functools.partial(
        attn_bwd, place, first_lengths, q, k, v, dc, c, lse, x_turned, c_turned, dh_low, cores=cores, spots=spots
    )
    if small:
        own_down = lax.psum_scatter(grad_down, "dp", scatter_dimension=0)
        up_got = swap(up_parts[1], "dp", 1)
        *parts_p, d_p, sums_p = attn(first=4, pairs=2, deps=up_parts[1:])
        up_plane = core_sum([(up_parts[0], up_got)], [d_p])
        got_p = swap(after(parts_p[1], up_plane[0]), "dp", 1)
        up_plane = exchange(up_plane, "dp", 2)
        *parts_q, d_q, sums_q = attn(first=0, pairs=3, deps=up_plane[:1], shard_first=True)
        own_down = lax.psum_scatter(own_down, "shard", scatter_dimension=0)
        (up_shards,) = plane_sum([up_plane], False, [d_q, own_down])
        own_up = lax.psum_scatter(up_shards, "shard", scatter_dimension=0)
        got_q = swap(after(parts_q[1], up_shards), "dp", 1)
        *parts_r, d_r, sums = attn(first=3, pairs=1, deps=[up_shards], before=(sums_q, sums_p, vec_grad, b1_grad))
        got_r = swap(parts_r[1], "dp", 1)
        plane_pr = core_sum([(parts_r[0], got_r), (parts_p[0], got_p)], [d_r])
        sum_q = pair_sum(parts_q[0], got_q, [plane_pr[0], own_up])
        plane_pr = exchange(plane_pr, "dp", 2)
        spots_q = lax.psum_scatter(sum_q, "shard", scatter_dimension=0)
        spots_q = exchange(after(spots_q, plane_pr[1]), "dp", 2)
        input_gradient = input_grad(place, quant_scales, pieces, [d_q, d_r, d_p], dh, [plane_pr[0]])
        slots_pr = exchange(plane_sum([plane_pr], True, [input_gradient]), "shard", 1)
    else:
        parts_p, d_p, sums_p = attn(first=4, pairs=2, deps=[])
        parts_q, d_q, sums_q = attn(first=0, pairs=3, deps=[])
        parts_r, d_r, sums = attn(first=3, pairs=1, deps=[], before=(sums_q, sums_p, vec_grad, b1_grad))
        attn_parts = [[parts_q], [parts_r], [parts_p]]
        input_gradient = input_grad(place, quant_scales, pieces, [d_q, d_r, d_p], dh, [])

    rows_own, cols_own = vector_master.shape
    states = (
        attn_master, attn_first, attn_second, attn_average,
        up_master, up_first, up_second, up_average,
        down_master, down_first, down_second, down_average,
        vector_master, vector_first, vector_second, vector_average,
    )
    if small:
        own_attn, own_vector, squares = own_sums(spots_q, slots_pr, own_up, own_down)
        news, grad_norm = update(total_sum(squares), own_attn, own_up, own_down, own_vector, states)
        return (layer_out, input_gradient, grad_norm.reshape(()), *news)
    vec_total = doubling_sum(sums[:12])
    own_vector = lax.dynamic_slice(vec_total, (shard_index * cols_own, dp_index * rows_own), (cols_own, rows_own)).T
    grad_down = grad_down.reshape(width, -1)
    grad_up = up_parts[0][0].transpose(1, 0, 2).reshape(width, -1)
    grad_attn = jnp.concatenate([parts[0][0] for parts in attn_parts], axis=2)
    grad_attn = grad_attn.transpose(1, 0, 2).reshape(width, -1)
    own_down = scatter(scatter(grad_down, "dp", scatter_dimension=1), "shard", scatter_dimension=0).astype(f32).T
    own_up = scatter(scatter(grad_up, "dp", scatter_dimension=0), "shard", scatter_dimension=1).astype(f32)
    own_attn = scatter(scatter(grad_attn, "dp", scatter_dimension=0), "shard", scatter_dimension=1).astype(f32)
    grads = (own_attn, own_up, own_down, own_vector)
    squares = sum(jnp.sum(grad * grad) for grad in grads)
    grad_norm = jnp.sqrt(doubling_sum(jnp.broadcast_to(squares, (8, 128)))[0, 0])
    factor = jnp.minimum(1.0, clip_limit / (grad_norm + norm_eps))
    news = []
    for index, grad in enumerate(grads):
        rates = (vector_rate, 0.0) if index == 3 else (matrix_rate, matrix_decay)
        news += adam_update(grad * factor, *states[4 * index : 4 * index + 4], *rates)
    return (layer_out, input_gradient, grad_norm, *news)


def solution(mesh):
    rows = P(("dp", "shard"), None)
    block = P("dp", "shard")
    in_specs = (rows, rows, P(("dp", "shard")), P()) + (block,) * 19
    out_specs = (rows, rows, P()) + (block,) * 16
    return jax.shard_map(
        on_device, mesh=mesh, in_specs=in_specs, out_specs=out_specs, check_vma=False
    )
```

```python
import functools
import math

import jax
import jax.numpy as jnp
from jax import lax
from jax.experimental import pallas as pl
from jax.experimental.pallas import tpu as pltpu
from jax.sharding import PartitionSpec as P

HEAD_DIM = 64
STEP = 10

norm_eps = 1e-06
clip_limit = 1.0
beta_first = 0.9
beta_second = 0.999
adam_eps = 1e-08
matrix_rate = 0.08
vector_rate = 0.5
matrix_decay = 0.01
average_keep = 0.9

VMEM = 62 * 2**20
GELU_K = math.sqrt(2.0 / math.pi)
GELU_C = 0.044715
f32 = jnp.float32
bf16 = jnp.bfloat16
SDS = jax.ShapeDtypeStruct


def dot(left, right):
    return jnp.dot(left, right, preferred_element_type=f32)


def dot_last(left, right):
    return lax.dot_general(left, right, (((1,), (1,)), ((), ())), preferred_element_type=f32)


def col_sum(value):
    return jnp.sum(value, axis=0, keepdims=True)


def params(**extra):
    return pltpu.CompilerParams(vmem_limit_bytes=VMEM, **extra)


def cost(flops, moved, trans=0):
    return pl.CostEstimate(flops=int(flops), bytes_accessed=int(moved), transcendentals=int(trans))


SMEM = pl.BlockSpec(memory_space=pltpu.SMEM)
ANY = pl.BlockSpec(memory_space=pl.ANY)


def piece_row(place_ref, index, count):
    if count == 1:
        return 0
    half = count // 2
    return ((place_ref[1] ^ (index % half)) * 2) + (place_ref[0] ^ (index // half))


def block_copies(place_ref, pieces, blocks, dest, sems):
    count = len(pieces)
    rows, width = dest.shape[0] // count, pieces[0].shape[1]

    def copy(at, block, index):
        def make():
            row = pl.multiple_of(piece_row(place_ref, index, count) * rows, 16)
            return pltpu.make_async_copy(
                pieces[index].at[block * rows : (block + 1) * rows],
                dest.at[pl.ds(row, rows), at * width : (at + 1) * width],
                sems.at[at * count + index],
            )

        return make

    return [copy(at, block, index) for at, block in enumerate(blocks) for index in range(count)]


def some_copies(copies, part, parts):
    size = len(copies) // parts
    return copies[part * size : (part + 1) * size]


def down_copies(place_ref, sources, dest, sems):
    slots, spots, rows, width = sources[0].shape
    count = len(sources)

    def copy(spot, core, slot):
        def make():
            col = (spot * count + (place_ref[0] ^ core)) * width
            return pltpu.make_async_copy(
                sources[core].at[slot, spot],
                dest.at[slot * rows : (slot + 1) * rows, pl.ds(pl.multiple_of(col, 128), width)],
                sems.at[(spot * count + core) * slots + slot],
            )

        return make

    return [copy(spot, core, slot) for spot in range(spots) for core in range(count) for slot in range(slots)]


def start_all(copies):
    for copy in copies:
        copy().start()


def wait_all(copies):
    for copy in copies:
        copy().wait()


def normalize(value):
    centre = value - jnp.mean(value, axis=-1, keepdims=True)
    inv_std = lax.rsqrt(jnp.mean(centre * centre, axis=-1, keepdims=True) + norm_eps)
    return centre * inv_std, inv_std


def normalize_back(scaled, normed, inv_std):
    return inv_std * (
        scaled
        - jnp.mean(scaled, axis=-1, keepdims=True)
        - normed * jnp.mean(scaled * normed, axis=-1, keepdims=True)
    )


def attn_stack_kernel(place_ref, *refs):
    blocks, qkv_ref, out_ref = refs[:4], refs[-2], refs[-1]
    rows = out_ref.shape[0]
    vectors = None
    for slot, block in enumerate(blocks):
        plane = slot ^ place_ref[2]
        more = pltpu.roll(block[rows:, :].astype(f32), 3 * plane, 0)
        vectors = more if vectors is None else vectors + more

        @pl.when(plane < 3)
        def _():
            qkv_ref[pl.ds(pl.multiple_of(plane * rows, 16), rows), :] = block[:rows, :]

        @pl.when(plane == 3)
        def _():
            out_ref[...] = block[:rows, :]

    qkv_ref[3 * rows :, :] = vectors.astype(bf16)


def attn_stack(place, blocks, deps):
    rows, width = blocks[0].shape
    rows -= 16
    return pl.pallas_call(
        attn_stack_kernel,
        in_specs=[SMEM] + [pl.BlockSpec(memory_space=pltpu.VMEM)] * 4 + [ANY] * len(deps),
        out_specs=[pl.BlockSpec(memory_space=pltpu.VMEM)] * 2,
        out_shape=[SDS((3 * rows + 16, width), bf16), SDS((rows, width), bf16)],
        compiler_params=params(),
        cost_estimate=cost(1e6, 1e6),
        name="attention_weight_order",
    )(place, *blocks, *deps)


def stack_kernel(place_ref, *refs, which, extra):
    blocks, out_ref = refs[:4], refs[-1]
    rows = blocks[0].shape[0]
    for slot, block in enumerate(blocks):
        at = pl.multiple_of((slot ^ place_ref[which]) * rows, 16)
        out_ref[pl.ds(at, rows), :] = block[...]
    if extra:
        out_ref[4 * rows :, :] = refs[4][...]


def stack(place, blocks, which, *extra, deps=()):
    rows, width = blocks[0].shape
    return pl.pallas_call(
        functools.partial(stack_kernel, which=which, extra=len(extra)),
        in_specs=[SMEM] + [pl.BlockSpec(memory_space=pltpu.VMEM)] * (4 + len(extra)) + [ANY] * len(deps),
        out_specs=pl.BlockSpec(memory_space=pltpu.VMEM),
        out_shape=SDS((rows * (4 + len(extra)), width), bf16),
        compiler_params=params(),
        cost_estimate=cost(1e6, 1e6),
        name="weight_order",
    )(place, *blocks, *extra, *deps)


def attn_fwd_kernel(place_ref, len_ref, scale_ref, *refs, block, count, deps):
    pieces = refs[:count]
    refs = refs[:count] + refs[count + deps :]
    x_ref, q_ref, k_ref, v_ref, c_ref, lse_ref, vec_ref, w_ref, packed, sems, vec_sems = refs[count:]
    rows, width = q_ref.shape
    total_width = x_ref.shape[1]
    group = pl.program_id(0)
    weights = block_copies(place_ref, pieces, range(3), w_ref, sems)

    @pl.when(group == 0)
    def _():
        top = pieces[0].shape[0] - 16
        vec_copies = [
            pltpu.make_async_copy(piece.at[top : top + 16], packed.at[index], vec_sems.at[index])
            for index, piece in enumerate(pieces)
        ]
        for copy in vec_copies:
            copy.start()
        start_all(weights)
        for copy in vec_copies:
            copy.wait()
        vectors = None
        for index in range(count):
            shift = piece_row(place_ref, index, count) * (total_width // count)
            more = packed[index].astype(f32)
            more = more if count == 1 else pltpu.roll(more, shift, 1)
            vectors = more if vectors is None else vectors + more
        vec_ref[...] = vectors
        wait_all(weights)

    x = x_ref[...]
    cols = pl.ds(pl.multiple_of(group * width, 128), width)
    for index, out in enumerate((q_ref, k_ref, v_ref)):
        part = w_ref[:, pl.ds(pl.multiple_of(index * total_width + group * width, 128), width)]
        value = dot(x, part) * scale_ref[index]
        if index != 1:
            value = value + vec_ref[index // 2 : index // 2 + 1, cols]
        out[...] = value.astype(bf16)
    lane = lax.broadcasted_iota(jnp.int32, (1, 128), 1)

    def run(span):
        step = min(block, span)
        for pair in range(width // 128):
            cols = pl.ds(pair * 128, 128)
            for start in range(0, rows, step):
                low = start // span * span
                q_rows = q_ref[start : start + step, cols]
                k_rows = k_ref[low : low + span, cols]
                v_rows = v_ref[low : low + span, cols]
                found = []
                for head in range(2):
                    own = (lane < 64) if head == 0 else (lane >= 64)
                    q_own = jnp.where(own, q_rows, jnp.zeros_like(q_rows)) * jnp.asarray(0.125, bf16)
                    v_ones = jnp.where(own, v_rows, jnp.ones_like(v_rows))
                    scores = dot_last(q_own, k_rows)
                    top = jnp.max(scores, axis=1, keepdims=True)
                    found.append((dot(jnp.exp(scores - top).astype(bf16), v_ones), top))
                (out_a, top_a), (out_b, top_b) = found
                value = jnp.where(lane < 64, out_a, out_b)
                total = jnp.where(lane < 64, pltpu.roll(out_a, 64, 1), pltpu.roll(out_b, 64, 1))
                c_ref[start : start + step, cols] = (value / total).astype(bf16)
                lse_ref[start : start + step, cols] = jnp.where(lane < 64, top_a, top_b) + jnp.log(total)

    two = len_ref[0] < rows

    @pl.when(two)
    def _():
        run(rows // 2)

    @pl.when(jnp.logical_not(two))
    def _():
        run(rows)


def attn_fwd(place, lengths, scales, pieces, x, deps):
    rows, width = x.shape
    group = 256
    count = len(pieces)
    cols = pl.BlockSpec((rows, group), lambda g: (0, g))
    return pl.pallas_call(
        functools.partial(attn_fwd_kernel, block=512, count=count, deps=len(deps)),
        grid=(width // group,),
        in_specs=[SMEM] * 3 + [ANY] * (count + len(deps)) + [pl.BlockSpec((rows, width), lambda g: (0, 0))],
        out_specs=[cols] * 5 + [pl.BlockSpec((16, width), lambda g: (0, 0))],
        out_shape=[SDS((rows, width), bf16)] * 4 + [SDS((rows, width), f32), SDS((16, width), f32)],
        scratch_shapes=[pltpu.VMEM((width, 3 * width), bf16), pltpu.VMEM((count, 16, width), bf16),
                        pltpu.SemaphoreType.DMA((3 * count,)), pltpu.SemaphoreType.DMA((count,))],
        compiler_params=params(),
        cost_estimate=cost(20e9, 12e6, 12e6),
        name="attention_forward",
    )(place, lengths, scales, *pieces, *deps, x)


def order_rows(place_ref, source_t, dest):
    cores = dest.shape[0]
    if cores == 1:
        dest[0] = source_t
        return
    blocks = 8
    size = source_t.shape[0] // blocks
    for block in range(blocks):
        at = pl.multiple_of(((block // 2) ^ place_ref[1]) * size, 16)
        dest[(block % 2) ^ place_ref[0], pl.ds(at, size), :] = source_t[block * size : (block + 1) * size]


def turn_kernel(place_ref, source_ref, out_ref):
    order_rows(place_ref, source_ref[...].T, out_ref)


def turn(place, source, cores):
    rows, width = source.shape
    vmem = pl.BlockSpec(memory_space=pltpu.VMEM)
    return pl.pallas_call(
        turn_kernel,
        in_specs=[SMEM, vmem],
        out_specs=vmem,
        out_shape=SDS((cores, width // cores, rows), bf16),
        compiler_params=params(),
        cost_estimate=cost(1e6, 3e6),
        name="turn",
    )(place, source)


def attn_bwd_kernel(
    place_ref, len_ref, q_ref, k_ref, v_ref, dc_ref, c_ref, lse_ref, x_hbm, c_hbm, dh_ref, *refs, block, cores, last, shard_first, deps,
):
    refs = refs[deps:]
    if last:
        before_a_ref, before_b_ref, vg_first_ref, vg_second_ref, b1g_ref, *refs = refs
    grads = refs[:cores]
    dqkv_ref, sum_ref, dk_acc, dv_acc, dq_acc, x_t, c_t, sems = refs[cores:]
    rows = q_ref.shape[0]
    pair = pl.program_id(0)
    pairs = pl.num_programs(0)
    span_cols = dqkv_ref.shape[1] // 3
    total_width = x_t.shape[0] * x_t.shape[1]
    lane = lax.broadcasted_iota(jnp.int32, (1, 128), 1)
    masks = [lane < 64, lane >= 64]

    turned_copies = [
        pltpu.make_async_copy(x_hbm, x_t, sems.at[0]),
        pltpu.make_async_copy(c_hbm, c_t, sems.at[1]),
    ]

    @pl.when(pair == 0)
    def _():
        for copy in turned_copies:
            copy.start()

    prod = (dc_ref[...].astype(f32) * c_ref[...].astype(f32)).T
    row_dots = [col_sum(prod[:64]), col_sum(prod[64:])]
    lse = lse_ref[...].T
    lse_rows = [lse[0:1], lse[64:65]]

    def run(span):
        step = min(block, span)
        for low in range(0, rows, span):
            k_rows = k_ref[low : low + span, :]
            v_rows = v_ref[low : low + span, :]
            k_cols = k_rows.astype(f32).T.astype(bf16)
            for start in range(low, low + span, step):
                q_rows = q_ref[start : start + step, :]
                dc_rows = dc_ref[start : start + step, :]
                probs, d_scores, q_own, dc_own, dq_parts = [], [], [], [], []
                for head in range(2):
                    q_head = jnp.where(masks[head], q_rows, jnp.zeros_like(q_rows)) * jnp.asarray(0.125, bf16)
                    dc_head = jnp.where(masks[head], dc_rows, jnp.zeros_like(dc_rows))
                    prob = jnp.exp(dot_last(k_rows, q_head) - lse_rows[head][:, start : start + step])
                    d_prob = dot_last(v_rows, dc_head)
                    d_score = (prob * (d_prob - row_dots[head][:, start : start + step])).astype(bf16)
                    probs.append(prob.astype(bf16))
                    d_scores.append(d_score)
                    q_own.append(q_head)
                    dc_own.append(dc_head)
                    dq_parts.append(dot(k_cols[head * 64 : head * 64 + 64], d_score))
                dq_acc[:, start : start + step] = jnp.concatenate(dq_parts, axis=0)
                dv = dot(jnp.concatenate(probs, axis=1), jnp.concatenate(dc_own, axis=0))
                dk = dot(jnp.concatenate(d_scores, axis=1), jnp.concatenate(q_own, axis=0))
                if start == low:
                    dv_acc[low : low + span, :] = dv
                    dk_acc[low : low + span, :] = dk
                else:
                    dv_acc[low : low + span, :] += dv
                    dk_acc[low : low + span, :] += dk

    two = len_ref[0] < rows

    @pl.when(two)
    def _():
        run(rows // 2)

    @pl.when(jnp.logical_not(two))
    def _():
        run(rows)

    dq = dq_acc[...].T * 0.125

    def put(part, value):
        at = pl.multiple_of(part * span_cols + pair * 128, 128)
        dqkv_ref[:, pl.ds(at, 128)] = value.astype(bf16)

    put(0, dq)
    put(1, dk_acc[...])
    put(2, dv_acc[...])
    low = before_a_ref.shape[1] if last else 0
    here = pl.ds(pl.multiple_of(low + pair * 128, 128), 128)
    if last:
        @pl.when(pair == 0)
        def _():
            sum_ref[0:2, : before_a_ref.shape[1]] = before_a_ref[0:2, :]
            sum_ref[0:2, low + span_cols :] = before_b_ref[0:2, :]
            sum_ref[2:5, :] = vg_first_ref[2:5, :]
            sum_ref[5:8, :] = vg_second_ref[5:8, :]
            for row in range(b1g_ref.shape[1] // total_width):
                sum_ref[8 + row : 9 + row, :] = b1g_ref[0:1, row * total_width : (row + 1) * total_width]

    sum_ref[0:1, here] = col_sum(dq)
    sum_ref[1:2, here] = col_sum(dv_acc[...])

    @pl.when(pair == pairs - 1)
    def _():
        for copy in turned_copies:
            copy.wait()
        for core in reversed(range(cores)):
            out = grads[core]
            spots = out.shape[1 if shard_first else 0]
            size = x_t.shape[1] // spots
            for plane in range(4):
                left = x_t if plane < 3 else c_t
                right = dqkv_ref[:, plane * span_cols : (plane + 1) * span_cols] if plane < 3 else dh_ref[...]
                value = dot(left[core], right).astype(bf16)
                if shard_first:
                    out[plane] = value.reshape(spots, size, span_cols)
                else:
                    out[:, pl.ds(plane ^ place_ref[2], 1), :size] = value.reshape(spots, 1, size, span_cols)
        if last and cores == 2:
            row = lax.broadcasted_iota(jnp.int32, (16, span_cols), 0)
            col = lax.broadcasted_iota(jnp.int32, (16, span_cols), 1)
            kept = (row < 3) & (col < size)
            even = place_ref[0] == 0
            for plane in range(4):
                rows_here = sum_ref[...] if plane == 0 else pltpu.roll(sum_ref[...], 16 - 3 * plane, 0)
                for spot in range(4):
                    tiles = []
                    for core in range(2):
                        start = (2 * spot + core) * size
                        turned = rows_here if start == 0 else pltpu.roll(rows_here, total_width - start, 1)
                        tiles.append(jnp.where(kept, turned[:, :span_cols], 0.0).astype(bf16))
                    for core in range(2):
                        tile = jnp.where(even, tiles[core], tiles[1 - core])
                        grads[core][spot ^ place_ref[1], plane ^ place_ref[2], size:, :] = tile


def attn_bwd(place, lengths, q, k, v, dc, c, lse, x_turned, c_turned, dh_low, first, pairs, cores, spots, deps, before=None, shard_first=False):
    rows, width = q.shape
    last = before is not None
    size = pairs * 128
    cols = pl.BlockSpec((rows, 128), lambda g: (0, first + g))

    def whole(shape):
        return pl.BlockSpec(shape, lambda g: (0,) * len(shape))

    depth = width // (cores * spots)
    shape = (spots, 4, depth + (16 if last and cores == 2 else 0), size)
    shape = (shape[1], shape[0]) + shape[2:] if shard_first else shape
    sums = (16, width if last else size)
    more = list(before) if last else []
    return pl.pallas_call(
        functools.partial(attn_bwd_kernel, block=512, cores=cores, last=last, shard_first=shard_first, deps=len(deps)),
        grid=(pairs,),
        in_specs=[SMEM] * 2 + [cols] * 6 + [ANY] * 2
        + [pl.BlockSpec((rows, size), lambda g: (0, first // pairs))] + [ANY] * len(deps) + [whole(m.shape) for m in more],
        out_specs=[whole(shape)] * cores + [whole((rows, 3 * size)), whole(sums)],
        out_shape=[SDS(shape, bf16)] * cores + [SDS((rows, 3 * size), bf16), SDS(sums, f32)],
        scratch_shapes=[
            pltpu.VMEM((rows, 128), f32), pltpu.VMEM((rows, 128), f32), pltpu.VMEM((128, rows), f32),
            pltpu.VMEM((cores, width // cores, rows), bf16), pltpu.VMEM((cores, width // cores, rows), bf16),
            pltpu.SemaphoreType.DMA((2,)),
        ],
        compiler_params=params(),
        cost_estimate=cost(50e9 * size / width, 30e6 * size / width, 12e6 * size / width),
        name="attention_backward",
    )(place, lengths, q, k, v, dc, c, lse, x_turned, c_turned, dh_low, *deps, *more)


def mid_fwd_kernel(place_ref, scale_ref, *refs, chunk, count, deps):
    pieces = refs[:count]
    refs = refs[:count] + refs[count + deps :]
    (x_ref, c_ref, vec_ref, n1_ref, r1_ref, y1_ref, a_ref, gp_ref,
     wo_ref, w1_ref, out_sems, up_sems) = refs[count:]
    rows, width = x_ref.shape
    first = pl.program_id(0) == 0
    out_copies = block_copies(place_ref, pieces, [4], wo_ref, out_sems)
    up_copies = block_copies(place_ref, pieces, range(4), w1_ref, up_sems)

    @pl.when(first)
    def _():
        start_all(out_copies)
        start_all(up_copies)
        wait_all(out_copies)

    residual = x_ref[...].astype(f32) + dot(c_ref[...], wo_ref[...]) * scale_ref[3] + vec_ref[2:3]
    normed, inv_std = normalize(residual)
    n1_ref[...] = normed
    r1_ref[...] = jnp.broadcast_to(inv_std, (rows, 128))
    y1 = (normed * vec_ref[3:4] + vec_ref[4:5]).astype(bf16)
    y1_ref[...] = y1

    @pl.when(first)
    def _():
        wait_all(up_copies)

    for start in range(0, w1_ref.shape[1], chunk):
        block, at = divmod(start, width)
        cols = slice(start, start + chunk)
        bias = vec_ref[8 + block : 9 + block, at : at + chunk]
        u = dot(y1, w1_ref[:, cols]) * scale_ref[4] + bias
        square = u * u
        half = 0.5 + 0.5 * jnp.tanh(u * (GELU_K + (GELU_K * GELU_C) * square))
        act = u * half
        a_ref[:, cols] = act.astype(bf16)
        gp_ref[:, cols] = (half + act * (1.0 - half) * (2 * GELU_K + (6 * GELU_K * GELU_C) * square)).astype(bf16)


def mid_fwd(place, scales, pieces, x, c, vec, deps):
    rows, width = x.shape
    hidden = 4 * pieces[0].shape[1]
    tile = 512
    count = len(pieces)

    def row(size):
        return pl.BlockSpec((tile, size), lambda i: (i, 0))

    def full(arr):
        return pl.BlockSpec(arr.shape, lambda i: (0, 0))

    return pl.pallas_call(
        functools.partial(mid_fwd_kernel, chunk=256, count=count, deps=len(deps)),
        grid=(rows // tile,),
        in_specs=[SMEM] * 2 + [ANY] * (count + len(deps)) + [row(width), row(width), full(vec)],
        out_specs=[row(width), row(128), row(width), row(hidden), row(hidden)],
        out_shape=[SDS((rows, width), f32), SDS((rows, 128), f32), SDS((rows, width), bf16),
                   SDS((rows, hidden), bf16), SDS((rows, hidden), bf16)],
        scratch_shapes=[pltpu.VMEM((width, width), bf16), pltpu.VMEM((width, hidden), bf16),
                        pltpu.SemaphoreType.DMA((count,)), pltpu.SemaphoreType.DMA((4 * count,))],
        compiler_params=params(),
        cost_estimate=cost(12e9, 25e6, 3e6),
        name="middle_forward",
    )(place, scales, *pieces, *deps, x, c, vec)


def second_norm_kernel(place_ref, scale_ref, *refs, cores, tiles):
    downs = refs[:cores]
    (act_ref, n1_ref, do_ref, vec_ref, out_ref, dz_ref, dzb_ref, vg_ref, grad_ref,
     w2_ref, act, dz_all, left_t, down_sems, act_sems) = refs[cores:]
    step = pl.program_id(0)
    tile = n1_ref.shape[0]

    def act_copy(index):
        rows = pl.ds(pl.multiple_of(index * tile, tile), tile)
        return pltpu.make_async_copy(act_ref.at[rows], act.at[rows], act_sems.at[index])

    copies = down_copies(place_ref, downs, w2_ref, down_sems)
    spots = downs[0].shape[1]
    size = w2_ref.shape[1] // spots

    def body(arriving):
        if arriving:
            act_copy(0).start()
            start_all(copies)
            for index in range(1, tiles):
                act_copy(index).start()
            vg_ref[...] = jnp.zeros_like(vg_ref)
        act_copy(step).wait()
        rows = pl.ds(pl.multiple_of(step * tile, tile), tile)
        g1, c1, b2, g2, c2 = [vec_ref[i : i + 1] for i in range(3, 8)]
        if arriving:
            product = None
            for spot in range(spots):
                wait_all(some_copies(copies, spot, spots))
                cols = slice(spot * size, (spot + 1) * size)
                more = dot_last(act[rows, cols], w2_ref[:, cols])
                product = more if product is None else product + more
        else:
            product = dot_last(act[rows, :], w2_ref[...])
        residual = n1_ref[...] * g1 + c1 + product * scale_ref[5] + b2
        n2, r2 = normalize(residual)
        out_ref[...] = (n2 * g2 + c2).astype(bf16)
        d_out = do_ref[...].astype(f32)
        vg_ref[6:7] += col_sum(d_out * n2)
        vg_ref[7:8] += col_sum(d_out)
        dz = normalize_back(d_out * g2, n2, r2)
        vg_ref[5:6] += col_sum(dz)
        dz_ref[...] = dz
        dz_low = dz.astype(bf16)
        dzb_ref[...] = dz_low
        dz_all[rows, :] = dz_low

    @pl.when(step == 0)
    def _():
        body(True)

    @pl.when((step > 0) & (step < tiles))
    def _():
        body(False)

    @pl.when(step == tiles)
    def _():
        left_t[...] = dz_all[...].T

    @pl.when(step >= tiles)
    def _():
        blocks, slots, size, cols = grad_ref.shape
        wide = blocks * cols
        start = pl.multiple_of((step - tiles) * wide, 128)
        value = dot(left_t[...], act[:, pl.ds(start, wide)]).astype(bf16)
        for block in range(blocks):
            grad_ref[block] = value[:, block * cols : (block + 1) * cols].reshape(slots, size, cols)


def second_norm(place, scales, downs, n1, act, d_out, vec, blocks):
    rows, width = n1.shape
    hidden = act.shape[1]
    tile = 256
    tiles = rows // tile
    some = min(2, blocks)
    block = (some, 4, width // 4, hidden // blocks)

    def row(size):
        return pl.BlockSpec((tile, size), lambda i: (jnp.minimum(i, tiles - 1), 0))

    return pl.pallas_call(
        functools.partial(second_norm_kernel, cores=len(downs), tiles=tiles),
        grid=(tiles + blocks // some,),
        in_specs=[SMEM] * 2 + [ANY] * (len(downs) + 1)
        + [row(width), row(width), pl.BlockSpec(vec.shape, lambda i: (0, 0))],
        out_specs=[row(width)] * 3 + [pl.BlockSpec((8, width), lambda i: (0, 0)),
                                      pl.BlockSpec(block, lambda i: (jnp.maximum(i - tiles, 0), 0, 0, 0))],
        out_shape=[SDS((rows, width), bf16), SDS((rows, width), f32), SDS((rows, width), bf16), SDS((8, width), f32),
                   SDS((blocks,) + block[1:], bf16)],
        scratch_shapes=[pltpu.VMEM((width, hidden), bf16), pltpu.VMEM((rows, hidden), bf16),
                        pltpu.VMEM((rows, width), bf16), pltpu.VMEM((width, rows), bf16),
                        pltpu.SemaphoreType.DMA((4 * downs[0].shape[1] * len(downs),)),
                        pltpu.SemaphoreType.DMA((tiles,))],
        compiler_params=params(),
        cost_estimate=cost(16e9, 30e6),
        name="second_norm",
    )(place, scales, *downs, act, n1, d_out, vec)


def mid_bwd_kernel(place_ref, scale_ref, *refs, chunk, count, cores, outs, tiles, deps):
    downs, pieces, refs = refs[:cores], refs[cores : cores + count], refs[cores + count + deps :]
    y1_hbm, n1_ref, r1_ref, gp_ref, dz_ref, dzb_ref, vec_ref = refs[:7]
    dh_ref, dhb_ref, dc_ref, vg_ref, b1g_ref = refs[7:12]
    grads = refs[12 : 12 + outs]
    wo_ref, w1_ref, w2_ref, du_all, y1, left_t, out_sems, up_sems, down_sems, y1_sem = refs[12 + outs :]
    step = pl.program_id(0)
    tile, width = n1_ref.shape
    first = step == 0
    y1_copy = pltpu.make_async_copy(y1_hbm, y1, y1_sem.at[0])

    w2_copies = down_copies(place_ref, downs, w2_ref, down_sems)
    w1_copies = block_copies(place_ref, pieces, range(4), w1_ref, up_sems)
    wo_copies = block_copies(place_ref, pieces, [4], wo_ref, out_sems)
    spots = downs[0].shape[1]

    def body(arriving):
        if arriving:
            start_all(w2_copies)
            start_all(w1_copies)
            start_all(wo_copies)
            y1_copy.start()
            vg_ref[...] = jnp.zeros_like(vg_ref)
            b1g_ref[...] = jnp.zeros_like(b1g_ref)
        rows = pl.ds(pl.multiple_of(step * tile, tile), tile)
        g1 = vec_ref[3:4]
        n1 = n1_ref[...]
        dz_low = dzb_ref[...]
        for start in range(0, w1_ref.shape[1], chunk):
            spot, rest = divmod(start * spots, w1_ref.shape[1])
            if arriving and rest == 0:
                wait_all(some_copies(w2_copies, spot, spots))
            cols = slice(start, start + chunk)
            du = dot(dz_low, w2_ref[:, cols]) * scale_ref[5] * gp_ref[:, cols].astype(f32)
            b1g_ref[0:1, cols] += col_sum(du)
            du_all[rows, cols] = du.astype(bf16)
        if arriving:
            wait_all(w1_copies)
            wait_all(wo_copies)
        dy = dz_ref[...] + dot_last(du_all[rows, :], w1_ref[...]) * scale_ref[4]
        vg_ref[3:4] += col_sum(dy * n1)
        vg_ref[4:5] += col_sum(dy)
        dh = normalize_back(dy * g1, n1, r1_ref[:, 0:1])
        vg_ref[2:3] += col_sum(dh)
        dh_ref[...] = dh
        dh_low = dh.astype(bf16)
        dhb_ref[...] = dh_low
        dc_ref[...] = (dot_last(dh_low, wo_ref[...]) * scale_ref[3]).astype(bf16)

    @pl.when(first)
    def _():
        body(True)

    @pl.when((step > 0) & (step < tiles))
    def _():
        body(False)

    @pl.when(step == tiles)
    def _():
        y1_copy.wait()
        order_rows(place_ref, y1[...].T, left_t)

    @pl.when(step >= tiles)
    def _():
        cols = pl.ds(pl.multiple_of((step - tiles) * width, 128), width)
        for core in reversed(range(outs)):
            grads[core][...] = dot(left_t[core], du_all[:, cols]).astype(bf16).reshape(grads[core].shape)


def mid_bwd(place, scales, pieces, downs, n1, r1, y1, gelu_grad, dz, dz_low, vec, cores, spots, deps):
    rows, width = n1.shape
    hidden = gelu_grad.shape[1]
    tile = 256
    tiles = rows // tile
    count = len(pieces)
    block = (spots, 1, width // (cores * spots), width)

    def row(size):
        return pl.BlockSpec((tile, size), lambda i: (jnp.minimum(i, tiles - 1), 0))

    def whole(shape):
        return pl.BlockSpec(shape, lambda i: (0,) * len(shape))

    return pl.pallas_call(
        functools.partial(
            mid_bwd_kernel, chunk=256, count=count, cores=len(downs), outs=cores, tiles=tiles, deps=len(deps)
        ),
        grid=(tiles + 4,),
        in_specs=[SMEM] * 2 + [ANY] * (count + len(downs) + len(deps) + 1)
        + [row(width), row(128), row(hidden), row(width), row(width), whole(vec.shape)],
        out_specs=[row(width), row(width), row(width), whole((8, width)), whole((8, hidden))]
        + [pl.BlockSpec(block, lambda i: (0, jnp.maximum(i - tiles, 0), 0, 0))] * cores,
        out_shape=[SDS((rows, width), f32), SDS((rows, width), bf16), SDS((rows, width), bf16),
                   SDS((8, width), f32), SDS((8, hidden), f32)]
        + [SDS((spots, 4) + block[2:], bf16)] * cores,
        scratch_shapes=[pltpu.VMEM((width, width), bf16), pltpu.VMEM((width, hidden), bf16),
                        pltpu.VMEM((width, hidden), bf16), pltpu.VMEM((rows, hidden), bf16),
                        pltpu.VMEM((rows, width), bf16), pltpu.VMEM((cores, width // cores, rows), bf16),
                        pltpu.SemaphoreType.DMA((count,)), pltpu.SemaphoreType.DMA((4 * count,)),
                        pltpu.SemaphoreType.DMA((4 * downs[0].shape[1] * len(downs),)),
                        pltpu.SemaphoreType.DMA((1,))],
        compiler_params=params(),
        cost_estimate=cost(28e9, 40e6),
        name="middle_backward",
    )(place, scales, *downs, *pieces, *deps, y1, n1, r1, gelu_grad, dz, dz_low, vec)


def input_grad_kernel(place_ref, scale_ref, *refs, count, chunks, deps):
    pieces = refs[:count]
    parts = refs[count : count + chunks]
    dh_ref, out_ref, w_ref, sems = refs[count + chunks + deps :]
    width = dh_ref.shape[1]

    @pl.when(pl.program_id(0) == 0)
    def _():
        copies = block_copies(place_ref, pieces, range(3), w_ref, sems)
        start_all(copies)
        wait_all(copies)

    total = dh_ref[...]
    for plane in range(3):
        product = None
        start = plane * width
        for part in parts:
            size = part.shape[1] // 3
            more = dot_last(part[:, plane * size : (plane + 1) * size], w_ref[:, start : start + size])
            product = more if product is None else product + more
            start += size
        total = total + product * scale_ref[plane]
    out_ref[...] = total.astype(bf16)


def input_grad(place, scales, pieces, parts, dh, deps):
    rows, width = dh.shape
    tile = 512
    count, chunks = len(pieces), len(parts)

    def row(size):
        return pl.BlockSpec((tile, size), lambda i: (i, 0))

    return pl.pallas_call(
        functools.partial(input_grad_kernel, count=count, chunks=chunks, deps=len(deps)),
        grid=(rows // tile,),
        in_specs=[SMEM] * 2 + [ANY] * count + [row(p.shape[1]) for p in parts] + [ANY] * len(deps) + [row(width)],
        out_specs=row(width),
        out_shape=SDS((rows, width), bf16),
        scratch_shapes=[pltpu.VMEM((width, 3 * width), bf16), pltpu.SemaphoreType.DMA((3 * count,))],
        compiler_params=params(),
        cost_estimate=cost(9e9, 2 * (rows * width * 6 + 3 * width * width)),
        name="input_gradient",
    )(place, scales, *pieces, *parts, *deps, dh)


def swap(value, axis, mask):
    count = lax.axis_size(axis)
    return lax.ppermute(value, axis, [(i, i ^ mask) for i in range(count)])


def bits(axis):
    return [1 << b for b in range(lax.axis_size(axis).bit_length() - 1)]


def doubling_gather(value, axis, dim):
    index = lax.axis_index(axis)
    for bit in bits(axis):
        other = swap(value, axis, bit)
        high = (index & bit) != 0
        value = jnp.concatenate(
            [jnp.where(high, other, value), jnp.where(high, value, other)], axis=dim
        )
    return value


def doubling_sum(value):
    for axis in ("dp", "shard"):
        for bit in bits(axis):
            value = value + swap(value, axis, bit)
    return value


def total_sum(value):
    value = value + swap(value, "dp", 1)
    for axis, masks in (("dp", (6, 4, 2)), ("shard", (3, 2, 1))):
        others = [swap(value, axis, mask) for mask in masks]
        value = (value + others[0]) + (others[1] + others[2])
    return value


def four(block, axis, unit):
    return [block] + [swap(block, axis, unit * m) for m in (1, 2, 3)]


def core_sum_kernel(*refs, sizes, deps):
    count = len(sizes)
    outs = refs[2 * count + deps :]
    at = 0
    for index, (depth, width) in enumerate(sizes):
        mine, got = refs[2 * index : 2 * index + 2]
        for spot, out in enumerate(outs):
            out[:, :depth, at : at + width] = mine[spot] + got[spot]
            if depth < out.shape[1]:
                rest = (out.shape[0], out.shape[1] - depth, width)
                out[:, depth:, at : at + width] = jnp.zeros(rest, bf16)
        at += width


def core_sum(pairs, deps=()):
    spots, slots = pairs[0][0].shape[:2]
    sizes = [mine.shape[2:] for mine, _ in pairs]
    rows, width = max(s[0] for s in sizes), sum(s[1] for s in sizes)
    specs = []
    for depth, wide in sizes:
        specs += [pl.BlockSpec((spots, 2, depth, wide), lambda i: (0, i, 0, 0))] * 2
    return pl.pallas_call(
        functools.partial(core_sum_kernel, sizes=sizes, deps=len(deps)),
        grid=(slots // 2,),
        in_specs=specs + [ANY] * len(deps),
        out_specs=[pl.BlockSpec((2, rows, width), lambda i: (i, 0, 0))] * spots,
        out_shape=[SDS((slots, rows, width), bf16)] * spots,
        compiler_params=params(),
        cost_estimate=cost(1e6, 6 * spots * slots * rows * width),
        name="core_sum",
    )(*[part for pair in pairs for part in pair], *deps)


def pair_sum_kernel(mine_ref, got_ref, *refs):
    refs[-1][...] = mine_ref[...] + got_ref[...]


def pair_sum(mine, got, deps=()):
    block = pl.BlockSpec((2,) + mine.shape[1:], lambda i: (i, 0, 0, 0))
    return pl.pallas_call(
        pair_sum_kernel,
        grid=(mine.shape[0] // 2,),
        in_specs=[block, block] + [ANY] * len(deps),
        out_specs=block,
        out_shape=SDS(mine.shape, bf16),
        compiler_params=params(),
        cost_estimate=cost(1e6, 6 * mine.size),
        name="pair_sum",
    )(mine, got, *deps)


def plane_sum_kernel(*refs, count, deps):
    outs = refs[4 * count + deps :]
    at = 0
    for index in range(count):
        parts = refs[4 * index : 4 * index + 4]
        depth, width = parts[0].shape[1:]
        for slot in range(parts[0].shape[0]):
            total = parts[0][slot].astype(f32) + parts[1][slot].astype(f32)
            total = total + (parts[2][slot].astype(f32) + parts[3][slot].astype(f32))
            out = outs[0].at[slot] if len(outs) == 1 else outs[slot]
            out[:depth, at : at + width] = total.astype(out.dtype)
            if depth < out.shape[0]:
                out[depth:, at : at + width] = jnp.zeros((out.shape[0] - depth, width), out.dtype)
        at += width


def plane_sum(groups, split, deps=()):
    slots = groups[0][0].shape[0]
    rows = max(parts[0].shape[1] for parts in groups)
    width = sum(parts[0].shape[2] for parts in groups)
    vmem = pl.BlockSpec(memory_space=pltpu.VMEM)
    shapes = [SDS((rows, width), f32)] + [SDS((rows, width), bf16)] * (slots - 1)
    if not split:
        shapes = [SDS((slots, rows, width), bf16)]
    return pl.pallas_call(
        functools.partial(plane_sum_kernel, count=len(groups), deps=len(deps)),
        in_specs=[vmem] * (4 * len(groups)) + [ANY] * len(deps),
        out_specs=[vmem] * len(shapes),
        out_shape=shapes,
        compiler_params=params(),
        cost_estimate=cost(1e6, 4 * slots * rows * width),
        name="plane_sum",
    )(*[part for parts in groups for part in parts], *deps)


def exchange(parts, axis, unit):
    return [parts[0]] + [swap(parts[m], axis, unit * m) for m in (1, 2, 3)]


def after(value, *others):
    return lax.optimization_barrier((value,) + others)[0]

def adam_update(gradient, master, first_old, second_old, average, step_rate, decay_rate):
    first_new = beta_first * first_old + (1.0 - beta_first) * gradient
    second_new = beta_second * second_old + (1.0 - beta_second) * gradient * gradient
    first_hat = first_new / (1.0 - beta_first**STEP)
    second_hat = second_new / (1.0 - beta_second**STEP)
    master_new = master - step_rate * (
        first_hat / (jnp.sqrt(second_hat) + adam_eps) + decay_rate * master
    )
    average_new = average_keep * average + (1.0 - average_keep) * master_new
    return (first_new, second_new, master_new, average_new)


def own_sums_kernel(*refs):
    firsts, lasts, (up_ref, down_ref, attn_ref, vec_ref, square_ref) = refs[:4], refs[4:8], refs[8:]
    rows = attn_ref.shape[0]
    first, last = [
        (parts[0][...].astype(f32) + parts[1][...].astype(f32)) + (parts[2][...].astype(f32) + parts[3][...].astype(f32))
        for parts in (firsts, lasts)
    ]
    attn_ref[:, : first.shape[1]] = first
    attn_ref[:, first.shape[1] :] = last[:rows]
    at = 0
    vec_ref[...] = last[rows:, at : at + 128]
    total = jnp.sum(first * first) + jnp.sum(last * last)
    for ref in (up_ref, down_ref):
        value = ref[...].astype(f32)
        total = total + jnp.sum(value * value)
    square_ref[...] = jnp.full(square_ref.shape, total, f32)


def own_sums(firsts, lasts, own_up, own_down):
    vmem = pl.BlockSpec(memory_space=pltpu.VMEM)
    rows, width = firsts[0].shape[0], firsts[0].shape[1] + lasts[0].shape[1]
    return pl.pallas_call(
        own_sums_kernel,
        in_specs=[vmem] * 10,
        out_specs=[vmem] * 3,
        out_shape=[SDS((rows, width), f32), SDS((16, 128), f32), SDS((8, 128), f32)],
        compiler_params=params(),
        cost_estimate=cost(1e6, 2e6),
        name="own_sums",
    )(*firsts, *lasts, own_up, own_down)


def update_kernel(square_ref, attn_ref, up_ref, down_ref, vec_ref, *refs):
    states, news, norm_ref = refs[:16], refs[16:32], refs[32]
    norm = jnp.sqrt(square_ref[...])
    norm_ref[0, 0] = jnp.max(norm)
    factor = jnp.minimum(1.0, clip_limit / (norm + norm_eps))[0:1, 0:1]
    rows, cols = states[12].shape
    grads = (
        attn_ref[...],
        up_ref[...].astype(f32),
        down_ref[...].astype(f32),
        vec_ref[:rows, :cols],
    )
    for index, grad in enumerate(grads):
        rates = (vector_rate, 0.0) if index == 3 else (matrix_rate, matrix_decay)
        old = [ref[...] for ref in states[4 * index : 4 * index + 4]]
        for ref, new in zip(news[4 * index : 4 * index + 4], adam_update(grad * factor, *old, *rates)):
            ref[...] = new


def update(squares, own_attn, own_up, own_down, own_vector, states):
    vmem = pl.BlockSpec(memory_space=pltpu.VMEM)
    states = list(states[:8]) + [state.T for state in states[8:]]
    *news, norm = pl.pallas_call(
        update_kernel,
        in_specs=[vmem] * 21,
        out_specs=[vmem] * 16 + [SMEM],
        out_shape=[SDS(state.shape, f32) for state in states] + [SDS((1, 1), f32)],
        compiler_params=params(),
        cost_estimate=cost(1e7, 8e6),
        name="state_update",
    )(squares, own_attn, own_up, own_down, own_vector, *states)
    return news[:8] + [new.T for new in news[8:]], norm


def on_device(
    tokens, out_grad, first_lengths, quant_scales, attn_quant, up_quant, down_quant,
    attn_master, attn_first, attn_second, attn_average,
    up_master, up_first, up_second, up_average,
    down_master, down_first, down_second, down_average,
    vector_master, vector_first, vector_second, vector_average,
):
    width = tokens.shape[1]
    dp_index, shard_index = lax.axis_index("dp"), lax.axis_index("shard")
    small = lax.axis_size("dp") == 8 and lax.axis_size("shard") == 4 and attn_quant.shape == (96, 768)
    gather = functools.partial(lax.all_gather, tiled=True)
    scatter = functools.partial(lax.psum_scatter, tiled=True)
    down_turned = down_quant.T
    vector_low = vector_master.astype(bf16)
    if small:
        cores, spots = 2, 4
        place = jnp.stack([dp_index & 1, dp_index >> 1, shard_index]).astype(jnp.int32)
        packed = jnp.pad(vector_low.T, ((0, 13), (0, width - 96)))
        blocks = four(jnp.concatenate([attn_quant, packed]), "shard", 1)
        x_turned = turn(place, tokens, cores)
        qkv, w_out = attn_stack(place, blocks, [x_turned])
        pieces = four(qkv, "dp", 2)
        up_blocks = four(after(up_quant, qkv), "shard", 1)
        down = after(lax.all_gather(down_turned, "dp"), pieces[1]).reshape(4, 2, 192, -1)
        down = lax.dynamic_index_in_dim(down, dp_index & 1, 1, keepdims=False)
        half = down
        down = lax.all_gather(after(down, *pieces[1:], *up_blocks), "shard")
        up = stack(place, up_blocks, 2, w_out, deps=pieces[1:2])
        ups = four(up, "dp", 2)
        pieces = pieces + [swap(after(piece, up, half), "dp", 1) for piece in pieces]
        early = [up]
    else:
        cores, spots = 1, 1
        place = jnp.zeros((3,), jnp.int32)
        x_turned = turn(place, tokens, cores)
        vec_w = doubling_gather(doubling_gather(vector_low, "shard", 1), "dp", 0)
        attn_w = gather(gather(attn_quant, "shard", axis=1), "dp", axis=0)
        up_w = gather(gather(up_quant, "shard", axis=1), "dp", axis=0)
        down_w = gather(gather(down_turned, "shard", axis=0), "dp", axis=1)
        planes = [attn_w[:, i * width : (i + 1) * width] for i in range(4)]
        pieces = [jnp.concatenate(planes[:3] + [jnp.pad(vec_w.T, ((0, 4), (0, 0)))])]
        ups = [jnp.concatenate([up_w[:, i * width : (i + 1) * width] for i in range(4)] + planes[3:])]
        downs = [down_w.reshape(4, 1, width // 4, -1)]
        early = []

    q, k, v, c, lse, vec = attn_fwd(place, first_lengths, quant_scales, pieces, tokens, early)
    c_turned = turn(place, c, cores)
    if small:
        ups = [ups[0]] + [after(piece, c_turned) for piece in ups[1:]]
        ups = ups + [swap(piece, "dp", 1) for piece in ups]
    n1, r1, y1, act, gelu_grad = mid_fwd(place, quant_scales, ups, tokens, c, vec, [c_turned])
    if small:
        downs = [down, swap(after(down, act), "dp", 1)]
    layer_out, dz, dz_low, vec_second, grad_down = second_norm(
        place, quant_scales, downs, n1, act, out_grad, vec, cores * spots
    )
    dh, dh_low, dc, vec_first, b1_grad, *up_parts = mid_bwd(
        place, quant_scales, ups, downs, n1, r1, y1, gelu_grad, dz, dz_low, vec, cores, spots, [grad_down]
    )
    attn = functools.partial(
        attn_bwd, place, first_lengths, q, k, v, dc, c, lse, x_turned, c_turned, dh_low, cores=cores, spots=spots
    )
    if small:
        own_down = lax.psum_scatter(grad_down, "dp", scatter_dimension=0)
        up_got = swap(up_parts[1], "dp", 1)
        *parts_p, d_p, sums_p = attn(first=4, pairs=2, deps=up_parts[1:])
        up_plane = core_sum([(up_parts[0], up_got)], [d_p])
        got_p = swap(after(parts_p[1], up_plane[0]), "dp", 1)
        up_plane = exchange(up_plane, "dp", 2)
        *parts_q, d_q, sums_q = attn(first=0, pairs=3, deps=up_plane[:1], shard_first=True)
        own_down = lax.psum_scatter(own_down, "shard", scatter_dimension=0)
        (up_shards,) = plane_sum([up_plane], False, [d_q, own_down])
        own_up = lax.psum_scatter(up_shards, "shard", scatter_dimension=0)
        got_q = swap(after(parts_q[1], up_shards), "dp", 1)
        *parts_r, d_r, sums = attn(first=3, pairs=1, deps=[up_shards], before=(sums_q, sums_p, vec_first, vec_second, b1_grad))
        got_r = swap(parts_r[1], "dp", 1)
        sum_q = pair_sum(parts_q[0], got_q, [d_r])
        plane_pr = core_sum([(parts_r[0], got_r), (parts_p[0], got_p)], [sum_q, own_up])
        plane_pr = exchange(plane_pr, "dp", 2)
        spots_q = lax.psum_scatter(sum_q, "shard", scatter_dimension=0)
        spots_q = exchange(after(spots_q, plane_pr[1]), "dp", 2)
        input_gradient = input_grad(place, quant_scales, pieces, [d_q, d_r, d_p], dh, [plane_pr[0]])
        slots_pr = exchange(plane_sum([plane_pr], True, [input_gradient]), "shard", 1)
    else:
        parts_p, d_p, sums_p = attn(first=4, pairs=2, deps=[])
        parts_q, d_q, sums_q = attn(first=0, pairs=3, deps=[])
        parts_r, d_r, sums = attn(first=3, pairs=1, deps=[], before=(sums_q, sums_p, vec_first, vec_second, b1_grad))
        attn_parts = [[parts_q], [parts_r], [parts_p]]
        input_gradient = input_grad(place, quant_scales, pieces, [d_q, d_r, d_p], dh, [])

    rows_own, cols_own = vector_master.shape
    states = (
        attn_master, attn_first, attn_second, attn_average,
        up_master, up_first, up_second, up_average,
        down_master, down_first, down_second, down_average,
        vector_master, vector_first, vector_second, vector_average,
    )
    if small:
        own_attn, own_vector, squares = own_sums(spots_q, slots_pr, own_up, own_down)
        news, grad_norm = update(total_sum(squares), own_attn, own_up, own_down, own_vector, states)
        return (layer_out, input_gradient, grad_norm.reshape(()), *news)
    vec_total = doubling_sum(sums[:12])
    own_vector = lax.dynamic_slice(vec_total, (shard_index * cols_own, dp_index * rows_own), (cols_own, rows_own)).T
    grad_down = grad_down.reshape(width, -1)
    grad_up = up_parts[0][0].transpose(1, 0, 2).reshape(width, -1)
    grad_attn = jnp.concatenate([parts[0][0] for parts in attn_parts], axis=2)
    grad_attn = grad_attn.transpose(1, 0, 2).reshape(width, -1)
    own_down = scatter(scatter(grad_down, "dp", scatter_dimension=1), "shard", scatter_dimension=0).astype(f32).T
    own_up = scatter(scatter(grad_up, "dp", scatter_dimension=0), "shard", scatter_dimension=1).astype(f32)
    own_attn = scatter(scatter(grad_attn, "dp", scatter_dimension=0), "shard", scatter_dimension=1).astype(f32)
    grads = (own_attn, own_up, own_down, own_vector)
    squares = sum(jnp.sum(grad * grad) for grad in grads)
    grad_norm = jnp.sqrt(doubling_sum(jnp.broadcast_to(squares, (8, 128)))[0, 0])
    factor = jnp.minimum(1.0, clip_limit / (grad_norm + norm_eps))
    news = []
    for index, grad in enumerate(grads):
        rates = (vector_rate, 0.0) if index == 3 else (matrix_rate, matrix_decay)
        news += adam_update(grad * factor, *states[4 * index : 4 * index + 4], *rates)
    return (layer_out, input_gradient, grad_norm, *news)


def solution(mesh):
    rows = P(("dp", "shard"), None)
    block = P("dp", "shard")
    in_specs = (rows, rows, P(("dp", "shard")), P()) + (block,) * 19
    out_specs = (rows, rows, P()) + (block,) * 16
    return jax.shard_map(
        on_device, mesh=mesh, in_specs=in_specs, out_specs=out_specs, check_vma=False
    )
```

```python
import functools
import math

import jax
import jax.numpy as jnp
from jax import lax
from jax.experimental import pallas as pl
from jax.experimental.pallas import tpu as pltpu
from jax.sharding import PartitionSpec as P

HEAD_DIM = 64
STEP = 10

norm_eps = 1e-06
clip_limit = 1.0
beta_first = 0.9
beta_second = 0.999
adam_eps = 1e-08
matrix_rate = 0.08
vector_rate = 0.5
matrix_decay = 0.01
average_keep = 0.9

VMEM = 255 * 2**18
GELU_K = math.sqrt(2.0 / math.pi)
GELU_C = 0.044715
f32 = jnp.float32
bf16 = jnp.bfloat16
SDS = jax.ShapeDtypeStruct


def dot(left, right):
    return jnp.dot(left, right, preferred_element_type=f32)


def dot_last(left, right):
    return lax.dot_general(left, right, (((1,), (1,)), ((), ())), preferred_element_type=f32)


def col_sum(value):
    return jnp.sum(value, axis=0, keepdims=True)


def params(**extra):
    return pltpu.CompilerParams(vmem_limit_bytes=VMEM, **extra)


def cost(flops, moved, trans=0):
    return pl.CostEstimate(flops=int(flops), bytes_accessed=int(moved), transcendentals=int(trans))


SMEM = pl.BlockSpec(memory_space=pltpu.SMEM)
ANY = pl.BlockSpec(memory_space=pl.ANY)


def piece_row(place_ref, index, count):
    if count == 1:
        return 0
    half = count // 2
    return ((place_ref[1] ^ (index % half)) * 2) + (place_ref[0] ^ (index // half))


def block_copies(place_ref, pieces, blocks, dest, sems):
    count = len(pieces)
    rows, width = dest.shape[0] // count, pieces[0].shape[1]

    def copy(at, block, index):
        def make():
            row = pl.multiple_of(piece_row(place_ref, index, count) * rows, 16)
            return pltpu.make_async_copy(
                pieces[index].at[block * rows : (block + 1) * rows],
                dest.at[pl.ds(row, rows), at * width : (at + 1) * width],
                sems.at[at * count + index],
            )

        return make

    return [copy(at, block, index) for at, block in enumerate(blocks) for index in range(count)]


def some_copies(copies, part, parts):
    size = len(copies) // parts
    return copies[part * size : (part + 1) * size]


def down_copies(place_ref, sources, dest, sems):
    slots, spots, rows, width = sources[0].shape
    count = len(sources)

    def copy(spot, core, slot):
        def make():
            col = (spot * count + (place_ref[0] ^ core)) * width
            return pltpu.make_async_copy(
                sources[core].at[slot, spot],
                dest.at[slot * rows : (slot + 1) * rows, pl.ds(pl.multiple_of(col, 128), width)],
                sems.at[(spot * count + core) * slots + slot],
            )

        return make

    return [copy(spot, core, slot) for spot in range(spots) for core in range(count) for slot in range(slots)]


def start_all(copies):
    for copy in copies:
        copy().start()


def wait_all(copies):
    for copy in copies:
        copy().wait()


def normalize(value):
    centre = value - jnp.mean(value, axis=-1, keepdims=True)
    inv_std = lax.rsqrt(jnp.mean(centre * centre, axis=-1, keepdims=True) + norm_eps)
    return centre * inv_std, inv_std


def normalize_back(scaled, normed, inv_std):
    return inv_std * (
        scaled
        - jnp.mean(scaled, axis=-1, keepdims=True)
        - normed * jnp.mean(scaled * normed, axis=-1, keepdims=True)
    )


def attn_stack_kernel(place_ref, *refs):
    blocks, qkv_ref, out_ref = refs[:4], refs[-2], refs[-1]
    rows = out_ref.shape[0]
    vectors = None
    for slot, block in enumerate(blocks):
        plane = slot ^ place_ref[2]
        more = pltpu.roll(block[rows:, :].astype(f32), 3 * plane, 0)
        vectors = more if vectors is None else vectors + more

        @pl.when(plane < 3)
        def _():
            qkv_ref[pl.ds(pl.multiple_of(plane * rows, 16), rows), :] = block[:rows, :]

        @pl.when(plane == 3)
        def _():
            out_ref[...] = block[:rows, :]

    qkv_ref[3 * rows :, :] = vectors.astype(bf16)


def attn_stack(place, blocks, deps):
    rows, width = blocks[0].shape
    rows -= 16
    return pl.pallas_call(
        attn_stack_kernel,
        in_specs=[SMEM] + [pl.BlockSpec(memory_space=pltpu.VMEM)] * 4 + [ANY] * len(deps),
        out_specs=[pl.BlockSpec(memory_space=pltpu.VMEM)] * 2,
        out_shape=[SDS((3 * rows + 16, width), bf16), SDS((rows, width), bf16)],
        compiler_params=params(),
        cost_estimate=cost(1e6, 1e6),
        name="attention_weight_order",
    )(place, *blocks, *deps)


def stack_kernel(place_ref, *refs, which, extra):
    blocks, out_ref = refs[:4], refs[-1]
    rows = blocks[0].shape[0]
    for slot, block in enumerate(blocks):
        at = pl.multiple_of((slot ^ place_ref[which]) * rows, 16)
        out_ref[pl.ds(at, rows), :] = block[...]
    if extra:
        out_ref[4 * rows :, :] = refs[4][...]


def stack(place, blocks, which, *extra, deps=()):
    rows, width = blocks[0].shape
    return pl.pallas_call(
        functools.partial(stack_kernel, which=which, extra=len(extra)),
        in_specs=[SMEM] + [pl.BlockSpec(memory_space=pltpu.VMEM)] * (4 + len(extra)) + [ANY] * len(deps),
        out_specs=pl.BlockSpec(memory_space=pltpu.VMEM),
        out_shape=SDS((rows * (4 + len(extra)), width), bf16),
        compiler_params=params(),
        cost_estimate=cost(1e6, 1e6),
        name="weight_order",
    )(place, *blocks, *extra, *deps)


def attn_fwd_kernel(place_ref, len_ref, scale_ref, *refs, block, count, deps):
    pieces = refs[:count]
    refs = refs[:count] + refs[count + deps :]
    x_ref, q_ref, k_ref, v_ref, c_ref, lse_ref, vec_ref, w_ref, packed, sems, vec_sems = refs[count:]
    rows, width = q_ref.shape
    total_width = x_ref.shape[1]
    group = pl.program_id(0)
    weights = block_copies(place_ref, pieces, range(3), w_ref, sems)

    @pl.when(group == 0)
    def _():
        top = pieces[0].shape[0] - 16
        vec_copies = [
            pltpu.make_async_copy(piece.at[top : top + 16], packed.at[index], vec_sems.at[index])
            for index, piece in enumerate(pieces)
        ]
        for copy in vec_copies:
            copy.start()
        start_all(weights)
        for copy in vec_copies:
            copy.wait()
        vectors = None
        for index in range(count):
            shift = piece_row(place_ref, index, count) * (total_width // count)
            more = packed[index].astype(f32)
            more = more if count == 1 else pltpu.roll(more, shift, 1)
            vectors = more if vectors is None else vectors + more
        vec_ref[...] = vectors
        wait_all(weights)

    x = x_ref[...]
    cols = pl.ds(pl.multiple_of(group * width, 128), width)
    for index, out in enumerate((q_ref, k_ref, v_ref)):
        part = w_ref[:, pl.ds(pl.multiple_of(index * total_width + group * width, 128), width)]
        value = dot(x, part) * scale_ref[index]
        if index != 1:
            value = value + vec_ref[index // 2 : index // 2 + 1, cols]
        out[...] = value.astype(bf16)
    lane = lax.broadcasted_iota(jnp.int32, (1, 128), 1)

    def run(span):
        step = min(block, span)
        for pair in range(width // 128):
            cols = pl.ds(pair * 128, 128)
            for start in range(0, rows, step):
                low = start // span * span
                q_rows = q_ref[start : start + step, cols]
                k_rows = k_ref[low : low + span, cols]
                v_rows = v_ref[low : low + span, cols]
                found = []
                for head in range(2):
                    own = (lane < 64) if head == 0 else (lane >= 64)
                    q_own = jnp.where(own, q_rows, jnp.zeros_like(q_rows)) * jnp.asarray(0.125, bf16)
                    v_ones = jnp.where(own, v_rows, jnp.ones_like(v_rows))
                    scores = dot_last(q_own, k_rows)
                    top = jnp.max(scores, axis=1, keepdims=True)
                    found.append((dot(jnp.exp(scores - top).astype(bf16), v_ones), top))
                (out_a, top_a), (out_b, top_b) = found
                value = jnp.where(lane < 64, out_a, out_b)
                total = jnp.where(lane < 64, pltpu.roll(out_a, 64, 1), pltpu.roll(out_b, 64, 1))
                c_ref[start : start + step, cols] = (value / total).astype(bf16)
                lse_ref[start : start + step, cols] = jnp.where(lane < 64, top_a, top_b) + jnp.log(total)

    two = len_ref[0] < rows

    @pl.when(two)
    def _():
        run(rows // 2)

    @pl.when(jnp.logical_not(two))
    def _():
        run(rows)


def attn_fwd(place, lengths, scales, pieces, x, deps):
    rows, width = x.shape
    group = 256
    count = len(pieces)
    cols = pl.BlockSpec((rows, group), lambda g: (0, g))
    return pl.pallas_call(
        functools.partial(attn_fwd_kernel, block=512, count=count, deps=len(deps)),
        grid=(width // group,),
        in_specs=[SMEM] * 3 + [ANY] * (count + len(deps)) + [pl.BlockSpec((rows, width), lambda g: (0, 0))],
        out_specs=[cols] * 5 + [pl.BlockSpec((16, width), lambda g: (0, 0))],
        out_shape=[SDS((rows, width), bf16)] * 4 + [SDS((rows, width), f32), SDS((16, width), f32)],
        scratch_shapes=[pltpu.VMEM((width, 3 * width), bf16), pltpu.VMEM((count, 16, width), bf16),
                        pltpu.SemaphoreType.DMA((3 * count,)), pltpu.SemaphoreType.DMA((count,))],
        compiler_params=params(),
        cost_estimate=cost(20e9, 12e6, 12e6),
        name="attention_forward",
    )(place, lengths, scales, *pieces, *deps, x)


def order_rows(place_ref, source_t, dest):
    cores = dest.shape[0]
    if cores == 1:
        dest[0] = source_t
        return
    blocks = 8
    size = source_t.shape[0] // blocks
    for block in range(blocks):
        at = pl.multiple_of(((block // 2) ^ place_ref[1]) * size, 16)
        dest[(block % 2) ^ place_ref[0], pl.ds(at, size), :] = source_t[block * size : (block + 1) * size]


def turn_kernel(place_ref, source_ref, out_ref):
    order_rows(place_ref, source_ref[...].T, out_ref)


def turn(place, source, cores):
    rows, width = source.shape
    vmem = pl.BlockSpec(memory_space=pltpu.VMEM)
    return pl.pallas_call(
        turn_kernel,
        in_specs=[SMEM, vmem],
        out_specs=vmem,
        out_shape=SDS((cores, width // cores, rows), bf16),
        compiler_params=params(),
        cost_estimate=cost(1e6, 3e6),
        name="turn",
    )(place, source)


def attn_bwd_kernel(
    place_ref, len_ref, q_ref, k_ref, v_ref, dc_ref, c_ref, lse_ref, x_hbm, c_hbm, dh_ref, *refs, block, cores, last, shard_first, deps,
):
    refs = refs[deps:]
    if last:
        before_a_ref, before_b_ref, vg_first_ref, vg_second_ref, b1g_ref, *refs = refs
    grads = refs[:cores]
    dqkv_ref, sum_ref, dk_acc, dv_acc, dq_acc, x_t, c_t, sems = refs[cores:]
    rows = q_ref.shape[0]
    pair = pl.program_id(0)
    pairs = pl.num_programs(0)
    span_cols = dqkv_ref.shape[1] // 3
    total_width = x_t.shape[0] * x_t.shape[1]
    lane = lax.broadcasted_iota(jnp.int32, (1, 128), 1)
    masks = [lane < 64, lane >= 64]

    turned_copies = [
        pltpu.make_async_copy(x_hbm, x_t, sems.at[0]),
        pltpu.make_async_copy(c_hbm, c_t, sems.at[1]),
    ]

    @pl.when(pair == 0)
    def _():
        for copy in turned_copies:
            copy.start()

    prod = (dc_ref[...].astype(f32) * c_ref[...].astype(f32)).T
    row_dots = [col_sum(prod[:64]), col_sum(prod[64:])]
    lse = lse_ref[...].T
    lse_rows = [lse[0:1], lse[64:65]]

    def run(span):
        step = min(block, span)
        for low in range(0, rows, span):
            k_rows = k_ref[low : low + span, :]
            v_rows = v_ref[low : low + span, :]
            k_cols = k_rows.astype(f32).T.astype(bf16)
            for start in range(low, low + span, step):
                q_rows = q_ref[start : start + step, :]
                dc_rows = dc_ref[start : start + step, :]
                probs, d_scores, q_own, dc_own, dq_parts = [], [], [], [], []
                for head in range(2):
                    q_head = jnp.where(masks[head], q_rows, jnp.zeros_like(q_rows)) * jnp.asarray(0.125, bf16)
                    dc_head = jnp.where(masks[head], dc_rows, jnp.zeros_like(dc_rows))
                    prob = jnp.exp(dot_last(k_rows, q_head) - lse_rows[head][:, start : start + step])
                    d_prob = dot_last(v_rows, dc_head)
                    d_score = (prob * (d_prob - row_dots[head][:, start : start + step])).astype(bf16)
                    probs.append(prob.astype(bf16))
                    d_scores.append(d_score)
                    q_own.append(q_head)
                    dc_own.append(dc_head)
                    dq_parts.append(dot(k_cols[head * 64 : head * 64 + 64], d_score))
                dq_acc[:, start : start + step] = jnp.concatenate(dq_parts, axis=0)
                dv = dot(jnp.concatenate(probs, axis=1), jnp.concatenate(dc_own, axis=0))
                dk = dot(jnp.concatenate(d_scores, axis=1), jnp.concatenate(q_own, axis=0))
                if start == low:
                    dv_acc[low : low + span, :] = dv
                    dk_acc[low : low + span, :] = dk
                else:
                    dv_acc[low : low + span, :] += dv
                    dk_acc[low : low + span, :] += dk

    two = len_ref[0] < rows

    @pl.when(two)
    def _():
        run(rows // 2)

    @pl.when(jnp.logical_not(two))
    def _():
        run(rows)

    dq = dq_acc[...].T * 0.125

    def put(part, value):
        at = pl.multiple_of(part * span_cols + pair * 128, 128)
        dqkv_ref[:, pl.ds(at, 128)] = value.astype(bf16)

    put(0, dq)
    put(1, dk_acc[...])
    put(2, dv_acc[...])
    low = before_a_ref.shape[1] if last else 0
    here = pl.ds(pl.multiple_of(low + pair * 128, 128), 128)
    if last:
        @pl.when(pair == 0)
        def _():
            sum_ref[0:2, : before_a_ref.shape[1]] = before_a_ref[0:2, :]
            sum_ref[0:2, low + span_cols :] = before_b_ref[0:2, :]
            sum_ref[2:5, :] = vg_first_ref[2:5, :]
            sum_ref[5:8, :] = vg_second_ref[5:8, :]
            for row in range(b1g_ref.shape[1] // total_width):
                sum_ref[8 + row : 9 + row, :] = b1g_ref[0:1, row * total_width : (row + 1) * total_width]

    sum_ref[0:1, here] = col_sum(dq)
    sum_ref[1:2, here] = col_sum(dv_acc[...])

    @pl.when(pair == pairs - 1)
    def _():
        for copy in turned_copies:
            copy.wait()
        for core in reversed(range(cores)):
            out = grads[core]
            spots = out.shape[1 if shard_first else 0]
            size = x_t.shape[1] // spots
            for plane in range(4):
                left = x_t if plane < 3 else c_t
                right = dqkv_ref[:, plane * span_cols : (plane + 1) * span_cols] if plane < 3 else dh_ref[...]
                value = dot(left[core], right).astype(bf16)
                if shard_first:
                    out[plane] = value.reshape(spots, size, span_cols)
                else:
                    out[:, pl.ds(plane ^ place_ref[2], 1), :size] = value.reshape(spots, 1, size, span_cols)
        if last and cores == 2:
            row = lax.broadcasted_iota(jnp.int32, (16, span_cols), 0)
            col = lax.broadcasted_iota(jnp.int32, (16, span_cols), 1)
            kept = (row < 3) & (col < size)
            even = place_ref[0] == 0
            for plane in range(4):
                rows_here = sum_ref[...] if plane == 0 else pltpu.roll(sum_ref[...], 16 - 3 * plane, 0)
                for spot in range(4):
                    tiles = []
                    for core in range(2):
                        start = (2 * spot + core) * size
                        turned = rows_here if start == 0 else pltpu.roll(rows_here, total_width - start, 1)
                        tiles.append(jnp.where(kept, turned[:, :span_cols], 0.0).astype(bf16))
                    for core in range(2):
                        tile = jnp.where(even, tiles[core], tiles[1 - core])
                        grads[core][spot ^ place_ref[1], plane ^ place_ref[2], size:, :] = tile


def attn_bwd(place, lengths, q, k, v, dc, c, lse, x_turned, c_turned, dh_low, first, pairs, cores, spots, deps, before=None, shard_first=False):
    rows, width = q.shape
    last = before is not None
    size = pairs * 128
    cols = pl.BlockSpec((rows, 128), lambda g: (0, first + g))

    def whole(shape):
        return pl.BlockSpec(shape, lambda g: (0,) * len(shape))

    depth = width // (cores * spots)
    shape = (spots, 4, depth + (16 if last and cores == 2 else 0), size)
    shape = (shape[1], shape[0]) + shape[2:] if shard_first else shape
    sums = (16, width if last else size)
    more = list(before) if last else []
    return pl.pallas_call(
        functools.partial(attn_bwd_kernel, block=512, cores=cores, last=last, shard_first=shard_first, deps=len(deps)),
        grid=(pairs,),
        in_specs=[SMEM] * 2 + [cols] * 6 + [ANY] * 2
        + [pl.BlockSpec((rows, size), lambda g: (0, first // pairs))] + [ANY] * len(deps) + [whole(m.shape) for m in more],
        out_specs=[whole(shape)] * cores + [whole((rows, 3 * size)), whole(sums)],
        out_shape=[SDS(shape, bf16)] * cores + [SDS((rows, 3 * size), bf16), SDS(sums, f32)],
        scratch_shapes=[
            pltpu.VMEM((rows, 128), f32), pltpu.VMEM((rows, 128), f32), pltpu.VMEM((128, rows), f32),
            pltpu.VMEM((cores, width // cores, rows), bf16), pltpu.VMEM((cores, width // cores, rows), bf16),
            pltpu.SemaphoreType.DMA((2,)),
        ],
        compiler_params=params(),
        cost_estimate=cost(50e9 * size / width, 30e6 * size / width, 12e6 * size / width),
        name="attention_backward",
    )(place, lengths, q, k, v, dc, c, lse, x_turned, c_turned, dh_low, *deps, *more)


def mid_fwd_kernel(place_ref, scale_ref, *refs, chunk, count, deps):
    pieces = refs[:count]
    refs = refs[:count] + refs[count + deps :]
    (x_ref, c_ref, vec_ref, n1_ref, r1_ref, y1_ref, a_ref, gp_ref,
     wo_ref, w1_ref, out_sems, up_sems) = refs[count:]
    rows, width = x_ref.shape
    first = pl.program_id(0) == 0
    out_copies = block_copies(place_ref, pieces, [4], wo_ref, out_sems)
    up_copies = block_copies(place_ref, pieces, range(4), w1_ref, up_sems)

    @pl.when(first)
    def _():
        start_all(out_copies)
        start_all(up_copies)
        wait_all(out_copies)

    residual = x_ref[...].astype(f32) + dot(c_ref[...], wo_ref[...]) * scale_ref[3] + vec_ref[2:3]
    normed, inv_std = normalize(residual)
    n1_ref[...] = normed
    r1_ref[...] = jnp.broadcast_to(inv_std, (rows, 128))
    y1 = (normed * vec_ref[3:4] + vec_ref[4:5]).astype(bf16)
    y1_ref[...] = y1

    @pl.when(first)
    def _():
        wait_all(up_copies)

    for start in range(0, w1_ref.shape[1], chunk):
        block, at = divmod(start, width)
        cols = slice(start, start + chunk)
        bias = vec_ref[8 + block : 9 + block, at : at + chunk]
        u = dot(y1, w1_ref[:, cols]) * scale_ref[4] + bias
        square = u * u
        half = 0.5 + 0.5 * jnp.tanh(u * (GELU_K + (GELU_K * GELU_C) * square))
        act = u * half
        a_ref[:, cols] = act.astype(bf16)
        gp_ref[:, cols] = (half + act * (1.0 - half) * (2 * GELU_K + (6 * GELU_K * GELU_C) * square)).astype(bf16)


def mid_fwd(place, scales, pieces, x, c, vec, deps):
    rows, width = x.shape
    hidden = 4 * pieces[0].shape[1]
    tile = 512
    count = len(pieces)

    def row(size):
        return pl.BlockSpec((tile, size), lambda i: (i, 0))

    def full(arr):
        return pl.BlockSpec(arr.shape, lambda i: (0, 0))

    return pl.pallas_call(
        functools.partial(mid_fwd_kernel, chunk=256, count=count, deps=len(deps)),
        grid=(rows // tile,),
        in_specs=[SMEM] * 2 + [ANY] * (count + len(deps)) + [row(width), row(width), full(vec)],
        out_specs=[row(width), row(128), row(width), row(hidden), row(hidden)],
        out_shape=[SDS((rows, width), f32), SDS((rows, 128), f32), SDS((rows, width), bf16),
                   SDS((rows, hidden), bf16), SDS((rows, hidden), bf16)],
        scratch_shapes=[pltpu.VMEM((width, width), bf16), pltpu.VMEM((width, hidden), bf16),
                        pltpu.SemaphoreType.DMA((count,)), pltpu.SemaphoreType.DMA((4 * count,))],
        compiler_params=params(),
        cost_estimate=cost(12e9, 25e6, 3e6),
        name="middle_forward",
    )(place, scales, *pieces, *deps, x, c, vec)


def second_norm_kernel(place_ref, scale_ref, *refs, cores, tiles):
    downs = refs[:cores]
    (act_ref, n1_ref, do_ref, vec_ref, out_ref, dz_ref, dzb_ref, vg_ref, grad_ref,
     w2_ref, act, dz_all, left_t, down_sems, act_sems) = refs[cores:]
    step = pl.program_id(0)
    tile = n1_ref.shape[0]

    def act_copy(index):
        rows = pl.ds(pl.multiple_of(index * tile, tile), tile)
        return pltpu.make_async_copy(act_ref.at[rows], act.at[rows], act_sems.at[index])

    copies = down_copies(place_ref, downs, w2_ref, down_sems)
    spots = downs[0].shape[1]
    size = w2_ref.shape[1] // spots

    def body(arriving):
        if arriving:
            act_copy(0).start()
            start_all(copies)
            for index in range(1, tiles):
                act_copy(index).start()
            vg_ref[...] = jnp.zeros_like(vg_ref)
        act_copy(step).wait()
        rows = pl.ds(pl.multiple_of(step * tile, tile), tile)
        g1, c1, b2, g2, c2 = [vec_ref[i : i + 1] for i in range(3, 8)]
        if arriving:
            product = None
            for spot in range(spots):
                wait_all(some_copies(copies, spot, spots))
                cols = slice(spot * size, (spot + 1) * size)
                more = dot_last(act[rows, cols], w2_ref[:, cols])
                product = more if product is None else product + more
        else:
            product = dot_last(act[rows, :], w2_ref[...])
        residual = n1_ref[...] * g1 + c1 + product * scale_ref[5] + b2
        n2, r2 = normalize(residual)
        out_ref[...] = (n2 * g2 + c2).astype(bf16)
        d_out = do_ref[...].astype(f32)
        vg_ref[6:7] += col_sum(d_out * n2)
        vg_ref[7:8] += col_sum(d_out)
        dz = normalize_back(d_out * g2, n2, r2)
        vg_ref[5:6] += col_sum(dz)
        dz_ref[...] = dz
        dz_low = dz.astype(bf16)
        dzb_ref[...] = dz_low
        dz_all[rows, :] = dz_low

    @pl.when(step == 0)
    def _():
        body(True)

    @pl.when((step > 0) & (step < tiles))
    def _():
        body(False)

    @pl.when(step == tiles)
    def _():
        left_t[...] = dz_all[...].T

    @pl.when(step >= tiles)
    def _():
        blocks, slots, size, cols = grad_ref.shape
        wide = blocks * cols
        start = pl.multiple_of((step - tiles) * wide, 128)
        value = dot(left_t[...], act[:, pl.ds(start, wide)]).astype(bf16)
        for block in range(blocks):
            grad_ref[block] = value[:, block * cols : (block + 1) * cols].reshape(slots, size, cols)


def second_norm(place, scales, downs, n1, act, d_out, vec, blocks):
    rows, width = n1.shape
    hidden = act.shape[1]
    tile = 256
    tiles = rows // tile
    some = min(4, blocks)
    block = (some, 4, width // 4, hidden // blocks)

    def row(size):
        return pl.BlockSpec((tile, size), lambda i: (jnp.minimum(i, tiles - 1), 0))

    return pl.pallas_call(
        functools.partial(second_norm_kernel, cores=len(downs), tiles=tiles),
        grid=(tiles + blocks // some,),
        in_specs=[SMEM] * 2 + [ANY] * (len(downs) + 1)
        + [row(width), row(width), pl.BlockSpec(vec.shape, lambda i: (0, 0))],
        out_specs=[row(width)] * 3 + [pl.BlockSpec((8, width), lambda i: (0, 0)),
                                      pl.BlockSpec(block, lambda i: (jnp.maximum(i - tiles, 0), 0, 0, 0))],
        out_shape=[SDS((rows, width), bf16), SDS((rows, width), f32), SDS((rows, width), bf16), SDS((8, width), f32),
                   SDS((blocks,) + block[1:], bf16)],
        scratch_shapes=[pltpu.VMEM((width, hidden), bf16), pltpu.VMEM((rows, hidden), bf16),
                        pltpu.VMEM((rows, width), bf16), pltpu.VMEM((width, rows), bf16),
                        pltpu.SemaphoreType.DMA((4 * downs[0].shape[1] * len(downs),)),
                        pltpu.SemaphoreType.DMA((tiles,))],
        compiler_params=params(),
        cost_estimate=cost(16e9, 30e6),
        name="second_norm",
    )(place, scales, *downs, act, n1, d_out, vec)


def mid_bwd_kernel(place_ref, scale_ref, *refs, chunk, count, cores, outs, tiles, deps):
    downs, pieces, refs = refs[:cores], refs[cores : cores + count], refs[cores + count + deps :]
    y1_hbm, n1_ref, r1_ref, gp_ref, dz_ref, dzb_ref, vec_ref = refs[:7]
    dh_ref, dhb_ref, dc_ref, vg_ref, b1g_ref = refs[7:12]
    grads = refs[12 : 12 + outs]
    wo_ref, w1_ref, w2_ref, du_all, y1, left_t, out_sems, up_sems, down_sems, y1_sem = refs[12 + outs :]
    step = pl.program_id(0)
    tile, width = n1_ref.shape
    first = step == 0
    y1_copy = pltpu.make_async_copy(y1_hbm, y1, y1_sem.at[0])

    w2_copies = down_copies(place_ref, downs, w2_ref, down_sems)
    w1_copies = block_copies(place_ref, pieces, range(4), w1_ref, up_sems)
    wo_copies = block_copies(place_ref, pieces, [4], wo_ref, out_sems)
    spots = downs[0].shape[1]

    def body(arriving):
        if arriving:
            start_all(w2_copies)
            start_all(w1_copies)
            start_all(wo_copies)
            y1_copy.start()
            vg_ref[...] = jnp.zeros_like(vg_ref)
            b1g_ref[...] = jnp.zeros_like(b1g_ref)
        rows = pl.ds(pl.multiple_of(step * tile, tile), tile)
        g1 = vec_ref[3:4]
        n1 = n1_ref[...]
        dz_low = dzb_ref[...]
        for start in range(0, w1_ref.shape[1], chunk):
            spot, rest = divmod(start * spots, w1_ref.shape[1])
            if arriving and rest == 0:
                wait_all(some_copies(w2_copies, spot, spots))
            cols = slice(start, start + chunk)
            du = dot(dz_low, w2_ref[:, cols]) * scale_ref[5] * gp_ref[:, cols].astype(f32)
            b1g_ref[0:1, cols] += col_sum(du)
            du_all[rows, cols] = du.astype(bf16)
        if arriving:
            wait_all(w1_copies)
            wait_all(wo_copies)
        dy = dz_ref[...] + dot_last(du_all[rows, :], w1_ref[...]) * scale_ref[4]
        vg_ref[3:4] += col_sum(dy * n1)
        vg_ref[4:5] += col_sum(dy)
        dh = normalize_back(dy * g1, n1, r1_ref[:, 0:1])
        vg_ref[2:3] += col_sum(dh)
        dh_ref[...] = dh
        dh_low = dh.astype(bf16)
        dhb_ref[...] = dh_low
        dc_ref[...] = (dot_last(dh_low, wo_ref[...]) * scale_ref[3]).astype(bf16)

    @pl.when(first)
    def _():
        body(True)

    @pl.when((step > 0) & (step < tiles))
    def _():
        body(False)

    @pl.when(step == tiles)
    def _():
        y1_copy.wait()
        order_rows(place_ref, y1[...].T, left_t)

    @pl.when(step >= tiles)
    def _():
        cols = pl.ds(pl.multiple_of((step - tiles) * width, 128), width)
        for core in reversed(range(outs)):
            grads[core][...] = dot(left_t[core], du_all[:, cols]).astype(bf16).reshape(grads[core].shape)


def mid_bwd(place, scales, pieces, downs, n1, r1, y1, gelu_grad, dz, dz_low, vec, cores, spots, deps):
    rows, width = n1.shape
    hidden = gelu_grad.shape[1]
    tile = 256
    tiles = rows // tile
    count = len(pieces)
    block = (spots, 1, width // (cores * spots), width)

    def row(size):
        return pl.BlockSpec((tile, size), lambda i: (jnp.minimum(i, tiles - 1), 0))

    def whole(shape):
        return pl.BlockSpec(shape, lambda i: (0,) * len(shape))

    return pl.pallas_call(
        functools.partial(
            mid_bwd_kernel, chunk=256, count=count, cores=len(downs), outs=cores, tiles=tiles, deps=len(deps)
        ),
        grid=(tiles + 4,),
        in_specs=[SMEM] * 2 + [ANY] * (count + len(downs) + len(deps) + 1)
        + [row(width), row(128), row(hidden), row(width), row(width), whole(vec.shape)],
        out_specs=[row(width), row(width), row(width), whole((8, width)), whole((8, hidden))]
        + [pl.BlockSpec(block, lambda i: (0, jnp.maximum(i - tiles, 0), 0, 0))] * cores,
        out_shape=[SDS((rows, width), f32), SDS((rows, width), bf16), SDS((rows, width), bf16),
                   SDS((8, width), f32), SDS((8, hidden), f32)]
        + [SDS((spots, 4) + block[2:], bf16)] * cores,
        scratch_shapes=[pltpu.VMEM((width, width), bf16), pltpu.VMEM((width, hidden), bf16),
                        pltpu.VMEM((width, hidden), bf16), pltpu.VMEM((rows, hidden), bf16),
                        pltpu.VMEM((rows, width), bf16), pltpu.VMEM((cores, width // cores, rows), bf16),
                        pltpu.SemaphoreType.DMA((count,)), pltpu.SemaphoreType.DMA((4 * count,)),
                        pltpu.SemaphoreType.DMA((4 * downs[0].shape[1] * len(downs),)),
                        pltpu.SemaphoreType.DMA((1,))],
        compiler_params=params(),
        cost_estimate=cost(28e9, 40e6),
        name="middle_backward",
    )(place, scales, *downs, *pieces, *deps, y1, n1, r1, gelu_grad, dz, dz_low, vec)


def input_grad_kernel(place_ref, scale_ref, *refs, count, chunks, deps):
    pieces = refs[:count]
    parts = refs[count : count + chunks]
    dh_ref, out_ref, w_ref, sems = refs[count + chunks + deps :]
    width = dh_ref.shape[1]

    @pl.when(pl.program_id(0) == 0)
    def _():
        copies = block_copies(place_ref, pieces, range(3), w_ref, sems)
        start_all(copies)
        wait_all(copies)

    total = dh_ref[...]
    for plane in range(3):
        product = None
        start = plane * width
        for part in parts:
            size = part.shape[1] // 3
            more = dot_last(part[:, plane * size : (plane + 1) * size], w_ref[:, start : start + size])
            product = more if product is None else product + more
            start += size
        total = total + product * scale_ref[plane]
    out_ref[...] = total.astype(bf16)


def input_grad(place, scales, pieces, parts, dh, deps):
    rows, width = dh.shape
    tile = 512
    count, chunks = len(pieces), len(parts)

    def row(size):
        return pl.BlockSpec((tile, size), lambda i: (i, 0))

    return pl.pallas_call(
        functools.partial(input_grad_kernel, count=count, chunks=chunks, deps=len(deps)),
        grid=(rows // tile,),
        in_specs=[SMEM] * 2 + [ANY] * count + [row(p.shape[1]) for p in parts] + [ANY] * len(deps) + [row(width)],
        out_specs=row(width),
        out_shape=SDS((rows, width), bf16),
        scratch_shapes=[pltpu.VMEM((width, 3 * width), bf16), pltpu.SemaphoreType.DMA((3 * count,))],
        compiler_params=params(),
        cost_estimate=cost(9e9, 2 * (rows * width * 6 + 3 * width * width)),
        name="input_gradient",
    )(place, scales, *pieces, *parts, *deps, dh)


def swap(value, axis, mask):
    count = lax.axis_size(axis)
    return lax.ppermute(value, axis, [(i, i ^ mask) for i in range(count)])


def bits(axis):
    return [1 << b for b in range(lax.axis_size(axis).bit_length() - 1)]


def doubling_gather(value, axis, dim):
    index = lax.axis_index(axis)
    for bit in bits(axis):
        other = swap(value, axis, bit)
        high = (index & bit) != 0
        value = jnp.concatenate(
            [jnp.where(high, other, value), jnp.where(high, value, other)], axis=dim
        )
    return value


def doubling_sum(value):
    for axis in ("dp", "shard"):
        for bit in bits(axis):
            value = value + swap(value, axis, bit)
    return value


def total_sum(value):
    value = value + swap(value, "dp", 1)
    for axis, masks in (("dp", (6, 4, 2)), ("shard", (3, 2, 1))):
        others = [swap(value, axis, mask) for mask in masks]
        value = (value + others[0]) + (others[1] + others[2])
    return value


def four(block, axis, unit):
    return [block] + [swap(block, axis, unit * m) for m in (1, 2, 3)]


def core_sum_kernel(*refs, sizes, deps):
    count = len(sizes)
    outs = refs[2 * count + deps :]
    at = 0
    for index, (depth, width) in enumerate(sizes):
        mine, got = refs[2 * index : 2 * index + 2]
        for spot, out in enumerate(outs):
            out[:, :depth, at : at + width] = mine[spot] + got[spot]
            if depth < out.shape[1]:
                rest = (out.shape[0], out.shape[1] - depth, width)
                out[:, depth:, at : at + width] = jnp.zeros(rest, bf16)
        at += width


def core_sum(pairs, deps=()):
    spots, slots = pairs[0][0].shape[:2]
    sizes = [mine.shape[2:] for mine, _ in pairs]
    rows, width = max(s[0] for s in sizes), sum(s[1] for s in sizes)
    specs = []
    for depth, wide in sizes:
        specs += [pl.BlockSpec((spots, 2, depth, wide), lambda i: (0, i, 0, 0))] * 2
    return pl.pallas_call(
        functools.partial(core_sum_kernel, sizes=sizes, deps=len(deps)),
        grid=(slots // 2,),
        in_specs=specs + [ANY] * len(deps),
        out_specs=[pl.BlockSpec((2, rows, width), lambda i: (i, 0, 0))] * spots,
        out_shape=[SDS((slots, rows, width), bf16)] * spots,
        compiler_params=params(),
        cost_estimate=cost(1e6, 6 * spots * slots * rows * width),
        name="core_sum",
    )(*[part for pair in pairs for part in pair], *deps)


def pair_sum_kernel(mine_ref, got_ref, *refs):
    refs[-1][...] = mine_ref[...] + got_ref[...]


def pair_sum(mine, got, deps=()):
    block = pl.BlockSpec((2,) + mine.shape[1:], lambda i: (i, 0, 0, 0))
    return pl.pallas_call(
        pair_sum_kernel,
        grid=(mine.shape[0] // 2,),
        in_specs=[block, block] + [ANY] * len(deps),
        out_specs=block,
        out_shape=SDS(mine.shape, bf16),
        compiler_params=params(),
        cost_estimate=cost(1e6, 6 * mine.size),
        name="pair_sum",
    )(mine, got, *deps)


def plane_sum_kernel(*refs, count, deps):
    outs = refs[4 * count + deps :]
    at = 0
    for index in range(count):
        parts = refs[4 * index : 4 * index + 4]
        depth, width = parts[0].shape[1:]
        for slot in range(parts[0].shape[0]):
            total = parts[0][slot].astype(f32) + parts[1][slot].astype(f32)
            total = total + (parts[2][slot].astype(f32) + parts[3][slot].astype(f32))
            out = outs[0].at[slot] if len(outs) == 1 else outs[slot]
            out[:depth, at : at + width] = total.astype(out.dtype)
            if depth < out.shape[0]:
                out[depth:, at : at + width] = jnp.zeros((out.shape[0] - depth, width), out.dtype)
        at += width


def plane_sum(groups, split, deps=()):
    slots = groups[0][0].shape[0]
    rows = max(parts[0].shape[1] for parts in groups)
    width = sum(parts[0].shape[2] for parts in groups)
    vmem = pl.BlockSpec(memory_space=pltpu.VMEM)
    shapes = [SDS((rows, width), f32)] + [SDS((rows, width), bf16)] * (slots - 1)
    if not split:
        shapes = [SDS((slots, rows, width), bf16)]
    return pl.pallas_call(
        functools.partial(plane_sum_kernel, count=len(groups), deps=len(deps)),
        in_specs=[vmem] * (4 * len(groups)) + [ANY] * len(deps),
        out_specs=[vmem] * len(shapes),
        out_shape=shapes,
        compiler_params=params(),
        cost_estimate=cost(1e6, 4 * slots * rows * width),
        name="plane_sum",
    )(*[part for parts in groups for part in parts], *deps)


def exchange(parts, axis, unit):
    return [parts[0]] + [swap(parts[m], axis, unit * m) for m in (1, 2, 3)]


def after(value, *others):
    return lax.optimization_barrier((value,) + others)[0]

def adam_update(gradient, master, first_old, second_old, average, step_rate, decay_rate):
    first_new = beta_first * first_old + (1.0 - beta_first) * gradient
    second_new = beta_second * second_old + (1.0 - beta_second) * gradient * gradient
    first_hat = first_new / (1.0 - beta_first**STEP)
    second_hat = second_new / (1.0 - beta_second**STEP)
    master_new = master - step_rate * (
        first_hat / (jnp.sqrt(second_hat) + adam_eps) + decay_rate * master
    )
    average_new = average_keep * average + (1.0 - average_keep) * master_new
    return (first_new, second_new, master_new, average_new)


def own_sums_kernel(*refs):
    firsts, lasts, (up_ref, down_ref, attn_ref, vec_ref, square_ref) = refs[:4], refs[4:8], refs[8:]
    rows = attn_ref.shape[0]
    first, last = [
        (parts[0][...].astype(f32) + parts[1][...].astype(f32)) + (parts[2][...].astype(f32) + parts[3][...].astype(f32))
        for parts in (firsts, lasts)
    ]
    attn_ref[:, : first.shape[1]] = first
    attn_ref[:, first.shape[1] :] = last[:rows]
    at = 0
    vec_ref[...] = last[rows:, at : at + 128]
    total = jnp.sum(first * first) + jnp.sum(last * last)
    for ref in (up_ref, down_ref):
        value = ref[...].astype(f32)
        total = total + jnp.sum(value * value)
    square_ref[...] = jnp.full(square_ref.shape, total, f32)


def own_sums(firsts, lasts, own_up, own_down):
    vmem = pl.BlockSpec(memory_space=pltpu.VMEM)
    rows, width = firsts[0].shape[0], firsts[0].shape[1] + lasts[0].shape[1]
    return pl.pallas_call(
        own_sums_kernel,
        in_specs=[vmem] * 10,
        out_specs=[vmem] * 3,
        out_shape=[SDS((rows, width), f32), SDS((16, 128), f32), SDS((8, 128), f32)],
        compiler_params=params(),
        cost_estimate=cost(1e6, 2e6),
        name="own_sums",
    )(*firsts, *lasts, own_up, own_down)


def update_kernel(square_ref, attn_ref, up_ref, down_ref, vec_ref, *refs):
    states, news, norm_ref = refs[:16], refs[16:32], refs[32]
    norm = jnp.sqrt(square_ref[...])
    norm_ref[0, 0] = jnp.max(norm)
    factor = jnp.minimum(1.0, clip_limit / (norm + norm_eps))[0:1, 0:1]
    rows, cols = states[12].shape
    grads = (
        attn_ref[...],
        up_ref[...].astype(f32),
        down_ref[...].astype(f32),
        vec_ref[:rows, :cols],
    )
    for index, grad in enumerate(grads):
        rates = (vector_rate, 0.0) if index == 3 else (matrix_rate, matrix_decay)
        old = [ref[...] for ref in states[4 * index : 4 * index + 4]]
        for ref, new in zip(news[4 * index : 4 * index + 4], adam_update(grad * factor, *old, *rates)):
            ref[...] = new


def update(squares, own_attn, own_up, own_down, own_vector, states):
    vmem = pl.BlockSpec(memory_space=pltpu.VMEM)
    states = list(states[:8]) + [state.T for state in states[8:]]
    *news, norm = pl.pallas_call(
        update_kernel,
        in_specs=[vmem] * 21,
        out_specs=[vmem] * 16 + [SMEM],
        out_shape=[SDS(state.shape, f32) for state in states] + [SDS((1, 1), f32)],
        compiler_params=params(),
        cost_estimate=cost(1e7, 8e6),
        name="state_update",
    )(squares, own_attn, own_up, own_down, own_vector, *states)
    return news[:8] + [new.T for new in news[8:]], norm


def on_device(
    tokens, out_grad, first_lengths, quant_scales, attn_quant, up_quant, down_quant,
    attn_master, attn_first, attn_second, attn_average,
    up_master, up_first, up_second, up_average,
    down_master, down_first, down_second, down_average,
    vector_master, vector_first, vector_second, vector_average,
):
    width = tokens.shape[1]
    dp_index, shard_index = lax.axis_index("dp"), lax.axis_index("shard")
    small = lax.axis_size("dp") == 8 and lax.axis_size("shard") == 4 and attn_quant.shape == (96, 768)
    gather = functools.partial(lax.all_gather, tiled=True)
    scatter = functools.partial(lax.psum_scatter, tiled=True)
    down_turned = down_quant.T
    vector_low = vector_master.astype(bf16)
    if small:
        cores, spots = 2, 4
        place = jnp.stack([dp_index & 1, dp_index >> 1, shard_index]).astype(jnp.int32)
        packed = jnp.pad(vector_low.T, ((0, 13), (0, width - 96)))
        blocks = four(jnp.concatenate([attn_quant, packed]), "shard", 1)
        x_turned = turn(place, tokens, cores)
        qkv, w_out = attn_stack(place, blocks, [x_turned])
        pieces = four(qkv, "dp", 2)
        up_blocks = four(after(up_quant, qkv), "shard", 1)
        down = after(lax.all_gather(down_turned, "dp"), pieces[1]).reshape(4, 2, 192, -1)
        down = lax.dynamic_index_in_dim(down, dp_index & 1, 1, keepdims=False)
        half = down
        down = lax.all_gather(after(down, *pieces[1:], *up_blocks), "shard")
        up = stack(place, up_blocks, 2, w_out, deps=pieces[1:2])
        ups = four(up, "dp", 2)
        pieces = pieces + [swap(after(piece, up, half), "dp", 1) for piece in pieces]
        early = [up]
    else:
        cores, spots = 1, 1
        place = jnp.zeros((3,), jnp.int32)
        x_turned = turn(place, tokens, cores)
        vec_w = doubling_gather(doubling_gather(vector_low, "shard", 1), "dp", 0)
        attn_w = gather(gather(attn_quant, "shard", axis=1), "dp", axis=0)
        up_w = gather(gather(up_quant, "shard", axis=1), "dp", axis=0)
        down_w = gather(gather(down_turned, "shard", axis=0), "dp", axis=1)
        planes = [attn_w[:, i * width : (i + 1) * width] for i in range(4)]
        pieces = [jnp.concatenate(planes[:3] + [jnp.pad(vec_w.T, ((0, 4), (0, 0)))])]
        ups = [jnp.concatenate([up_w[:, i * width : (i + 1) * width] for i in range(4)] + planes[3:])]
        downs = [down_w.reshape(4, 1, width // 4, -1)]
        early = []

    q, k, v, c, lse, vec = attn_fwd(place, first_lengths, quant_scales, pieces, tokens, early)
    c_turned = turn(place, c, cores)
    if small:
        ups = [ups[0]] + [after(piece, c_turned) for piece in ups[1:]]
        ups = ups + [swap(piece, "dp", 1) for piece in ups]
    n1, r1, y1, act, gelu_grad = mid_fwd(place, quant_scales, ups, tokens, c, vec, [c_turned])
    if small:
        downs = [down, swap(after(down, act), "dp", 1)]
    layer_out, dz, dz_low, vec_second, grad_down = second_norm(
        place, quant_scales, downs, n1, act, out_grad, vec, cores * spots
    )
    dh, dh_low, dc, vec_first, b1_grad, *up_parts = mid_bwd(
        place, quant_scales, ups, downs, n1, r1, y1, gelu_grad, dz, dz_low, vec, cores, spots, [grad_down]
    )
    attn = functools.partial(
        attn_bwd, place, first_lengths, q, k, v, dc, c, lse, x_turned, c_turned, dh_low, cores=cores, spots=spots
    )
    if small:
        own_down = lax.psum_scatter(grad_down, "dp", scatter_dimension=0)
        up_got = swap(up_parts[1], "dp", 1)
        *parts_p, d_p, sums_p = attn(first=4, pairs=2, deps=up_parts[1:])
        up_plane = core_sum([(up_parts[0], up_got)], [d_p])
        got_p = swap(after(parts_p[1], up_plane[0]), "dp", 1)
        up_plane = exchange(up_plane, "dp", 2)
        *parts_q, d_q, sums_q = attn(first=0, pairs=3, deps=up_plane[:1], shard_first=True)
        own_down = lax.psum_scatter(own_down, "shard", scatter_dimension=0)
        (up_shards,) = plane_sum([up_plane], False, [d_q, own_down])
        own_up = lax.psum_scatter(up_shards, "shard", scatter_dimension=0)
        got_q = swap(after(parts_q[1], up_shards), "dp", 1)
        *parts_r, d_r, sums = attn(first=3, pairs=1, deps=[up_shards], before=(sums_q, sums_p, vec_first, vec_second, b1_grad))
        got_r = swap(parts_r[1], "dp", 1)
        sum_q = pair_sum(parts_q[0], got_q, [d_r])
        plane_pr = core_sum([(parts_r[0], got_r), (parts_p[0], got_p)])
        plane_pr = exchange(plane_pr, "dp", 2)
        spots_q = lax.psum_scatter(sum_q, "shard", scatter_dimension=0)
        spots_q = exchange(after(spots_q, plane_pr[1]), "dp", 2)
        input_gradient = input_grad(place, quant_scales, pieces, [d_q, d_r, d_p], dh, [plane_pr[0], own_up])
        slots_pr = exchange(plane_sum([plane_pr], True, [input_gradient]), "shard", 1)
    else:
        parts_p, d_p, sums_p = attn(first=4, pairs=2, deps=[])
        parts_q, d_q, sums_q = attn(first=0, pairs=3, deps=[])
        parts_r, d_r, sums = attn(first=3, pairs=1, deps=[], before=(sums_q, sums_p, vec_first, vec_second, b1_grad))
        attn_parts = [[parts_q], [parts_r], [parts_p]]
        input_gradient = input_grad(place, quant_scales, pieces, [d_q, d_r, d_p], dh, [])

    rows_own, cols_own = vector_master.shape
    states = (
        attn_master, attn_first, attn_second, attn_average,
        up_master, up_first, up_second, up_average,
        down_master, down_first, down_second, down_average,
        vector_master, vector_first, vector_second, vector_average,
    )
    if small:
        own_attn, own_vector, squares = own_sums(spots_q, slots_pr, own_up, own_down)
        news, grad_norm = update(total_sum(squares), own_attn, own_up, own_down, own_vector, states)
        return (layer_out, input_gradient, grad_norm.reshape(()), *news)
    vec_total = doubling_sum(sums[:12])
    own_vector = lax.dynamic_slice(vec_total, (shard_index * cols_own, dp_index * rows_own), (cols_own, rows_own)).T
    grad_down = grad_down.reshape(width, -1)
    grad_up = up_parts[0][0].transpose(1, 0, 2).reshape(width, -1)
    grad_attn = jnp.concatenate([parts[0][0] for parts in attn_parts], axis=2)
    grad_attn = grad_attn.transpose(1, 0, 2).reshape(width, -1)
    own_down = scatter(scatter(grad_down, "dp", scatter_dimension=1), "shard", scatter_dimension=0).astype(f32).T
    own_up = scatter(scatter(grad_up, "dp", scatter_dimension=0), "shard", scatter_dimension=1).astype(f32)
    own_attn = scatter(scatter(grad_attn, "dp", scatter_dimension=0), "shard", scatter_dimension=1).astype(f32)
    grads = (own_attn, own_up, own_down, own_vector)
    squares = sum(jnp.sum(grad * grad) for grad in grads)
    grad_norm = jnp.sqrt(doubling_sum(jnp.broadcast_to(squares, (8, 128)))[0, 0])
    factor = jnp.minimum(1.0, clip_limit / (grad_norm + norm_eps))
    news = []
    for index, grad in enumerate(grads):
        rates = (vector_rate, 0.0) if index == 3 else (matrix_rate, matrix_decay)
        news += adam_update(grad * factor, *states[4 * index : 4 * index + 4], *rates)
    return (layer_out, input_gradient, grad_norm, *news)


def solution(mesh):
    rows = P(("dp", "shard"), None)
    block = P("dp", "shard")
    in_specs = (rows, rows, P(("dp", "shard")), P()) + (block,) * 19
    out_specs = (rows, rows, P()) + (block,) * 16
    return jax.shard_map(
        on_device, mesh=mesh, in_specs=in_specs, out_specs=out_specs, check_vma=False
    )
```
